32 devices in a mesh: dp: 8 (over z, y), grp: 4 (over x, core).
Axes of the slice: x: 2, y: 2, z: 4, core: 2. Of those that a mesh axis runs over, the one named last changes fastest.
Arguments:
- hidden_in: bfloat16 [64, 768, 512], P('dp', 'grp'), may hold values from -6 to 6
- segment_ids: int32 [64, 512], P('dp'), may hold values from 0 to 4, as said below
- w_query: bfloat16 [2, 4, 192, 192], P(None, 'grp'), may hold values from -0.625 to 0.625
- b_query: float32 [2, 4, 192], P(None, 'grp'), may hold values from -3 to 3
- w_key: bfloat16 [2, 4, 192, 192], P(None, 'grp'), may hold values from -0.625 to 0.625
- w_value: bfloat16 [2, 4, 192, 192], P(None, 'grp'), may hold values from -0.4375 to 0.4375
- b_value: float32 [2, 4, 192], P(None, 'grp'), may hold values from -3 to 3
- w_post: bfloat16 [2, 768, 768], replicated, may hold values from -0.625 to 0.625
- b_post: float32 [2, 768], replicated, may hold values from -3 to 3
- ln1_gain: float32 [2, 768], replicated, may hold values from 0.5 to 1.5
- ln1_bias: float32 [2, 768], replicated, may hold values from -2 to 2
- w_inter: bfloat16 [2, 4, 192, 768], P(None, 'grp'), may hold values from -0.4375 to 0.4375
- b_inter: float32 [2, 4, 768], P(None, 'grp'), may hold values from -3 to 3
- w_output: bfloat16 [2, 4, 192, 768], P(None, 'grp'), may hold values from -0.21875 to 0.21875
- b_output: float32 [2, 4, 192], P(None, 'grp'), may hold values from -3 to 3
- ln2_gain: float32 [2, 768], replicated, may hold values from 0.5 to 1.5
- ln2_bias: float32 [2, 768], replicated, may hold values from -2 to 2
- cotangent: bfloat16 [64, 768, 512], P('dp', 'grp'), may hold values from -6 to 6
Outputs:
- hidden_out: float32 [64, 768, 512], P('dp', 'grp')
- grad_input: float32 [64, 768, 512], P('dp', 'grp')
- grad_w_query: float32 [2, 4, 192, 192], P(None, 'grp')
- grad_b_query: float32 [2, 4, 192], P(None, 'grp')
- grad_w_key: float32 [2, 4, 192, 192], P(None, 'grp')
- grad_w_value: float32 [2, 4, 192, 192], P(None, 'grp')
- grad_b_value: float32 [2, 4, 192], P(None, 'grp')
- grad_w_post: float32 [2, 768, 768], replicated
- grad_b_post: float32 [2, 768], replicated
- grad_ln1_gain: float32 [2, 768], replicated
- grad_ln1_bias: float32 [2, 768], replicated
- grad_w_inter: float32 [2, 4, 192, 768], P(None, 'grp')
- grad_b_inter: float32 [2, 4, 768], P(None, 'grp')
- grad_w_output: float32 [2, 4, 192, 768], P(None, 'grp')
- grad_b_output: float32 [2, 4, 192], P(None, 'grp')
- grad_ln2_gain: float32 [2, 768], replicated
- grad_ln2_bias: float32 [2, 768], replicated
The draws below stay inside these ranges and needn't reach their ends.
Inputs may be any that keep to these rules, and one draw needn't show every extreme that they name: `segment_ids`: along each row the ids never fall, start at 0 and end at 4; the first two boundaries between documents lie in the row's first quarter, the last two in its last quarter.
All inputs are finite; a program needn't handle non-finite values.
Results may differ from the reference program's by a relative error of at most 0.03.
Values may be sent and summed in bfloat16 or wider, within the bound.
No kernel may reach another device: no remote copies, remote signals or barrier semaphores. Data moves between devices by JAX's collectives and lax.ppermute only.
A program may use at most 256 MiB of HBM per device.

```python
import jax
import jax.numpy as jnp
from jax import lax

D = 768
HEADS = 12
FF = 3072
GROUPS = 4
SEQ = 512
LAYERS = 2
ROWS = 64


def draw_segment_ids(key, part):
    key = jax.random.fold_in(key, 11)
    first_key, second_key = jax.random.split(key, 2)
    early_cuts = jax.random.randint(first_key, (ROWS, 2), 1, SEQ // 4)
    late_cuts = jax.random.randint(second_key, (ROWS, 2), 3 * (SEQ // 4) + 1, SEQ)
    boundaries = jnp.concatenate([early_cuts, late_cuts], axis=1)
    positions = jnp.arange(SEQ, dtype=jnp.int32)
    passed = positions[None, :, None] >= boundaries[:, None, :]
    return jnp.sum(passed.astype(jnp.int32), axis=-1).astype(jnp.int32)


def block_scale(rng, extent, pieces, smallest, high):
    loudness, own = 1.0, jax.random.fold_in(rng, 6)
    for dim, shards_of in pieces:
        draws = jnp.exp(jax.random.uniform(jax.random.fold_in(own, dim), (shards_of,), jnp.float32, smallest / len(pieces), high / len(pieces)))
        loudness = loudness * jnp.repeat(draws, extent[dim] // shards_of).reshape([-1 if axis == dim else 1 for axis in range(len(extent))])
    return loudness


def noise(stream_key, dims, scale, reach, cuts=(), kind=jnp.bfloat16):
    loudness = block_scale(stream_key, dims, cuts, -0.22, 0.18) if cuts else 1.0
    values = jax.random.normal(stream_key, dims, jnp.float32) * scale * loudness
    return jnp.minimum(jnp.maximum(values, -reach), reach).astype(kind)


def setup_inputs(seed: int = 0) -> dict:
    key_of = jax.random.split(jax.random.key(seed), 19)
    hidden_in = noise(key_of[0], (ROWS, D, SEQ), 1.0, 6.0, ((0, 8), (1, 4)))
    segment_ids = draw_segment_ids(jax.random.fold_in(key_of[18], 71), 0)
    w_query = noise(key_of[2], (LAYERS, GROUPS, D // GROUPS, D // GROUPS), (D // (2 * GROUPS)) ** -0.5, 0.625, ((1, 4),))
    b_query = noise(key_of[3], (LAYERS, GROUPS, D // GROUPS), 0.5, 3.0, ((1, 4),), jnp.float32)
    w_key = noise(key_of[4], (LAYERS, GROUPS, D // GROUPS, D // GROUPS), (D // (2 * GROUPS)) ** -0.5, 0.625, ((1, 4),))
    w_value = noise(key_of[5], (LAYERS, GROUPS, D // GROUPS, D // GROUPS), (D // GROUPS) ** -0.5, 0.4375, ((1, 4),))
    b_value = noise(key_of[6], (LAYERS, GROUPS, D // GROUPS), 0.5, 3.0, ((1, 4),), jnp.float32)
    w_post = noise(key_of[7], (LAYERS, D, D), (D // 8) ** -0.5, 0.625)
    b_post = noise(key_of[8], (LAYERS, D), 0.5, 3.0, (), jnp.float32)
    ln1_gain = jnp.clip(1.0 + 0.1 * jax.random.normal(key_of[9], (LAYERS, D), jnp.float32), 0.5, 1.5)
    ln1_bias = noise(key_of[10], (LAYERS, D), 0.3, 2.0, (), jnp.float32)
    w_inter = noise(key_of[11], (LAYERS, GROUPS, D // GROUPS, FF // GROUPS), (D // GROUPS) ** -0.5, 0.4375, ((1, 4),))
    b_inter = noise(key_of[12], (LAYERS, GROUPS, FF // GROUPS), 0.5, 3.0, ((1, 4),), jnp.float32)
    w_output = noise(key_of[13], (LAYERS, GROUPS, D // GROUPS, FF // GROUPS), (FF // GROUPS) ** -0.5, 0.21875, ((1, 4),))
    b_output = noise(key_of[14], (LAYERS, GROUPS, D // GROUPS), 0.5, 3.0, ((1, 4),), jnp.float32)
    ln2_gain = jnp.clip(1.0 + 0.1 * jax.random.normal(key_of[15], (LAYERS, D), jnp.float32), 0.5, 1.5)
    ln2_bias = noise(key_of[16], (LAYERS, D), 0.3, 2.0, (), jnp.float32)
    cotangent = noise(key_of[17], (ROWS, D, SEQ), 1.0, 6.0, ((0, 8), (1, 4)))
    return dict(hidden_in=hidden_in, segment_ids=segment_ids, w_query=w_query, b_query=b_query, w_key=w_key, w_value=w_value, b_value=b_value, w_post=w_post, b_post=b_post, ln1_gain=ln1_gain, ln1_bias=ln1_bias, w_inter=w_inter, b_inter=b_inter, w_output=w_output, b_output=b_output, ln2_gain=ln2_gain, ln2_bias=ln2_bias, cotangent=cotangent)


@jax.custom_vjp
def low(v):
    return lax.optimization_barrier(v.astype(jnp.bfloat16)).astype(jnp.float32)

@jax.custom_vjp
def low_back(v):
    return v

def low_keep(v):
    return (low(v), None)

def low_pass(kept, grad):
    return (grad,)

def back_keep(v):
    return (v, None)

def back_low(kept, grad):
    return (low(grad),)
low.defvjp(low_keep, low_pass)
low_back.defvjp(back_keep, back_low)
highest = lax.Precision.HIGHEST
epsilon = 1e-05
masked_score = -1e+30

def grouped(values, weight):
    lead_rows, seq_len, width = values.shape
    split_in = values.reshape(lead_rows, seq_len, weight.shape[0], weight.shape[1])
    mixed = jnp.einsum('bsgc,gcd->bsgd', split_in, weight, precision=highest)
    return mixed.reshape(lead_rows, seq_len, weight.shape[0] * weight.shape[2])

def layer_norm(values, gain, shift):
    center = lax.optimization_barrier(jnp.mean(values, axis=-1, keepdims=True))
    spread = lax.optimization_barrier(jnp.mean(values * values, axis=-1, keepdims=True)) - center * center
    return (values - center) * lax.rsqrt(spread + epsilon) * gain + shift

def attend_row(query, keys, values, segment):
    head_dim = D // HEADS
    query_heads = query.reshape(SEQ, HEADS, head_dim)
    key_heads = keys.reshape(SEQ, HEADS, head_dim)
    value_heads = values.reshape(SEQ, HEADS, head_dim)
    raw_scores = low_back(jnp.einsum('qhd,khd->hqk', query_heads, key_heads, precision=highest))
    scores = raw_scores * head_dim ** (-0.5)
    same_doc = segment[:, None] == segment[None, :]
    scores = jnp.where(same_doc[None, :, :], scores, masked_score)
    weights = low(jax.nn.softmax(scores, axis=-1))
    mixed = jnp.einsum('hqk,khd->qhd', weights, value_heads, precision=highest)
    return mixed.reshape(SEQ, D)
attend_saved = jax.checkpoint(attend_row)

def one_layer(values, segment, params, depth):
    weight_query, bias_query, weight_key, weight_value, bias_value, weight_post, bias_post, gain_first, shift_first, weight_inter, bias_inter, weight_output, bias_output, gain_second, shift_second = params
    skip_path = low_back(low(values))
    inputs = low(values)
    query = low_back(low(grouped(inputs, weight_query[depth]) + bias_query[depth].reshape(D)))
    keys = low_back(low(grouped(inputs, weight_key[depth])))
    vals = low_back(low(grouped(inputs, weight_value[depth]) + bias_value[depth].reshape(D)))
    attended = lax.map(lambda item: attend_saved(item[0], item[1], item[2], item[3]), (query, keys, vals, segment))
    attended = low_back(low(attended))
    branch = low_back(jnp.einsum('bsc,cd->bsd', attended, weight_post[depth], precision=highest) + bias_post[depth])
    normed = low_back(low(layer_norm(skip_path + branch, gain_first[depth], shift_first[depth])))
    pre_act = low_back(grouped(normed, weight_inter[depth]) + bias_inter[depth].reshape(FF))
    activ = low(jax.nn.gelu(pre_act, approximate=False))
    ffn_out = low_back(grouped(activ, jnp.swapaxes(weight_output[depth], 1, 2)) + bias_output[depth].reshape(D))
    return layer_norm(normed + ffn_out, gain_second[depth], shift_second[depth])

def forward(values, segment, params):
    for depth in range(LAYERS):
        values = one_layer(values, segment, params, depth)
    return values

def reference(hidden_in, segment_ids, w_query, b_query, w_key, w_value, b_value, w_post, b_post, ln1_gain, ln1_bias, w_inter, b_inter, w_output, b_output, ln2_gain, ln2_bias, cotangent):
    params = tuple((item.astype(jnp.float32) for item in (w_query, b_query, w_key, w_value, b_value, w_post, b_post, ln1_gain, ln1_bias, w_inter, b_inter, w_output, b_output, ln2_gain, ln2_bias)))
    row_total = hidden_in.shape[0]
    block_rows = 8 if row_total % 8 == 0 else 2
    block_count = row_total // block_rows
    tokens_last = jnp.swapaxes(hidden_in.astype(jnp.float32), 1, 2)
    cot_last = jnp.swapaxes(cotangent.astype(jnp.float32), 1, 2)

    def split_rows(array):
        return array.reshape((block_count, block_rows) + array.shape[1:])

    def step(carry, item):
        block_in, block_seg, block_cot = item

        def run(values, weights):
            return forward(values, block_seg, weights)
        result, pull = jax.vjp(run, block_in, params)
        grad_in, grad_params = pull(block_cot)
        return (tuple((total + part_grad for total, part_grad in zip(carry, grad_params))), (result, grad_in))
    start = tuple((jnp.zeros_like(item) for item in params))
    totals, stacked = lax.scan(step, start, (split_rows(tokens_last), split_rows(segment_ids), split_rows(cot_last)))
    hidden_out = jnp.swapaxes(stacked[0].reshape(row_total, SEQ, D), 1, 2)
    grad_input = jnp.swapaxes(stacked[1].reshape(row_total, SEQ, D), 1, 2)
    g_wq, g_bq, g_wk, g_wv, g_bv, g_wp, g_bp, g_ga, g_sa, g_wi, g_bi, g_wo, g_bo, g_gb, g_sb = totals
    return (hidden_out, grad_input, g_wq, g_bq, g_wk, g_wv, g_bv, g_wp, g_bp, g_ga, g_sa, g_wi, g_bi, g_wo, g_bo, g_gb, g_sb)
```

```python
import functools

import jax
import jax.numpy as jnp
from jax import lax
from jax.experimental import pallas as pl
from jax.experimental.pallas import tpu as pltpu
from jax.sharding import PartitionSpec as P


HEADS = 12
LAYERS = 2
GROUPS = 4
EPSILON = 1e-05
MASKED = -1e30

F32 = jnp.float32
BF16 = jnp.bfloat16
NN = (((1,), (0,)), ((), ()))
NT = (((1,), (1,)), ((), ()))
TN = (((0,), (0,)), ((), ()))
MIB = 1 << 20


def dot(left, right, dims):
    return lax.dot_general(left, right, dims, preferred_element_type=F32)


def params(limit=60):
    return pltpu.CompilerParams(vmem_limit_bytes=limit * MIB)


def cost(micros):
    return pl.CostEstimate(flops=int(micros * 1e9), bytes_accessed=1 << 10, transcendentals=0)


def shape(dims, dtype):
    return jax.ShapeDtypeStruct(dims, dtype)


SMEM = pl.BlockSpec(memory_space=pltpu.SMEM)
ANY = pl.BlockSpec(memory_space=pl.ANY)


def launch(body, arrays, in_specs, outs, out_specs, through=(), needs=(), aliases=None, **kwargs):
    count, made = len(arrays), len(outs)
    extra = len(through) + len(needs)

    def kernel(*refs):
        body(*refs[:count], *refs[count + extra : count + extra + made], *refs[count + extra + made + len(through) :])

    results = pl.pallas_call(
        kernel,
        in_specs=list(in_specs) + [ANY] * extra,
        out_specs=list(out_specs) + [ANY] * len(through),
        out_shape=list(outs) + [shape(a.shape, a.dtype) for a in through],
        input_output_aliases={
            **(aliases or {}),
            **{count + i: made + i for i in range(len(through))},
        },
        **kwargs,
    )(*arrays, *through, *needs)
    return results[:made], results[made:]


def attend_kernel(head_dim, aliased, count, *refs):
    x_ref, km_ref, qm_ref = refs[:3]
    w_refs, b_refs = refs[3 : 3 + count], refs[3 + count : 3 + 2 * count]
    o_ref, qkv_ref, lse_ref, xs_ref, wt_ref, bias_ref = refs[3 + 2 * count + aliased :]
    narrow = x_ref.shape[-2]
    for k in range(count):

        @pl.when((pl.program_id(1) == 0) & (pl.program_id(0) == k))
        def _(k=k):
            wt_ref[...] = w_refs[k][0].T[: 3 * narrow]
            bias_ref[...] = b_refs[k][0].T[: 3 * narrow]

    x = x_ref[0, 0]
    xs_ref[0, 0] = x
    qkv = dot(wt_ref[...], x, NN) + bias_ref[:, 1:2]
    query = qkv[:narrow].astype(BF16) * (head_dim**-0.5)
    rest_low = qkv[narrow:].astype(BF16)
    qkv_ref[0, 0, :narrow] = query
    qkv_ref[0, 0, narrow:] = rest_low
    key_mask, query_mask = km_ref[0], qm_ref[0]
    logs = []
    for head in range(narrow // head_dim):
        lo = head * head_dim
        q_h = jnp.concatenate([query[lo : lo + head_dim], query_mask], 0)
        k_h = jnp.concatenate([rest_low[lo : lo + head_dim], key_mask], 0)
        v_h = rest_low[narrow + lo : narrow + lo + head_dim]
        scores = dot(k_h, q_h, TN)
        top = jnp.max(scores, axis=0, keepdims=True)
        raised = jnp.exp(scores - top)
        total = jnp.sum(raised, axis=0, keepdims=True)
        mixed = dot(v_h, raised.astype(BF16), NN) * (1.0 / total)
        o_ref[0, 0, lo : lo + head_dim] = mixed.astype(BF16)
        logs.append(top + jnp.log(total))
    pad = jnp.zeros((8 - len(logs), x.shape[1]), F32)
    lse_ref[0, 0] = jnp.concatenate(logs + [pad], 0)


def attend(x, first, earlier, weights, biases, masks, layer, head_dim, through=(), needs=()):
    stacked, rows, narrow, seq = x.shape
    count = len(weights)
    dims = [(narrow, BF16), (3 * narrow, BF16), (8, F32), (narrow, BF16)]
    at = lambda s, r: (first + s, r, 0, 0)
    prior = [] if earlier is None else list(earlier)
    lanes = weights[0].shape[2]
    block = weights[0].shape[0] - 1
    here = 3 + 2 * count
    in_specs = (
        [pl.BlockSpec((1, 1, narrow, seq), at if stacked > 1 else (lambda s, r: (s, r, 0, 0)))]
        + [pl.BlockSpec((1, 16, seq), lambda s, r: (r, 0, 0))] * 2
        + [pl.BlockSpec((1, narrow, lanes), lambda s, r: (block, 0, 0))] * count
        + [pl.BlockSpec((1, 8, biases[0].shape[2]), lambda s, r: (layer, 0, 0))] * count
        + [ANY] * len(prior)
    )
    extra = len(through) + len(needs)
    inputs = [x, *masks, *weights, *biases, *prior]
    outs = [shape((GROUPS, rows, n, seq), t) for n, t in dims]
    made, base = len(outs), len(inputs)

    def kernel(*refs):
        attend_kernel(
            head_dim, len(prior), count,
            *refs[:base], *refs[base + extra : base + extra + made],
            *refs[base + extra + made + len(through) :],
        )

    aliases = {here + i: i for i in range(len(prior))}
    aliases.update({base + i: made + i for i in range(len(through))})
    results = pl.pallas_call(
        kernel,
        grid=(count, rows),
        in_specs=in_specs + [ANY] * extra,
        out_specs=[pl.BlockSpec((1, 1, n, seq), at) for n, _ in dims] + [ANY] * len(through),
        out_shape=outs + [shape(a.shape, a.dtype) for a in through],
        scratch_shapes=[
            pltpu.VMEM((3 * narrow, narrow), BF16),
            pltpu.VMEM((3 * narrow, 8), F32),
        ],
        input_output_aliases=aliases,
        compiler_params=params(),
        cost_estimate=cost(0.01),
        name="attend_fwd",
    )(*inputs, *through, *needs)
    return results[:made], results[made:]


def attend_back_kernel(head_dim, count, aliased, *refs):
    x_ref, qkv_ref, dout_ref, da_ref, lse_ref, delta_ref, km_ref, qm_ref = refs[:8]
    w_refs, refs = refs[8 : 8 + count], refs[8 + count + aliased :]
    gx_ref, dw_ref, acc_ref, dqkv_ref, w_ref = refs
    narrow, seq = x_ref.shape[-2:]
    place, row = pl.program_id(0), pl.program_id(1)
    for s in range(count):

        @pl.when((place == s) & (row == 0))
        def _(s=s):
            w_ref[...] = w_refs[s][0, :, : 3 * narrow]

    key_mask, query_mask = km_ref[0], qm_ref[0]
    scale = head_dim**-0.5
    for head in range(narrow // head_dim):
        lo = head * head_dim
        q_h = qkv_ref[0, 0, lo : lo + head_dim]
        k_h = qkv_ref[0, 0, narrow + lo : narrow + lo + head_dim]
        v_h = qkv_ref[0, 0, 2 * narrow + lo : 2 * narrow + lo + head_dim]
        do_h = dout_ref[0, 0, lo : lo + head_dim]
        scores = dot(
            jnp.concatenate([k_h, key_mask], 0), jnp.concatenate([q_h, query_mask], 0), TN
        )
        probs = jnp.exp(scores - lse_ref[0, 0, head : head + 1])
        grad_probs = dot(v_h, do_h, TN)
        grad_scores = (probs * (grad_probs - delta_ref[0, 0, head : head + 1])).astype(BF16)
        dqkv_ref[lo : lo + head_dim] = (dot(k_h, grad_scores, NN) * scale).astype(BF16)
        dqkv_ref[narrow + lo : narrow + lo + head_dim] = dot(q_h, grad_scores, NT).astype(BF16)
        dqkv_ref[2 * narrow + lo : 2 * narrow + lo + head_dim] = dot(
            do_h, probs.astype(BF16), NT
        ).astype(BF16)
    dqkv = dqkv_ref[...]
    gx_ref[0, 0] = (dot(w_ref[...], dqkv, NN) + da_ref[0, 0].astype(F32)).astype(gx_ref.dtype)
    ones = jnp.ones((16, seq), BF16)
    term = dot(jnp.concatenate([x_ref[0, 0], ones], 0), dqkv, NT)

    @pl.when(row == 0)
    def _():
        acc_ref[...] = term

    @pl.when(row > 0)
    def _():
        acc_ref[...] += term

    @pl.when(row == pl.num_programs(1) - 1)
    def _():
        pieces = dw_ref.shape[1]
        step = narrow // pieces
        sums = acc_ref[narrow : narrow + 1]
        extra = jnp.concatenate(
            [sums[:, :narrow], sums[:, 2 * narrow :], jnp.zeros((step - 2, narrow), F32)], 0
        ).astype(BF16)
        for piece in range(pieces):
            dw_ref[0, piece, :, : 3 * narrow] = acc_ref[piece * step : (piece + 1) * step].astype(BF16)
            dw_ref[0, piece, :, 3 * narrow :] = extra


def attend_back(order, pieces, acts, weights, masks, head_dim, out_type, stack, earlier=(), through=(), needs=()):
    _, rows, narrow, seq = acts[0].shape
    count = len(order)
    slot = lambda s: order[0] + (order[-1] - order[0]) * s
    at = lambda s, r: (slot(s), r, 0, 0)
    here = at if stack else (lambda s, r: (s, r, 0, 0))
    block = lambda n, where: pl.BlockSpec((1, 1, n, seq), where)
    lanes = weights[0].shape[2]
    last = weights[0].shape[0] - 1
    dims = (count, pieces, narrow // pieces, lanes)
    return launch(
        functools.partial(attend_back_kernel, head_dim, count, len(earlier)),
        [*acts, *masks, *[weights[k] for k in order], *earlier],
        [block(a.shape[2], at) for a in acts]
        + [pl.BlockSpec((1, 16, seq), lambda s, r: (r, 0, 0))] * 2
        + [pl.BlockSpec((1, narrow, lanes), lambda s, r: (last, 0, 0))] * count
        + [ANY] * len(earlier),
        [shape((GROUPS if stack else count, rows, narrow, seq), out_type), shape(dims, BF16)],
        [block(narrow, here), pl.BlockSpec((1,) + dims[1:], lambda s, r: (s, 0, 0, 0))],
        through,
        needs,
        aliases={8 + count: 0} if earlier else {},
        grid=(count, rows),
        scratch_shapes=[
            pltpu.VMEM((narrow + 16, 3 * narrow), F32),
            pltpu.VMEM((3 * narrow, seq), BF16),
            pltpu.VMEM((narrow, 3 * narrow), BF16),
        ],
        compiler_params=params(),
        cost_estimate=cost(3.5 * count * rows),
        name="attend_bwd",
    )


def norm(values):
    width = values.shape[0]
    center = jnp.sum(values, axis=0, keepdims=True) * (1.0 / width)
    spread = jnp.sum(values * values, axis=0, keepdims=True) * (1.0 / width) - center * center
    inverse = lax.rsqrt(spread + EPSILON)
    return (values - center) * inverse, inverse


def norm_back(weighted, scaled, inverse):
    width = weighted.shape[0]
    first = jnp.sum(weighted, axis=0, keepdims=True) * (1.0 / width)
    second = jnp.sum(weighted * scaled, axis=0, keepdims=True) * (1.0 / width)
    return inverse * (weighted - first - scaled * second)


def normal_cdf(values):
    return 0.5 + 0.5 * lax.erf(values * 0.7071067811865476)


def whole(ref, me):
    return jnp.concatenate([ref[me ^ j, 0] for j in range(GROUPS)], 0)


def columns(layer, narrow, me, vec_refs, small_refs, small_ref):
    for k in range(GROUPS):
        small_ref[me ^ k] = small_refs[k][layer]
    out_bias = jnp.concatenate([small_ref[j, 1:2, 3 * narrow :] for j in range(GROUPS)], 1)
    rows = [ref[layer : layer + 1] for ref in vec_refs] + [out_bias]
    rows += [small_ref[j, 0:1] for j in range(GROUPS)]
    rows.append(jnp.zeros((16 - len(rows), out_bias.shape[1]), F32))
    return jnp.concatenate(rows, 0).T


def first_step():
    return (pl.program_id(0) == 0) & (pl.program_id(1) == 0)


def mix_kernel(layer, split, *refs):
    me_ref, xs_ref, o_ref, wp_ref = refs[:4]
    vec_refs, small_refs, w_refs = refs[4:9], refs[9:13], refs[13:17]
    count = GROUPS if split else 1
    next_refs, refs = refs[17 : 17 + count], refs[17 + count :]
    y1_ref, xh1_ref, xh2_ref, inv_ref, wpt_ref, wit_ref, wo_ref, small_ref, state_ref = refs
    me = me_ref[0]
    narrow = xs_ref.shape[2]

    @pl.when(first_step())
    def _():
        wpt_ref[...] = wp_ref[0].T
        for k in range(GROUPS):
            wit_ref[me ^ k] = w_refs[k][0].T
            wo_ref[me ^ k] = w_refs[k][1]

    cols = columns(layer, narrow, me, vec_refs, small_refs, small_ref)
    a = dot(wpt_ref[...], whole(o_ref, me), NN) + whole(xs_ref, me).astype(F32) + cols[:, 0:1]
    scaled_one, inverse_one = norm(a)
    y1 = (scaled_one * cols[:, 1:2] + cols[:, 2:3]).astype(BF16)
    y1_ref[0] = y1
    xh1_ref[0] = scaled_one.astype(BF16)
    parts = []
    for j in range(GROUPS):
        lo = j * narrow
        y_j = y1[lo : lo + narrow]
        h = dot(wit_ref[j], y_j, NN) + cols[:, 6 + j : 7 + j]
        u = (h * normal_cdf(h)).astype(BF16)
        parts.append(y_j.astype(F32) + dot(wo_ref[j], u, NN) + cols[lo : lo + narrow, 5:6])
    scaled_two, inverse_two = norm(jnp.concatenate(parts, 0))
    xh2_ref[0] = scaled_two.astype(BF16)
    state = (scaled_two * cols[:, 3:4] + cols[:, 4:5]).astype(BF16)
    for j in range(GROUPS):
        piece = state[j * narrow : (j + 1) * narrow]
        if split:
            state_ref[j] = piece
        else:
            next_refs[0][me ^ j, 0] = piece
    if split:
        for k in range(GROUPS):
            next_refs[k][0] = state_ref[me ^ k]
    inv_ref[0] = jnp.concatenate(
        [inverse_one, inverse_two, jnp.zeros((6, inverse_one.shape[1]), F32)], 0
    )


def mix(me, layer, split, xs, o, w_post, vectors, smalls, weights, tile, through=(), needs=()):
    _, rows, narrow, seq = xs.shape
    width = narrow * GROUPS
    ff = weights[0].shape[2]
    stacked = pl.BlockSpec((GROUPS, 1, narrow, tile), lambda r, t: (0, r, 0, t))
    plain = lambda n: pl.BlockSpec((1, n, tile), lambda r, t: (r, 0, t))
    const = lambda a: pl.BlockSpec(a.shape, lambda r, t: (0,) * a.ndim)
    outs = [shape((rows, narrow, seq), BF16)] * GROUPS if split else [shape(xs.shape, BF16)]
    return launch(
        functools.partial(mix_kernel, layer, split),
        [me, xs, o, w_post, *vectors, *smalls, *weights],
        [SMEM, stacked, stacked, pl.BlockSpec((1, width, width), lambda r, t: (layer, 0, 0))]
        + [const(a) for a in (*vectors, *smalls)]
        + [pl.BlockSpec((2, narrow, ff), lambda r, t: (0, 0, 0))] * GROUPS,
        outs + [shape((rows, width, seq), BF16)] * 3 + [shape((rows, 8, seq), F32)],
        ([plain(narrow)] * GROUPS if split else [stacked]) + [plain(width)] * 3 + [plain(8)],
        through,
        needs,
        grid=(rows, seq // tile),
        scratch_shapes=[
            pltpu.VMEM((width, width), BF16),
            pltpu.VMEM((GROUPS, ff, narrow), BF16),
            pltpu.VMEM((GROUPS, narrow, ff), BF16),
            pltpu.VMEM((GROUPS, 8, ff), F32),
            pltpu.VMEM((GROUPS, narrow, tile), BF16),
        ],
        compiler_params=params(),
        cost_estimate=cost(0.01),
        name="mix_fwd",
    )


def lane_sum(values):
    total = values[:, :128]
    for lo in range(128, values.shape[1], 128):
        total = total + values[:, lo : lo + 128]
    return total


def mix_back_kernel(layer, head_dim, *refs):
    me_ref, y1_ref, xh1_ref, xh2_ref, inv_ref, o_ref = refs[:6]
    gz_refs, wp_ref, vec_refs, small_refs, w_refs = refs[6:10], refs[10], refs[11:16], refs[16:20], refs[20:24]
    da_ref, dout_ref, delta_ref, f_odd_ref, f_even_ref, p_odd_ref, p_even_ref = refs[24:31]
    accf_ref, accp_ref, accv_ref, wit_ref, wot_ref, wi_ref, small_ref, gz_ref, tail_ref = refs[31:]
    me = me_ref[0]
    narrow, tile = o_ref.shape[2:]
    width = narrow * GROUPS
    step = pl.program_id(0) * pl.num_programs(1) + pl.program_id(1)
    steps = pl.num_programs(0) * pl.num_programs(1)

    @pl.when(first_step())
    def _():
        for k in range(GROUPS):
            wit_ref[me ^ k] = w_refs[k][0].T
            wi_ref[me ^ k] = w_refs[k][0]
            wot_ref[me ^ k] = w_refs[k][1].T
        accf_ref[...] = jnp.zeros_like(accf_ref)
        accp_ref[...] = jnp.zeros_like(accp_ref)
        accv_ref[...] = jnp.zeros_like(accv_ref)

    cols = columns(layer, narrow, me, vec_refs, small_refs, small_ref)
    for k in range(GROUPS):
        gz_ref[me ^ k] = gz_refs[k][0, 0].astype(F32)
    gz = jnp.concatenate([gz_ref[j] for j in range(GROUPS)], 0)
    y1 = y1_ref[0]
    scaled_one = xh1_ref[0].astype(F32)
    scaled_two = xh2_ref[0].astype(F32)
    inverse_one, inverse_two = inv_ref[0, 0:1], inv_ref[0, 1:2]
    accv_ref[0] += lane_sum(gz * scaled_two)
    accv_ref[1] += lane_sum(gz)
    dz = norm_back(gz * cols[:, 3:4], scaled_two, inverse_two)
    df = dz.astype(BF16)
    accv_ref[2] += lane_sum(df.astype(F32))
    ones = jnp.ones((16, tile), BF16)
    parts = []
    for j in range(GROUPS):
        lo = j * narrow
        df_j, y_j = df[lo : lo + narrow], y1[lo : lo + narrow]
        h = dot(wit_ref[j], y_j, NN) + cols[:, 6 + j : 7 + j]
        cdf = normal_cdf(h)
        accf_ref[j, narrow + 16 :] += dot(df_j, (h * cdf).astype(BF16), NT)
        slope = cdf + h * jnp.exp(-0.5 * h * h) * 0.3989422804014327
        dh = (dot(wot_ref[j], df_j, NN) * slope).astype(BF16)
        accf_ref[j, : narrow + 16] += dot(jnp.concatenate([y_j, ones], 0), dh, NT)
        parts.append(dz[lo : lo + narrow] + dot(wi_ref[j], dh, NN))
    dy1 = jnp.concatenate(parts, 0).astype(BF16).astype(F32)
    accv_ref[3] += lane_sum(dy1 * scaled_one)
    accv_ref[4] += lane_sum(dy1)
    da = norm_back(dy1 * cols[:, 1:2], scaled_one, inverse_one).astype(BF16)
    o = whole(o_ref, me)
    accp_ref[...] += dot(jnp.concatenate([o, ones], 0), da, NT)
    dout = dot(wp_ref[0], da, NN).astype(BF16)
    product = (o.astype(F32) * dout.astype(F32)).reshape(width // head_dim, head_dim, tile)
    delta = jnp.sum(product, axis=1)
    per_group = narrow // head_dim
    pad = jnp.zeros((8 - per_group, tile), F32)
    for j in range(GROUPS):
        lo = j * narrow
        da_ref[me ^ j, 0] = da[lo : lo + narrow]
        dout_ref[me ^ j, 0] = dout[lo : lo + narrow]
        delta_ref[me ^ j, 0] = jnp.concatenate(
            [delta[j * per_group : (j + 1) * per_group], pad], 0
        )

    @pl.when(step == steps - 1)
    def _():
        pieces = f_odd_ref.shape[1]
        vec = [jnp.sum(accv_ref[i].T, axis=0, keepdims=True) for i in range(5)]
        vec.append(accp_ref[width : width + 1])
        half = pieces // 2
        size, post = narrow // half, narrow // pieces
        for j in range(GROUPS):
            lo = j * narrow
            own = [v[:, lo : lo + narrow] for v in vec]
            tail_ref[j] = jnp.concatenate(
                [
                    accf_ref[j, narrow : narrow + 1],
                    jnp.concatenate(own[:4], 1),
                    jnp.concatenate(own[4:] + own[4:], 1),
                    jnp.zeros((5, width), F32),
                ],
                0,
            ).astype(BF16)
        for k in range(GROUPS):
            f_ref, p_ref = (f_odd_ref, p_odd_ref) if k % 2 else (f_even_ref, p_even_ref)
            j = me ^ k
            for piece in range(pieces):
                at = (piece % half) * size + (0 if piece < half else narrow + 16)
                f_ref[k // 2, piece] = accf_ref[j, at : at + size].astype(BF16)
                at = pl.multiple_of(j * narrow + piece * post, 8)
                p_ref[k // 2, piece, :post] = accp_ref[pl.ds(at, post)].astype(BF16)
                p_ref[k // 2, piece, post:] = tail_ref[j]


def mix_back(me, layer, pieces, kept, o, gz, w_post, vectors, smalls, weights, head_dim, tile, through=(), needs=()):
    _, rows, narrow, seq = o.shape
    width = narrow * GROUPS
    ff = weights[0].shape[2]
    stacked = pl.BlockSpec((GROUPS, 1, narrow, tile), lambda r, t: (0, r, 0, t))
    plain = lambda n: pl.BlockSpec((1, n, tile), lambda r, t: (r, 0, t))
    const = lambda dims: pl.BlockSpec(dims, lambda r, t: (0,) * len(dims))
    if isinstance(gz, list):
        gz_specs = [pl.BlockSpec((1, 1, narrow, tile), lambda r, t: (0, r, 0, t))] * GROUPS
    else:
        gz_specs = [
            pl.BlockSpec((1, 1, narrow, tile), lambda r, t, k=k: (k, r, 0, t))
            for k in range(GROUPS)
        ]
        gz = [gz] * GROUPS
    grads_f = (2, pieces, 2 * narrow // pieces, ff)
    grads_p = (2, pieces, narrow // pieces + 8, width)
    grads = [grads_f, grads_f, grads_p, grads_p]
    return launch(
        functools.partial(mix_back_kernel, layer, head_dim),
        [me, *kept, o, *gz, w_post, *vectors, *smalls, *weights],
        [SMEM] + [plain(width)] * 3 + [plain(8), stacked] + gz_specs
        + [pl.BlockSpec((1, width, width), lambda r, t: (layer, 0, 0))]
        + [const(a.shape) for a in (*vectors, *smalls)]
        + [const((2, narrow, ff))] * GROUPS,
        [shape(o.shape, BF16)] * 2 + [shape((GROUPS, rows, 8, seq), F32)]
        + [shape(g, BF16) for g in grads],
        [stacked, stacked, pl.BlockSpec((GROUPS, 1, 8, tile), lambda r, t: (0, r, 0, t))]
        + [const(g) for g in grads],
        through,
        needs,
        grid=(rows, seq // tile),
        scratch_shapes=[
            pltpu.VMEM((GROUPS, 2 * narrow + 16, ff), F32),
            pltpu.VMEM((width + 16, width), F32),
            pltpu.VMEM((5, width, 128), F32),
            pltpu.VMEM((GROUPS, ff, narrow), BF16),
            pltpu.VMEM((GROUPS, ff, narrow), BF16),
            pltpu.VMEM((GROUPS, narrow, ff), BF16),
            pltpu.VMEM((GROUPS, 8, ff), F32),
            pltpu.VMEM((GROUPS, narrow, tile), F32),
            pltpu.VMEM((GROUPS, 8, width), BF16),
        ],
        compiler_params=params(),
        cost_estimate=cost(24.0),
        name="mix_bwd",
    )


def swap(array, axis, distance):
    size = lax.axis_size(axis)
    return lax.ppermute(array, axis, [(i, i ^ distance) for i in range(size)])


def collect_kernel(me_ref, *refs):
    out = refs[-1]
    for k, ref in enumerate(refs[:-1]):
        out[me_ref[0] ^ k, 0] = ref[0].astype(out.dtype)


def collect(me, arrays, needs=(), dtype=F32):
    rows, rest = arrays[0].shape[0], arrays[0].shape[1:]
    zeros = (0,) * len(rest)
    (out,), _ = launch(
        collect_kernel,
        [me, *arrays],
        [SMEM] + [pl.BlockSpec((1,) + rest, lambda r: (r,) + zeros)] * GROUPS,
        [shape((GROUPS, rows) + rest, dtype)],
        [pl.BlockSpec((GROUPS, 1) + rest, lambda r: (0, r) + zeros)],
        (),
        needs,
        grid=(rows,),
        compiler_params=params(),
        cost_estimate=cost(0.1),
        name="collect",
    )
    return out


def total(*arrays):
    return functools.reduce(lambda a, b: a + b, [a.astype(F32) for a in arrays])


def combine_kernel(sizes, spread, me_ref, *refs):
    count = sum(sizes)
    ins, outs = refs[:count], refs[count:]
    for d, out in enumerate(outs):
        start, row = 0, 0
        for size in sizes:
            terms = ins[start : start + size]
            rows = terms[0].shape[2]
            if spread:
                per = terms[0].shape[1] // len(outs)
                at = (me_ref[0] ^ d) * per
                part = total(*[ref[0, pl.ds(at, per)] for ref in terms])
            else:
                part = total(*[ref[0] for ref in terms])
            out[:, row : row + rows] = part.astype(BF16)
            start, row = start + size, row + rows


def combine(parts, me, spread=0, needs=()):
    flat = [a if isinstance(a, tuple) else (a[None], 0) for part in parts for a in part]
    pieces, _, lanes = flat[0][0].shape[1:]
    half = lanes // 2
    rows = sum((p[0][0].shape[2] if isinstance(p[0], tuple) else p[0].shape[1]) for p in parts)
    count = max(1, spread)
    outs, _ = launch(
        functools.partial(combine_kernel, [len(p) for p in parts], spread),
        [me] + [a for a, _ in flat],
        [SMEM]
        + [pl.BlockSpec((1, pieces, a.shape[2], half), lambda i, k=k: (k, 0, 0, i)) for a, k in flat],
        [shape((pieces // count, rows, lanes), BF16)] * count,
        [pl.BlockSpec((pieces // count, rows, half), lambda i: (0, 0, i))] * count,
        (),
        needs,
        grid=(2,),
        compiler_params=params(),
        cost_estimate=cost(0.1),
        name="combine",
    )
    return outs if spread else outs[0]


def spread_post_kernel(post, me_ref, *refs):
    dpost_ref, vec_ref = refs[-2:]
    for layer in range(LAYERS):

        @pl.when(pl.program_id(0) == layer)
        def _(layer=layer):
            ins = refs[layer * GROUPS : (layer + 1) * GROUPS]
            for k, ref in enumerate(ins):
                dpost_ref[0, me_ref[0] ^ k] = ref[:, :post].astype(F32)

    narrow = post * refs[0].shape[0]
    for layer in range(LAYERS):
        ins = refs[layer * GROUPS : (layer + 1) * GROUPS]
        for k, ref in enumerate(ins):
            both = ref[0, post:].astype(F32)[1:3]
            rows = [both[i // 4 : i // 4 + 1, i % 4 * narrow : (i % 4 + 1) * narrow] for i in range(8)]
            rows = jnp.concatenate(rows, 0)
            for j in range(GROUPS):

                @pl.when((me_ref[0] ^ k) == j)
                def _(j=j, rows=rows, layer=layer):
                    vec_ref[layer, :, j * narrow : (j + 1) * narrow] = rows


def spread_post(me, slots, post):
    pieces, rows, width = slots[0][0].shape
    flat = [a for layer in slots for a in layer]
    (dpost, vec), _ = launch(
        functools.partial(spread_post_kernel, post),
        [me, *flat],
        [SMEM] + [pl.BlockSpec(flat[0].shape, lambda l: (0, 0, 0))] * len(flat),
        [shape((LAYERS, GROUPS, pieces, post, width), F32), shape((LAYERS, 8, width), F32)],
        [
            pl.BlockSpec((1, GROUPS, pieces, post, width), lambda l: (l, 0, 0, 0, 0)),
            pl.BlockSpec((LAYERS, 8, width), lambda l: (0, 0, 0)),
        ],
        grid=(LAYERS,),
        compiler_params=params(),
        cost_estimate=cost(0.1),
        name="spread_post",
    )
    return dpost, vec


def fold_kernel(in_ref, out_ref):
    part = total(*[in_ref[i] for i in range(in_ref.shape[0])]).astype(BF16)
    for i in range(out_ref.shape[0]):
        out_ref[i] = part


def fold(array, through=(), needs=()):
    pieces, rows, lanes = array.shape
    block = pl.BlockSpec((pieces, rows, lanes // 2), lambda i: (0, 0, i))
    (out,), passed = launch(
        fold_kernel,
        [array],
        [block],
        [shape(array.shape, BF16)],
        [block],
        through,
        needs,
        grid=(2,),
        compiler_params=params(),
        cost_estimate=cost(0.1),
        name="fold",
    )
    return (out, *passed)


def dp_groups(pieces):
    return [list(range(i, i + pieces)) for i in range(0, lax.axis_size("dp"), pieces)]


def trade(array):
    return lax.all_to_all(
        array, "dp", split_axis=0, concat_axis=0, tiled=True,
        axis_index_groups=dp_groups(array.shape[0]),
    )


def beyond(copies):
    distance = copies.shape[0]
    while distance < lax.axis_size("dp"):
        copies = total(copies, swap(copies, "dp", distance)).astype(BF16)
        distance *= 2
    return copies


def near_dp(parts):
    return [parts[0]] + [swap(part, "dp", d) for d, part in enumerate(parts) if d]


def far_dp(mine, needs=(), block=4):
    distance = block
    while distance < lax.axis_size("dp"):
        (mine,) = add([mine, swap(mine, "dp", distance)], needs)
        distance *= 2
    return mine


def add_kernel(*refs):
    refs[-1][...] = total(*[ref[...] for ref in refs[:-1]]).astype(BF16)


def add(arrays, needs=()):
    pieces, rows, lanes = arrays[0].shape
    block = pl.BlockSpec((pieces, rows, lanes // 2), lambda i: (0, 0, i))
    outs, _ = launch(
        add_kernel,
        arrays,
        [block] * len(arrays),
        [shape(arrays[0].shape, BF16)],
        [block],
        (),
        needs,
        grid=(2,),
        compiler_params=params(),
        cost_estimate=cost(0.1),
        name="add",
    )
    return outs


def pick(array, index):
    return lax.dynamic_index_in_dim(array, index, 0, keepdims=False)


def shards(
    hidden_in,
    segment_ids,
    w_query,
    b_query,
    w_key,
    w_value,
    b_value,
    w_post,
    b_post,
    ln1_gain,
    ln1_bias,
    w_inter,
    b_inter,
    w_output,
    b_output,
    ln2_gain,
    ln2_bias,
    cotangent,
):
    row_count, narrow, seq = hidden_in.shape
    rows = row_count // GROUPS
    width = narrow * GROUPS
    ff = w_inter.shape[-1]
    head_dim = width // HEADS
    me = lax.axis_index("grp")
    me_ref = me.reshape(1).astype(jnp.int32)
    pieces = 8
    tile = 256

    by_owner = hidden_in.reshape(GROUPS, rows, narrow, seq)
    cot_owner = cotangent.reshape(GROUPS, rows, narrow, seq)
    no_bias = jnp.zeros_like(b_query)
    small = jnp.concatenate([b_query, no_bias, b_value, b_output], 2)
    small = jnp.pad(jnp.concatenate([b_inter, small], 1), ((0, 0), (0, 6), (0, 0)))
    pad = jnp.zeros((LAYERS, 1, narrow, ff - 3 * narrow), BF16)
    w_qkv = jnp.concatenate([w_query, w_key, w_value, pad], 3)
    ffn_own = jnp.concatenate([w_inter[0], w_output[0]], 0)
    both_own = jnp.concatenate([w_inter[1], w_output[1], w_qkv[1]], 0)

    segments = lax.dynamic_slice_in_dim(segment_ids, me * rows, rows, 0)
    hot = segments[:, None, :] == jnp.arange(16, dtype=segments.dtype)[None, :, None]
    masks = (hot.astype(BF16), jnp.where(hot, 0.0, MASKED).astype(BF16))

    small_far, qkv_far = swap(small, "grp", 2), swap(w_qkv[0], "grp", 2)
    smalls = [small, swap(small, "grp", 1), small_far, swap(small_far, "grp", 1)]
    qkv0 = [w_qkv[0], swap(w_qkv[0], "grp", 1), qkv_far, swap(qkv_far, "grp", 1)]
    x_slots = [pick(by_owner, me)] + [swap(pick(by_owner, me ^ k), "grp", k) for k in (1, 2, 3)]

    acts0, _ = attend(x_slots[0][None], 0, None, qkv0[:1], smalls[:1], masks, 0, head_dim)
    acts0, _ = attend(x_slots[1][None], 1, acts0, qkv0[1:2], smalls[1:2], masks, 0, head_dim)
    acts0, (ffn_own,) = attend(
        x_slots[2][None], 2, acts0, qkv0[2:3], smalls[2:3], masks, 0, head_dim, [ffn_own]
    )
    ffn_far = swap(ffn_own, "grp", 2)
    ffn0 = [ffn_own, swap(ffn_own, "grp", 1), ffn_far, swap(ffn_far, "grp", 1)]
    acts0, (both_own,) = attend(
        x_slots[3][None], 3, acts0, qkv0[3:4], smalls[3:4], masks, 0, head_dim, [both_own]
    )
    both_far = swap(both_own, "grp", 2)
    both_near = swap(both_own, "grp", 1)
    o0, qkvs0, lse0, xs0 = acts0
    vectors = (b_post, ln1_gain, ln1_bias, ln2_gain, ln2_bias)
    (state, *kept0), cot_send = mix(
        me_ref, 0, False, xs0, o0, w_post, vectors, smalls, ffn0, tile,
        [pick(cot_owner, me ^ k) for k in (1, 2, 3)],
    )
    cot_slots = [pick(cot_owner, me)[None]] + [
        swap(cot_send[k - 1], "grp", k)[None] for k in (1, 2, 3)
    ]
    acts1, (both_far,) = attend(
        state, 0, None, [both_own, both_near], smalls[:2], masks, 1, head_dim, [both_far]
    )
    both1 = [both_own, both_near, both_far, swap(both_far, "grp", 1)]
    acts1, _ = attend(state, 2, acts1, both1[2:], smalls[2:], masks, 1, head_dim)
    o1, qkvs1, lse1, xs1 = acts1
    results, _ = mix(me_ref, 1, True, xs1, o1, w_post, vectors, smalls, both1, tile)
    state_slots, kept1 = results[:GROUPS], results[GROUPS:]

    me_four = (lax.axis_index("dp") % 4).reshape(1).astype(jnp.int32)
    (da1, dout1, delta1, f_odd, f_even, p_odd, p_even), _ = mix_back(
        me_ref, 1, pieces, kept1, o1, cot_slots, w_post, vectors, smalls, both1, head_dim, tile
    )
    f_near, p_near = swap(f_odd, "grp", 1), swap(p_odd, "grp", 1)
    send = combine([[(f_even, 1), (f_near, 1)], [(p_even, 1), (p_near, 1)]], me_ref)
    far = swap(send, "grp", 2)
    acts = (xs1, qkvs1, dout1, da1, lse1, delta1)
    (gz, dw_odd1), state_send = attend_back(
        [1, 3], pieces, acts, both1, masks, head_dim, F32, True, (), state_slots[1:], (send,)
    )
    state_slots = [state_slots[0]] + [swap(state_send[k - 1], "grp", k) for k in (1, 2, 3)]
    near_q1 = swap(dw_odd1, "grp", 1)
    own_f = combine([[(f_even, 0), (f_near, 0)], [(p_even, 0), (p_near, 0)]], me_ref, 0, (dw_odd1,))
    (gz, dw_even1), _ = attend_back(
        [0, 2], pieces, acts, both1, masks, head_dim, F32, True, (gz,), (), (own_f,)
    )
    (own1,) = add([own_f, far], (dw_even1,))
    moved1 = trade(own1)
    send_q1 = combine([[(dw_even1, 1), (near_q1, 1)]], me_ref, 0, (own1,))
    far_q1 = swap(send_q1, "grp", 2)
    (da0, dout0, delta0, f_odd, f_even, p_odd, p_even), _ = mix_back(
        me_ref, 0, pieces, kept0, o0, gz, w_post, vectors, smalls, ffn0, head_dim, tile,
        (), (send_q1,),
    )
    p_near, f_near = swap(p_odd, "grp", 1), swap(f_odd, "grp", 1)
    send_p = combine([[(p_even, 1), (p_near, 1)]], me_ref)
    far_p = swap(send_p, "grp", 2)
    send_f = combine([[(f_even, 1), (f_near, 1)]], me_ref, 0, (send_p,))
    far_f = swap(send_f, "grp", 2)
    (mine1,) = fold(moved1, (), (send_f,))
    all1 = trade(beyond(mine1))
    acts = (xs0, qkvs0, dout0, da0, lse0, delta0)
    back = lambda k, kind, *needs: attend_back(
        [k], pieces, acts, qkv0, masks, head_dim, kind, False, (), (), needs
    )[0]
    gx3, dw3 = back(3, BF16, mine1, far_q1)
    near_w3 = swap(dw3, "grp", 1)
    gx3 = swap(gx3[0], "grp", 3)
    own_p = combine([[(p_even, 0), (p_near, 0), far_p]], me_four, 4, (dw3,))
    parts_p = near_dp(own_p)
    gx2, dw2 = back(2, BF16, own_p[0])
    send_w = combine([[(dw2, 0), (near_w3, 0)]], me_ref)
    far_w = swap(send_w, "grp", 2)
    gx2 = swap(gx2[0], "grp", 2)
    (mine_p,) = add(parts_p, (send_w,))
    own_f = combine(
        [[(f_even, 0), (f_near, 0), far_f], [(dw_even1, 0), (near_q1, 0), far_q1]], me_four, 4,
        (mine_p,),
    )
    parts_f = near_dp(own_f)
    gx1, dw1 = back(1, BF16, own_f[0])
    near_w1 = swap(dw1, "grp", 1)
    gx1 = swap(gx1[0], "grp", 1)
    mine_p = far_dp(mine_p, (dw1,))
    parts_p = near_dp([mine_p] * 4)
    (mine_f,) = add(parts_f, (mine_p,))
    gx0, dw0 = back(0, F32, mine_f)
    own_q = combine([[(dw0, 0), (near_w1, 0), far_w]], me_four, 4)
    parts_q = near_dp(own_q)
    mine_f = far_dp(mine_f, (own_q[0],))
    parts_f = near_dp([mine_f] * 4)
    all_p = collect(me_four, parts_p, (mine_f,), BF16).reshape(pieces, -1, width)
    grad_input = collect(me_ref, [gx0[0], gx1, gx2, gx3], (all_p,))
    (mine_q,) = add(parts_q, (grad_input,))
    hidden_out = collect(me_ref, state_slots, (mine_q,))
    all_f = collect(me_four, parts_f, (hidden_out,)).reshape(pieces, -1, ff)
    mine_q = far_dp(mine_q, (all_f,))
    all_q = collect(me_four, near_dp([mine_q] * 4)).reshape(pieces, -1, width)
    shared = [all_p, all1[:, 2 * narrow // pieces :]]

    size, post = 2 * narrow // pieces, narrow // pieces
    ffn = jnp.stack([all_f[:, :size], all1[:, :size].astype(F32)])
    ffn = ffn.reshape(LAYERS, 1, 2 * narrow, ff)
    own_rows = jnp.stack([all_p[0, post:], all1[0, size + post :]]).astype(F32)
    qkv = jnp.stack([all_q, all_f[:, size:]])
    dqkv = qkv[..., : 3 * narrow].reshape(LAYERS, 1, narrow, 3 * narrow)
    bqkv = qkv[:, :1, :2, 3 * narrow :]
    slots = []
    for layer in shared:
        far = swap(layer, "grp", 2)
        slots.append([layer, swap(layer, "grp", 1), far, swap(far, "grp", 1)])
    dpost, vec = spread_post(me_ref, slots, post)
    return (
        hidden_out.reshape(row_count, narrow, seq),
        grad_input.reshape(row_count, narrow, seq),
        dqkv[..., :narrow],
        bqkv[:, :, 0],
        dqkv[..., narrow : 2 * narrow],
        dqkv[..., 2 * narrow :],
        bqkv[:, :, 1],
        dpost.reshape(LAYERS, width, width),
        vec[:, 5],
        vec[:, 3],
        vec[:, 4],
        ffn[:, :, :narrow],
        own_rows[:, None, 0],
        ffn[:, :, narrow:],
        own_rows[:, 1].reshape(LAYERS, GROUPS, narrow)[:, 2][:, None],
        vec[:, 0],
        vec[:, 1],
    )


def solution(mesh):
    placed = (
        P("dp", "grp", None),
        P("dp", None),
        P(None, "grp", None, None),
        P(None, "grp", None),
        P(None, "grp", None, None),
        P(None, "grp", None, None),
        P(None, "grp", None),
        P(),
        P(),
        P(),
        P(),
        P(None, "grp", None, None),
        P(None, "grp", None),
        P(None, "grp", None, None),
        P(None, "grp", None),
        P(),
        P(),
        P("dp", "grp", None),
    )
    return jax.shard_map(
        shards,
        mesh=mesh,
        in_specs=placed,
        out_specs=(
            P("dp", "grp", None),
            P("dp", "grp", None),
            P(None, "grp", None, None),
            P(None, "grp", None),
            P(None, "grp", None, None),
            P(None, "grp", None, None),
            P(None, "grp", None),
            P(),
            P(),
            P(),
            P(),
            P(None, "grp", None, None),
            P(None, "grp", None),
            P(None, "grp", None, None),
            P(None, "grp", None),
            P(),
            P(),
        ),
        check_vma=False,
    )
```

```python
import functools

import jax
import jax.numpy as jnp
from jax import lax
from jax.experimental import pallas as pl
from jax.experimental.pallas import tpu as pltpu
from jax.sharding import PartitionSpec as P


HEADS = 12
LAYERS = 2
GROUPS = 4
EPSILON = 1e-05
MASKED = -1e30

F32 = jnp.float32
BF16 = jnp.bfloat16
NN = (((1,), (0,)), ((), ()))
NT = (((1,), (1,)), ((), ()))
TN = (((0,), (0,)), ((), ()))
MIB = 1 << 20


def dot(left, right, dims):
    return lax.dot_general(left, right, dims, preferred_element_type=F32)


def params(limit=60):
    return pltpu.CompilerParams(vmem_limit_bytes=limit * MIB)


def cost(micros):
    return pl.CostEstimate(flops=int(micros * 1e9), bytes_accessed=1 << 10, transcendentals=0)


def shape(dims, dtype):
    return jax.ShapeDtypeStruct(dims, dtype)


def hbm(dims, dtype):
    return pltpu.HBM(dims, dtype)


def vmem(dims, dtype):
    return pltpu.VMEM(dims, dtype)


def held(array, space=pltpu.VMEM):
    return pltpu.with_memory_space_constraint(array, space)


SMEM = pl.BlockSpec(memory_space=pltpu.SMEM)
ANY = pl.BlockSpec(memory_space=pl.ANY)


def launch(body, arrays, in_specs, outs, out_specs, through=(), needs=(), aliases=None, **kwargs):
    count, made = len(arrays), len(outs)
    extra = len(through) + len(needs)

    def kernel(*refs):
        body(*refs[:count], *refs[count + extra : count + extra + made], *refs[count + extra + made + len(through) :])

    results = pl.pallas_call(
        kernel,
        in_specs=list(in_specs) + [ANY] * extra,
        out_specs=list(out_specs) + [ANY] * len(through),
        out_shape=list(outs) + [shape(a.shape, a.dtype) for a in through],
        input_output_aliases={
            **(aliases or {}),
            **{count + i: made + i for i in range(len(through))},
        },
        **kwargs,
    )(*arrays, *through, *needs)
    return results[:made], results[made:]


def attend_kernel(head_dim, aliased, count, *refs):
    x_ref, km_ref, qm_ref = refs[:3]
    w_refs, b_refs = refs[3 : 3 + count], refs[3 + count : 3 + 2 * count]
    o_ref, qkv_ref, lse_ref, xs_ref, wt_ref, bias_ref = refs[3 + 2 * count + aliased :]
    narrow = x_ref.shape[-2]
    for k in range(count):

        @pl.when((pl.program_id(1) == 0) & (pl.program_id(0) == k))
        def _(k=k):
            wt_ref[...] = w_refs[k][0].T[: 3 * narrow]
            bias_ref[...] = b_refs[k][0].T[: 3 * narrow]

    x = x_ref[0, 0]
    xs_ref[0, 0] = x
    qkv = dot(wt_ref[...], x, NN) + bias_ref[:, 1:2]
    query = qkv[:narrow].astype(BF16) * (head_dim**-0.5)
    rest_low = qkv[narrow:].astype(BF16)
    qkv_ref[0, 0, :narrow] = query
    qkv_ref[0, 0, narrow:] = rest_low
    key_mask, query_mask = km_ref[0], qm_ref[0]
    logs = []
    for head in range(narrow // head_dim):
        lo = head * head_dim
        q_h = jnp.concatenate([query[lo : lo + head_dim], query_mask], 0)
        k_h = jnp.concatenate([rest_low[lo : lo + head_dim], key_mask], 0)
        v_h = rest_low[narrow + lo : narrow + lo + head_dim]
        scores = dot(k_h, q_h, TN)
        top = jnp.max(scores, axis=0, keepdims=True)
        raised = jnp.exp(scores - top)
        total = jnp.sum(raised, axis=0, keepdims=True)
        mixed = dot(v_h, raised.astype(BF16), NN) * (1.0 / total)
        o_ref[0, 0, lo : lo + head_dim] = mixed.astype(BF16)
        logs.append(top + jnp.log(total))
    pad = jnp.zeros((8 - len(logs), x.shape[1]), F32)
    lse_ref[0, 0] = jnp.concatenate(logs + [pad], 0)


def attend(x, first, earlier, weights, biases, masks, layer, head_dim, through=(), needs=(), kind=shape):
    stacked, rows, narrow, seq = x.shape
    count = len(weights)
    dims = [(narrow, BF16), (3 * narrow, BF16), (8, F32), (narrow, BF16)]
    at = lambda s, r: (first + s, r, 0, 0)
    prior = [] if earlier is None else list(earlier)
    lanes = weights[0].shape[2]
    block = weights[0].shape[0] - 1
    here = 3 + 2 * count
    in_specs = (
        [pl.BlockSpec((1, 1, narrow, seq), at if stacked > 1 else (lambda s, r: (s, r, 0, 0)))]
        + [pl.BlockSpec((1, 16, seq), lambda s, r: (r, 0, 0))] * 2
        + [pl.BlockSpec((1, narrow, lanes), lambda s, r: (block, 0, 0))] * count
        + [pl.BlockSpec((1, 8, biases[0].shape[2]), lambda s, r: (layer, 0, 0))] * count
        + [ANY] * len(prior)
    )
    extra = len(through) + len(needs)
    inputs = [x, *masks, *weights, *biases, *prior]
    outs = [kind((GROUPS, rows, n, seq), t) for n, t in dims]
    made, base = len(outs), len(inputs)

    def kernel(*refs):
        attend_kernel(
            head_dim, len(prior), count,
            *refs[:base], *refs[base + extra : base + extra + made],
            *refs[base + extra + made + len(through) :],
        )

    aliases = {here + i: i for i in range(len(prior))}
    aliases.update({base + i: made + i for i in range(len(through))})
    results = pl.pallas_call(
        kernel,
        grid=(count, rows),
        in_specs=in_specs + [ANY] * extra,
        out_specs=[pl.BlockSpec((1, 1, n, seq), at) for n, _ in dims] + [ANY] * len(through),
        out_shape=outs + [shape(a.shape, a.dtype) for a in through],
        scratch_shapes=[
            pltpu.VMEM((3 * narrow, narrow), BF16),
            pltpu.VMEM((3 * narrow, 8), F32),
        ],
        input_output_aliases=aliases,
        compiler_params=params(12),
        cost_estimate=cost(0.01),
        name="attend_fwd",
    )(*inputs, *through, *needs)
    return results[:made], results[made:]


def attend_back_kernel(head_dim, count, aliased, *refs):
    x_ref, qkv_ref, dout_ref, da_ref, lse_ref, delta_ref, km_ref, qm_ref = refs[:8]
    w_refs, refs = refs[8 : 8 + count], refs[8 + count + aliased :]
    gx_ref, dw_ref, acc_ref, dqkv_ref, w_ref = refs
    narrow, seq = x_ref.shape[-2:]
    place, row = pl.program_id(0), pl.program_id(1)
    for s in range(count):

        @pl.when((place == s) & (row == 0))
        def _(s=s):
            w_ref[...] = w_refs[s][0, :, : 3 * narrow]

    key_mask, query_mask = km_ref[0], qm_ref[0]
    scale = head_dim**-0.5
    for head in range(narrow // head_dim):
        lo = head * head_dim
        q_h = qkv_ref[0, 0, lo : lo + head_dim]
        k_h = qkv_ref[0, 0, narrow + lo : narrow + lo + head_dim]
        v_h = qkv_ref[0, 0, 2 * narrow + lo : 2 * narrow + lo + head_dim]
        do_h = dout_ref[0, 0, lo : lo + head_dim]
        scores = dot(
            jnp.concatenate([k_h, key_mask], 0), jnp.concatenate([q_h, query_mask], 0), TN
        )
        probs = jnp.exp(scores - lse_ref[0, 0, head : head + 1])
        grad_probs = dot(v_h, do_h, TN)
        grad_scores = (probs * (grad_probs - delta_ref[0, 0, head : head + 1])).astype(BF16)
        dqkv_ref[lo : lo + head_dim] = (dot(k_h, grad_scores, NN) * scale).astype(BF16)
        dqkv_ref[narrow + lo : narrow + lo + head_dim] = dot(q_h, grad_scores, NT).astype(BF16)
        dqkv_ref[2 * narrow + lo : 2 * narrow + lo + head_dim] = dot(
            do_h, probs.astype(BF16), NT
        ).astype(BF16)
    dqkv = dqkv_ref[...]
    gx_ref[0, 0] = (dot(w_ref[...], dqkv, NN) + da_ref[0, 0].astype(F32)).astype(gx_ref.dtype)
    ones = jnp.ones((16, seq), BF16)
    term = dot(jnp.concatenate([x_ref[0, 0], ones], 0), dqkv, NT)

    @pl.when(row == 0)
    def _():
        acc_ref[...] = term

    @pl.when(row > 0)
    def _():
        acc_ref[...] += term

    @pl.when(row == pl.num_programs(1) - 1)
    def _():
        pieces = dw_ref.shape[1]
        step = narrow // pieces
        sums = acc_ref[narrow : narrow + 1]
        extra = jnp.concatenate(
            [sums[:, :narrow], sums[:, 2 * narrow :], jnp.zeros((step - 2, narrow), F32)], 0
        ).astype(BF16)
        for piece in range(pieces):
            part = acc_ref[piece * step : (piece + 1) * step].astype(BF16)
            dw_ref[0, piece, :, : 3 * narrow] = part
            dw_ref[0, piece, :, 3 * narrow :] = extra


def attend_back(order, pieces, acts, weights, masks, head_dim, out_type, stack, earlier=(), through=(), needs=()):
    _, rows, narrow, seq = acts[0].shape
    count = len(order)
    slot = (lambda s: (2 * s + 1) % 5) if count == 4 else (lambda s: order[0] + (order[-1] - order[0]) * s)
    at = lambda s, r: (slot(s), r, 0, 0)
    block = lambda n, where: pl.BlockSpec((1, 1, n, seq), where)
    lanes = weights[0].shape[2]
    last = weights[0].shape[0] - 1
    dims = (1, pieces, narrow // pieces, lanes)
    gx_kind, gx_count = (hbm, GROUPS) if stack else (shape, count)
    outs = [gx_kind((gx_count, rows, narrow, seq), out_type), shape((count,) + dims[1:], BF16)]
    specs = [
        block(narrow, at if stack else (lambda s, r: (s, r, 0, 0))),
        pl.BlockSpec(dims, lambda s, r: (s, 0, 0, 0)),
    ]
    return launch(
        functools.partial(attend_back_kernel, head_dim, count, len(earlier)),
        [*acts, *masks, *[weights[k] for k in order], *earlier],
        [block(a.shape[2], at) for a in acts]
        + [pl.BlockSpec((1, 16, seq), lambda s, r: (r, 0, 0))] * 2
        + [pl.BlockSpec((1, narrow, lanes), lambda s, r: (last, 0, 0))] * count
        + [ANY] * len(earlier),
        outs,
        specs,
        through,
        needs,
        aliases={8 + count: 0} if earlier else {},
        grid=(count, rows),
        scratch_shapes=[
            pltpu.VMEM((narrow + 16, 3 * narrow), F32),
            pltpu.VMEM((3 * narrow, seq), BF16),
            pltpu.VMEM((narrow, 3 * narrow), BF16),
        ],
        compiler_params=params(16),
        cost_estimate=cost(3.5 * count * rows),
        name="attend_bwd",
    )


def norm(values):
    width = values.shape[0]
    center = jnp.sum(values, axis=0, keepdims=True) * (1.0 / width)
    spread = jnp.sum(values * values, axis=0, keepdims=True) * (1.0 / width) - center * center
    inverse = lax.rsqrt(spread + EPSILON)
    return (values - center) * inverse, inverse


def norm_back(weighted, scaled, inverse):
    width = weighted.shape[0]
    first = jnp.sum(weighted, axis=0, keepdims=True) * (1.0 / width)
    second = jnp.sum(weighted * scaled, axis=0, keepdims=True) * (1.0 / width)
    return inverse * (weighted - first - scaled * second)


def normal_cdf(values):
    return 0.5 + 0.5 * lax.erf(values * 0.7071067811865476)


def whole(ref, me):
    return jnp.concatenate([ref[me ^ j, 0] for j in range(GROUPS)], 0)


def columns(layer, narrow, me, vec_refs, small_refs, small_ref):
    for k in range(GROUPS):
        small_ref[me ^ k] = small_refs[k][layer]
    out_bias = jnp.concatenate([small_ref[j, 1:2, 3 * narrow :] for j in range(GROUPS)], 1)
    rows = [ref[layer : layer + 1] for ref in vec_refs] + [out_bias]
    rows += [small_ref[j, 0:1] for j in range(GROUPS)]
    rows.append(jnp.zeros((16 - len(rows), out_bias.shape[1]), F32))
    return jnp.concatenate(rows, 0).T


def first_step():
    return (pl.program_id(0) == 0) & (pl.program_id(1) == 0)


def mix_kernel(layer, split, *refs):
    me_ref, xs_ref, o_ref, wp_ref = refs[:4]
    vec_refs, small_refs, w_refs = refs[4:9], refs[9:13], refs[13:17]
    count = GROUPS if split else 1
    next_refs, refs = refs[17 : 17 + count], refs[17 + count :]
    y1_ref, xh1_ref, xh2_ref, inv_ref, wpt_ref, wit_ref, wo_ref, small_ref, state_ref = refs
    me = me_ref[0]
    narrow = xs_ref.shape[2]

    @pl.when(first_step())
    def _():
        wpt_ref[...] = wp_ref[0].T
        for k in range(GROUPS):
            wit_ref[me ^ k] = w_refs[k][0].T
            wo_ref[me ^ k] = w_refs[k][1]

    cols = columns(layer, narrow, me, vec_refs, small_refs, small_ref)
    a = dot(wpt_ref[...], whole(o_ref, me), NN) + whole(xs_ref, me).astype(F32) + cols[:, 0:1]
    scaled_one, inverse_one = norm(a)
    y1 = (scaled_one * cols[:, 1:2] + cols[:, 2:3]).astype(BF16)
    y1_ref[0] = y1
    xh1_ref[0] = scaled_one.astype(BF16)
    parts = []
    for j in range(GROUPS):
        lo = j * narrow
        y_j = y1[lo : lo + narrow]
        h = dot(wit_ref[j], y_j, NN) + cols[:, 6 + j : 7 + j]
        u = (h * normal_cdf(h)).astype(BF16)
        parts.append(y_j.astype(F32) + dot(wo_ref[j], u, NN) + cols[lo : lo + narrow, 5:6])
    scaled_two, inverse_two = norm(jnp.concatenate(parts, 0))
    xh2_ref[0] = scaled_two.astype(BF16)
    state = (scaled_two * cols[:, 3:4] + cols[:, 4:5]).astype(BF16)
    for j in range(GROUPS):
        piece = state[j * narrow : (j + 1) * narrow]
        if split:
            state_ref[j] = piece
        else:
            next_refs[0][me ^ j, 0] = piece
    if split:
        for k in range(GROUPS):
            next_refs[k][0] = state_ref[me ^ k]
    inv_ref[0] = jnp.concatenate(
        [inverse_one, inverse_two, jnp.zeros((6, inverse_one.shape[1]), F32)], 0
    )


def mix(me, layer, split, xs, o, w_post, vectors, smalls, weights, tile, through=(), needs=(), kind=shape):
    _, rows, narrow, seq = xs.shape
    width = narrow * GROUPS
    ff = weights[0].shape[2]
    stacked = pl.BlockSpec((GROUPS, 1, narrow, tile), lambda r, t: (0, r, 0, t))
    plain = lambda n: pl.BlockSpec((1, n, tile), lambda r, t: (r, 0, t))
    const = lambda a: pl.BlockSpec(a.shape, lambda r, t: (0,) * a.ndim)
    outs = [shape((rows, narrow, seq), BF16)] * GROUPS if split else [vmem(xs.shape, BF16)]
    return launch(
        functools.partial(mix_kernel, layer, split),
        [me, xs, o, w_post, *vectors, *smalls, *weights],
        [SMEM, stacked, stacked, pl.BlockSpec((1, width, width), lambda r, t: (layer, 0, 0))]
        + [const(a) for a in (*vectors, *smalls)]
        + [pl.BlockSpec((2, narrow, ff), lambda r, t: (0, 0, 0))] * GROUPS,
        outs + [kind((rows, width, seq), BF16)] * 3 + [kind((rows, 8, seq), F32)],
        ([plain(narrow)] * GROUPS if split else [stacked]) + [plain(width)] * 3 + [plain(8)],
        through,
        needs,
        grid=(rows, seq // tile),
        scratch_shapes=[
            pltpu.VMEM((width, width), BF16),
            pltpu.VMEM((GROUPS, ff, narrow), BF16),
            pltpu.VMEM((GROUPS, narrow, ff), BF16),
            pltpu.VMEM((GROUPS, 8, ff), F32),
            pltpu.VMEM((GROUPS, narrow, tile), BF16),
        ],
        compiler_params=params(16),
        cost_estimate=cost(0.01),
        name="mix_fwd",
    )


def lane_sum(values):
    total = values[:, :128]
    for lo in range(128, values.shape[1], 128):
        total = total + values[:, lo : lo + 128]
    return total


def mix_back_kernel(layer, head_dim, *refs):
    me_ref, y1_ref, xh1_ref, xh2_ref, inv_ref, o_ref = refs[:6]
    gz_refs, wp_ref, vec_refs, small_refs, w_refs = refs[6:10], refs[10], refs[11:16], refs[16:20], refs[20:24]
    da_ref, dout_ref, delta_ref, f_odd_ref, f_even_ref, p_odd_ref, p_even_ref = refs[24:31]
    accf_ref, accp_ref, accv_ref, wit_ref, wot_ref, wi_ref, small_ref, gz_ref, tail_ref = refs[31:]
    me = me_ref[0]
    narrow, tile = o_ref.shape[2:]
    width = narrow * GROUPS
    step = pl.program_id(0) * pl.num_programs(1) + pl.program_id(1)
    steps = pl.num_programs(0) * pl.num_programs(1)

    @pl.when(first_step())
    def _():
        for k in range(GROUPS):
            wit_ref[me ^ k] = w_refs[k][0].T
            wi_ref[me ^ k] = w_refs[k][0]
            wot_ref[me ^ k] = w_refs[k][1].T
        accf_ref[...] = jnp.zeros_like(accf_ref)
        accp_ref[...] = jnp.zeros_like(accp_ref)
        accv_ref[...] = jnp.zeros_like(accv_ref)

    cols = columns(layer, narrow, me, vec_refs, small_refs, small_ref)
    for k in range(GROUPS):
        gz_ref[me ^ k] = gz_refs[k][0, 0].astype(F32)
    gz = jnp.concatenate([gz_ref[j] for j in range(GROUPS)], 0)
    y1 = y1_ref[0]
    scaled_one = xh1_ref[0].astype(F32)
    scaled_two = xh2_ref[0].astype(F32)
    inverse_one, inverse_two = inv_ref[0, 0:1], inv_ref[0, 1:2]
    accv_ref[0] += lane_sum(gz * scaled_two)
    accv_ref[1] += lane_sum(gz)
    dz = norm_back(gz * cols[:, 3:4], scaled_two, inverse_two)
    df = dz.astype(BF16)
    accv_ref[2] += lane_sum(df.astype(F32))
    ones = jnp.ones((16, tile), BF16)
    parts = []
    for j in range(GROUPS):
        lo = j * narrow
        df_j, y_j = df[lo : lo + narrow], y1[lo : lo + narrow]
        h = dot(wit_ref[j], y_j, NN) + cols[:, 6 + j : 7 + j]
        cdf = normal_cdf(h)
        accf_ref[j, narrow + 16 :] += dot(df_j, (h * cdf).astype(BF16), NT)
        slope = cdf + h * jnp.exp(-0.5 * h * h) * 0.3989422804014327
        dh = (dot(wot_ref[j], df_j, NN) * slope).astype(BF16)
        accf_ref[j, : narrow + 16] += dot(jnp.concatenate([y_j, ones], 0), dh, NT)
        parts.append(dz[lo : lo + narrow] + dot(wi_ref[j], dh, NN))
    dy1 = jnp.concatenate(parts, 0).astype(BF16).astype(F32)
    accv_ref[3] += lane_sum(dy1 * scaled_one)
    accv_ref[4] += lane_sum(dy1)
    da = norm_back(dy1 * cols[:, 1:2], scaled_one, inverse_one).astype(BF16)
    o = whole(o_ref, me)
    accp_ref[...] += dot(jnp.concatenate([o, ones], 0), da, NT)
    dout = dot(wp_ref[0], da, NN).astype(BF16)
    product = (o.astype(F32) * dout.astype(F32)).reshape(width // head_dim, head_dim, tile)
    delta = jnp.sum(product, axis=1)
    per_group = narrow // head_dim
    pad = jnp.zeros((8 - per_group, tile), F32)
    for j in range(GROUPS):
        lo = j * narrow
        da_ref[me ^ j, 0] = da[lo : lo + narrow]
        dout_ref[me ^ j, 0] = dout[lo : lo + narrow]
        delta_ref[me ^ j, 0] = jnp.concatenate(
            [delta[j * per_group : (j + 1) * per_group], pad], 0
        )

    @pl.when(step == steps - 1)
    def _():
        pieces = f_odd_ref.shape[1]
        vec = [jnp.sum(accv_ref[i].T, axis=0, keepdims=True) for i in range(5)]
        vec.append(accp_ref[width : width + 1])
        half = pieces // 2
        size, post = narrow // half, narrow // pieces
        for j in range(GROUPS):
            lo = j * narrow
            own = [v[:, lo : lo + narrow] for v in vec]
            tail_ref[j] = jnp.concatenate(
                [
                    accf_ref[j, narrow : narrow + 1],
                    jnp.concatenate(own[:4], 1),
                    jnp.concatenate(own[4:] + own[4:], 1),
                    jnp.zeros((5, width), F32),
                ],
                0,
            ).astype(BF16)
        for k in range(GROUPS):
            f_ref, p_ref = (f_odd_ref, p_odd_ref) if k % 2 else (f_even_ref, p_even_ref)
            j = me ^ k
            for piece in range(pieces):
                at = (piece % half) * size + (0 if piece < half else narrow + 16)
                f_ref[k // 2, piece] = accf_ref[j, at : at + size].astype(BF16)
                at = pl.multiple_of(j * narrow + piece * post, 8)
                p_ref[k // 2, piece, :post] = accp_ref[pl.ds(at, post)].astype(BF16)
                p_ref[k // 2, piece, post:] = tail_ref[j]


def mix_back(me, layer, pieces, kept, o, gz, w_post, vectors, smalls, weights, head_dim, tile, through=(), needs=(), kind=shape):
    _, rows, narrow, seq = o.shape
    width = narrow * GROUPS
    ff = weights[0].shape[2]
    stacked = pl.BlockSpec((GROUPS, 1, narrow, tile), lambda r, t: (0, r, 0, t))
    plain = lambda n: pl.BlockSpec((1, n, tile), lambda r, t: (r, 0, t))
    const = lambda dims: pl.BlockSpec(dims, lambda r, t: (0,) * len(dims))
    if isinstance(gz, list):
        gz_specs = [pl.BlockSpec((1, 1, narrow, tile), lambda r, t: (0, r, 0, t))] * GROUPS
    else:
        gz_specs = [
            pl.BlockSpec((1, 1, narrow, tile), lambda r, t, k=k: (k, r, 0, t))
            for k in range(GROUPS)
        ]
        gz = [gz] * GROUPS
    grads_f = (2, pieces, 2 * narrow // pieces, ff)
    grads_p = (2, pieces, narrow // pieces + 8, width)
    grads = [grads_f, grads_f, grads_p, grads_p]
    return launch(
        functools.partial(mix_back_kernel, layer, head_dim),
        [me, *kept, o, *gz, w_post, *vectors, *smalls, *weights],
        [SMEM] + [plain(width)] * 3 + [plain(8), stacked] + gz_specs
        + [pl.BlockSpec((1, width, width), lambda r, t: (layer, 0, 0))]
        + [const(a.shape) for a in (*vectors, *smalls)]
        + [const((2, narrow, ff))] * GROUPS,
        [kind(o.shape, BF16)] * 2 + [kind((GROUPS, rows, 8, seq), F32)]
        + [shape(g, BF16) for g in grads],
        [stacked, stacked, pl.BlockSpec((GROUPS, 1, 8, tile), lambda r, t: (0, r, 0, t))]
        + [const(g) for g in grads],
        through,
        needs,
        grid=(rows, seq // tile),
        scratch_shapes=[
            pltpu.VMEM((GROUPS, 2 * narrow + 16, ff), F32),
            pltpu.VMEM((width + 16, width), F32),
            pltpu.VMEM((5, width, 128), F32),
            pltpu.VMEM((GROUPS, ff, narrow), BF16),
            pltpu.VMEM((GROUPS, ff, narrow), BF16),
            pltpu.VMEM((GROUPS, narrow, ff), BF16),
            pltpu.VMEM((GROUPS, 8, ff), F32),
            pltpu.VMEM((GROUPS, narrow, tile), F32),
            pltpu.VMEM((GROUPS, 8, width), BF16),
        ],
        compiler_params=params(30),
        cost_estimate=cost(24.0),
        name="mix_bwd",
    )


def swap(array, axis, distance):
    size = lax.axis_size(axis)
    return lax.ppermute(array, axis, [(i, i ^ distance) for i in range(size)])


def collect_kernel(me_ref, *refs):
    out = refs[-1]
    for k, ref in enumerate(refs[:-1]):
        out[me_ref[0] ^ k, 0] = ref[0].astype(out.dtype)


def collect(me, arrays, needs=(), dtype=F32, through=None):
    rows, rest = arrays[0].shape[0], arrays[0].shape[1:]
    zeros = (0,) * len(rest)
    (out,), passed = launch(
        collect_kernel,
        [me, *arrays],
        [SMEM] + [pl.BlockSpec((1,) + rest, lambda r: (r,) + zeros)] * GROUPS,
        [(hbm if dtype == F32 else shape)((GROUPS, rows) + rest, dtype)],
        [pl.BlockSpec((GROUPS, 1) + rest, lambda r: (0, r) + zeros)],
        through or (),
        needs,
        grid=(rows,),
        compiler_params=params(12),
        cost_estimate=cost(0.1),
        name="collect",
    )
    return out if through is None else (out, passed)


def total(*arrays):
    return functools.reduce(lambda a, b: a + b, [a.astype(F32) for a in arrays])


def combine_kernel(sizes, spread, me_ref, *refs):
    count = sum(sizes)
    ins, outs = refs[:count], refs[count:]
    for d, out in enumerate(outs):
        start, row = 0, 0
        for size in sizes:
            terms = ins[start : start + size]
            rows = terms[0].shape[2]
            if spread:
                per = terms[0].shape[1] // len(outs)
                at = (me_ref[0] ^ d) * per
                part = total(*[ref[0, pl.ds(at, per)] for ref in terms])
            else:
                part = total(*[ref[0] for ref in terms])
            out[:, row : row + rows] = part.astype(BF16)
            start, row = start + size, row + rows


def combine(parts, me, spread=0, needs=()):
    flat = [a if isinstance(a, tuple) else (a[None], 0) for part in parts for a in part]
    pieces, _, lanes = flat[0][0].shape[1:]
    half = lanes // 2
    rows = sum((p[0][0].shape[2] if isinstance(p[0], tuple) else p[0].shape[1]) for p in parts)
    count = max(1, spread)
    outs, _ = launch(
        functools.partial(combine_kernel, [len(p) for p in parts], spread),
        [me] + [a for a, _ in flat],
        [SMEM]
        + [pl.BlockSpec((1, pieces, a.shape[2], half), lambda i, k=k: (k, 0, 0, i)) for a, k in flat],
        [shape((pieces // count, rows, lanes), BF16)] * count,
        [pl.BlockSpec((pieces // count, rows, half), lambda i: (0, 0, i))] * count,
        (),
        needs,
        grid=(2,),
        compiler_params=params(12),
        cost_estimate=cost(0.1),
        name="combine",
    )
    return outs if spread else outs[0]


def finish_post_kernel(post, layers, me_ref, *refs):
    ins, refs = refs[:GROUPS], refs[GROUPS + 1 :]
    small, refs = refs[: layers * GROUPS], refs[layers * GROUPS :]
    dpost_ref, vec_refs = refs[0], refs[1:]
    me = me_ref[0]
    for k, ref in enumerate(ins):
        dpost_ref[0, me ^ k] = ref[:, :post].astype(F32)

    if layers:
        width = vec_refs[0].shape[1]
        narrow = width // GROUPS

        @pl.when(pl.program_id(0) == pl.num_programs(0) - 1)
        def _():
            for layer in range(layers):
                for k in range(GROUPS):
                    both = small[layer * GROUPS + k][0].astype(F32)
                    rows = [
                        both[1 + i // 4 : 2 + i // 4, i % 4 * narrow : (i % 4 + 1) * narrow]
                        for i in range(6)
                    ]
                    if k == 0:
                        vec_refs[6][layer] = both[0:1]
                        vec_refs[7][layer] = rows[2]
                    for j in range(GROUPS):

                        @pl.when((me ^ k) == j)
                        def _(j=j, rows=rows, layer=layer):
                            for i in range(6):
                                vec_refs[i][layer : layer + 1, j * narrow : (j + 1) * narrow] = rows[i]


def finish_post(me, layer, slots, prior, all_slots, post, needs=()):
    pieces, rows, width = slots[0].shape
    narrow = width // GROUPS
    small = [a for some in all_slots for a in some]
    outs = [hbm((LAYERS, GROUPS, pieces, post, width), F32)]
    specs = [pl.BlockSpec((1, GROUPS, pieces // 2, post, width), lambda i: (layer, 0, i, 0, 0))]
    if small:
        outs += [shape((LAYERS, width), F32)] * 6
        outs += [shape((LAYERS, 1, width), F32), shape((LAYERS, 1, narrow), F32)]
        specs += [pl.BlockSpec(o.shape, lambda i, n=len(o.shape): (0,) * n) for o in outs[1:]]
    if prior is None:
        prior, aliases = me, {}
    else:
        aliases = {1 + GROUPS: 0}
    return launch(
        functools.partial(finish_post_kernel, post, len(all_slots)),
        [me, *slots, prior, *small],
        [SMEM]
        + [pl.BlockSpec((pieces // 2, rows, width), lambda i: (i, 0, 0))] * GROUPS
        + [ANY if aliases else SMEM]
        + [pl.BlockSpec((1, 8, width), lambda i: (0, post // 8, 0))] * len(small),
        outs,
        specs,
        (),
        needs,
        aliases=aliases,
        grid=(2,),
        compiler_params=params(12),
        cost_estimate=cost(0.1),
        name="finish_post",
    )[0]


def finish_ffn_kernel(size, me_ref, *refs):
    parts, last_ref = refs[:4], refs[4]
    wi_ref, wo_ref = refs[5:]
    layer = pl.program_id(0)

    def put(shard, part):
        @pl.when(shard < 2)
        def _():
            wi_ref[0, shard] = part.astype(F32)

        @pl.when(shard >= 2)
        def _():
            wo_ref[0, shard - 2] = part.astype(F32)

    @pl.when(layer == 0)
    def _():
        for d, ref in enumerate(parts):
            put(me_ref[0] ^ d, ref[:, :size])

    @pl.when(layer > 0)
    def _():
        for d in range(4):
            put(d, last_ref[2 * d : 2 * d + 2, :size])


def finish_ffn(me, parts, last, size, needs=()):
    half, _, lanes = parts[0].shape
    out = hbm((LAYERS, 2, half, size, lanes), F32)
    return launch(
        functools.partial(finish_ffn_kernel, size),
        [me, *parts, last],
        [SMEM] + [pl.BlockSpec(a.shape, lambda l: (0, 0, 0)) for a in (*parts, last)],
        [out] * 2,
        [pl.BlockSpec((1, 2, half, size, lanes), lambda l: (l, 0, 0, 0, 0))] * 2,
        (),
        needs,
        grid=(LAYERS,),
        compiler_params=params(12),
        cost_estimate=cost(0.1),
        name="finish_ffn",
    )[0]


def finish_qkv_kernel(lo, post, me_ref, *refs):
    sets, outs = (refs[:4], refs[4:8]), refs[8:]
    narrow = outs[0].shape[-1]
    for layer, parts in enumerate(sets):
        start = lo if layer else 0
        for d, ref in enumerate(parts):
            part = ref[:, start : start + post].astype(F32)
            for i in range(3):
                outs[i][layer, me_ref[0] ^ d] = part[:, :, i * narrow : (i + 1) * narrow]
            if d == 0:
                outs[3][layer] = part[0, 0:1, 3 * narrow :]
                outs[4][layer] = part[0, 1:2, 3 * narrow :]


def finish_qkv(me, first, second, lo, narrow):
    half, post, lanes = first[0].shape
    big = shape((LAYERS, 4, half, post, narrow), F32)
    vec = shape((LAYERS, 1, narrow), F32)
    full = pl.BlockSpec(memory_space=pltpu.VMEM)
    return launch(
        functools.partial(finish_qkv_kernel, lo, post),
        [me, *first, *second],
        [SMEM] + [full] * 8,
        [big] * 3 + [vec] * 2,
        [full] * 5,
        compiler_params=params(12),
        cost_estimate=cost(0.1),
        name="finish_qkv",
    )[0]


def fold_kernel(in_ref, out_ref):
    part = total(*[in_ref[i] for i in range(in_ref.shape[0])]).astype(BF16)
    for i in range(out_ref.shape[0]):
        out_ref[i] = part


def fold(array, through=(), needs=()):
    pieces, rows, lanes = array.shape
    block = pl.BlockSpec((pieces, rows, lanes // 2), lambda i: (0, 0, i))
    (out,), passed = launch(
        fold_kernel,
        [array],
        [block],
        [shape(array.shape, BF16)],
        [block],
        through,
        needs,
        grid=(2,),
        compiler_params=params(12),
        cost_estimate=cost(0.1),
        name="fold",
    )
    return (out, *passed)


def dp_groups(pieces):
    return [list(range(i, i + pieces)) for i in range(0, lax.axis_size("dp"), pieces)]


def trade(array):
    return lax.all_to_all(
        array, "dp", split_axis=0, concat_axis=0, tiled=True,
        axis_index_groups=dp_groups(array.shape[0]),
    )


def beyond(copies):
    distance = copies.shape[0]
    while distance < lax.axis_size("dp"):
        copies = total(copies, swap(copies, "dp", distance)).astype(BF16)
        distance *= 2
    return copies


def near_dp(parts):
    return [parts[0]] + [swap(part, "dp", d) for d, part in enumerate(parts) if d]


def across_dp(sums, needs=(), block=4):
    distance = block
    while distance < lax.axis_size("dp"):
        sums = add([[mine, swap(mine, "dp", distance)] for mine in sums], (), needs)
        distance *= 2
    return sums


def add_kernel(sizes, *refs):
    ins, outs = refs[: sum(sizes)], refs[sum(sizes) :]
    start = 0
    for size, out in zip(sizes, outs):
        out[...] = total(*[ref[...] for ref in ins[start : start + size]]).astype(BF16)
        start += size


def add(lists, through=(), needs=()):
    flat = [a for arrays in lists for a in arrays]
    spec = lambda a: pl.BlockSpec(a.shape[:2] + (a.shape[2] // 2,), lambda i: (0, 0, i))
    outs, passed = launch(
        functools.partial(add_kernel, [len(arrays) for arrays in lists]),
        flat,
        [spec(a) for a in flat],
        [shape(arrays[0].shape, BF16) for arrays in lists],
        [spec(arrays[0]) for arrays in lists],
        through,
        needs,
        grid=(2,),
        compiler_params=params(16),
        cost_estimate=cost(0.1),
        name="add",
    )
    return (*outs, *passed)


def pick(array, index):
    return lax.dynamic_index_in_dim(array, index, 0, keepdims=False)


def shards(
    hidden_in,
    segment_ids,
    w_query,
    b_query,
    w_key,
    w_value,
    b_value,
    w_post,
    b_post,
    ln1_gain,
    ln1_bias,
    w_inter,
    b_inter,
    w_output,
    b_output,
    ln2_gain,
    ln2_bias,
    cotangent,
):
    row_count, narrow, seq = hidden_in.shape
    rows = row_count // GROUPS
    width = narrow * GROUPS
    ff = w_inter.shape[-1]
    head_dim = width // HEADS
    me = lax.axis_index("grp")
    me_ref = me.reshape(1).astype(jnp.int32)
    pieces = 8
    tile = 256

    by_owner = hidden_in.reshape(GROUPS, rows, narrow, seq)
    cot_owner = cotangent.reshape(GROUPS, rows, narrow, seq)
    no_bias = jnp.zeros_like(b_query)
    small = jnp.concatenate([b_query, no_bias, b_value, b_output], 2)
    small = jnp.pad(jnp.concatenate([b_inter, small], 1), ((0, 0), (0, 6), (0, 0)))
    pad = jnp.zeros((LAYERS, 1, narrow, ff - 3 * narrow), BF16)
    w_qkv = jnp.concatenate([w_query, w_key, w_value, pad], 3)
    ffn_own = jnp.concatenate([w_inter[0], w_output[0]], 0)
    both_own = jnp.concatenate([w_inter[1], w_output[1], w_qkv[1]], 0)

    segments = lax.dynamic_slice_in_dim(segment_ids, me * rows, rows, 0)
    hot = segments[:, None, :] == jnp.arange(16, dtype=segments.dtype)[None, :, None]
    masks = (hot.astype(BF16), jnp.where(hot, 0.0, MASKED).astype(BF16))

    small_far, qkv_far = swap(small, "grp", 2), swap(w_qkv[0], "grp", 2)
    smalls = [small, swap(small, "grp", 1), small_far, swap(small_far, "grp", 1)]
    qkv0 = [w_qkv[0], swap(w_qkv[0], "grp", 1), qkv_far, swap(qkv_far, "grp", 1)]
    x_slots = [pick(by_owner, me)] + [swap(pick(by_owner, me ^ k), "grp", k) for k in (1, 2, 3)]

    acts0, _ = attend(
        x_slots[0][None], 0, None, qkv0[:1], smalls[:1], masks, 0, head_dim, kind=hbm
    )
    acts0, _ = attend(
        x_slots[1][None], 1, acts0, qkv0[1:2], smalls[1:2], masks, 0, head_dim, kind=hbm
    )
    acts0, (ffn_own,) = attend(
        x_slots[2][None], 2, acts0, qkv0[2:3], smalls[2:3], masks, 0, head_dim, [ffn_own],
        kind=hbm,
    )
    ffn_far = swap(ffn_own, "grp", 2)
    ffn0 = [ffn_own, swap(ffn_own, "grp", 1), ffn_far, swap(ffn_far, "grp", 1)]
    acts0, (both_own,) = attend(
        x_slots[3][None], 3, acts0, qkv0[3:4], smalls[3:4], masks, 0, head_dim, [both_own],
        kind=hbm,
    )
    both_far = swap(both_own, "grp", 2)
    both_near = swap(both_own, "grp", 1)
    o0, qkvs0, lse0, xs0 = [held(a, pltpu.HBM) for a in acts0]
    vectors = (b_post, ln1_gain, ln1_bias, ln2_gain, ln2_bias)
    (state, *kept0), cot_send = mix(
        me_ref, 0, False, xs0, o0, w_post, vectors, smalls, ffn0, tile,
        [pick(cot_owner, me ^ k) for k in (1, 2, 3)],
        kind=hbm,
    )
    kept0 = [held(a, pltpu.HBM) for a in kept0]
    state = held(state)
    cot_slots = [pick(cot_owner, me)[None]] + [
        swap(cot_send[k - 1], "grp", k)[None] for k in (1, 2, 3)
    ]
    acts1, (both_far,) = attend(
        state, 0, None, [both_own, both_near], smalls[:2], masks, 1, head_dim, [both_far]
    )
    both1 = [both_own, both_near, both_far, swap(both_far, "grp", 1)]
    acts1, _ = attend(state, 2, acts1, both1[2:], smalls[2:], masks, 1, head_dim)
    o1, qkvs1, lse1, xs1 = acts1
    results, _ = mix(me_ref, 1, True, xs1, o1, w_post, vectors, smalls, both1, tile)
    state_slots, kept1 = results[:GROUPS], results[GROUPS:]
    state_slots = [state_slots[0]] + [swap(state_slots[k], "grp", k) for k in (1, 2, 3)]

    me_four = (lax.axis_index("dp") % 4).reshape(1).astype(jnp.int32)
    (da1, dout1, delta1, f_odd, f_even, p_odd, p_even), _ = mix_back(
        me_ref, 1, pieces, kept1, o1, cot_slots, w_post, vectors, smalls, both1, head_dim, tile
    )
    hidden_out, passed = collect(
        me_ref, state_slots, through=(da1, dout1, delta1, f_odd, f_even, p_odd, p_even)
    )
    da1, dout1, delta1, f_odd, f_even, p_odd, p_even = passed
    f_near, p_near = swap(f_odd, "grp", 1), swap(p_odd, "grp", 1)
    send = combine([[(f_even, 1), (f_near, 1)], [(p_even, 1), (p_near, 1)]], me_ref)
    far = swap(send, "grp", 2)
    acts = (xs1, qkvs1, dout1, da1, lse1, delta1)
    (gz, dw_odd1), _ = attend_back(
        [1, 3], pieces, acts, both1, masks, head_dim, F32, True, (), (), (send,)
    )
    near_q1 = swap(dw_odd1, "grp", 1)
    own_f = combine([[(f_even, 0), (f_near, 0)], [(p_even, 0), (p_near, 0)]], me_ref, 0, (dw_odd1,))
    (gz, dw_even1), _ = attend_back(
        [0, 2], pieces, acts, both1, masks, head_dim, F32, True, (gz,), (), (own_f,)
    )
    gz = held(gz, pltpu.HBM)
    (own1,) = add([[own_f, far]], (), (dw_even1,))
    moved1 = trade(own1)
    send_q1 = combine([[(dw_even1, 1), (near_q1, 1)]], me_ref, 0, (own1,))
    far_q1 = swap(send_q1, "grp", 2)
    (da0, dout0, delta0, f_odd, f_even, p_odd, p_even), _ = mix_back(
        me_ref, 0, pieces, kept0, o0, gz, w_post, vectors, smalls, ffn0, head_dim, tile,
        (), (send_q1,), hbm,
    )
    p_near, f_near = swap(p_odd, "grp", 1), swap(f_odd, "grp", 1)
    send_p = combine([[(p_even, 1), (p_near, 1)]], me_ref)
    far_p = swap(send_p, "grp", 2)
    send_f = combine([[(f_even, 1), (f_near, 1)]], me_ref, 0, (send_p,))
    far_f = swap(send_f, "grp", 2)
    dout0, da0, delta0 = [held(a, pltpu.HBM) for a in (dout0, da0, delta0)]
    acts = (xs0, qkvs0, dout0, da0, lse0, delta0)
    qkv0 = [held(w, pltpu.HBM) for w in qkv0]
    (mine1,) = fold(moved1, (), (send_f,))
    all1 = trade(beyond(mine1))
    back = lambda order, *rest: attend_back(
        order, pieces, acts, qkv0, masks, head_dim, BF16, False, (), *rest
    )
    (gx32, dw32), _ = back([3, 2], (), (mine1, far_q1))
    near_w3 = swap(dw32[:1], "grp", 1)
    own_p = combine([[(p_even, 0), (p_near, 0), far_p]], me_four, 4, (dw32,))
    parts_p = near_dp(own_p)
    send_w = combine([[(dw32, 1), (near_w3, 0)]], me_ref, 0, (own_p[0],))
    far_w = swap(send_w, "grp", 2)
    own_f = combine(
        [[(f_even, 0), (f_near, 0), far_f], [(dw_even1, 0), (near_q1, 0), far_q1]], me_four, 4,
        (send_w, all1),
    )
    parts_f = near_dp(own_f)
    size, post = 2 * narrow // pieces, narrow // pieces
    last_p = all1[:, size:]
    last_far = swap(last_p, "grp", 2)
    (mine_p,) = add([parts_p], (), (own_f[0],))
    across_p = swap(mine_p, "dp", 4)
    (gx10, dw10), _ = back([1, 0], (), (mine_p,))
    gx2, gx3 = swap(gx32[1], "grp", 2), swap(gx32[0], "grp", 3)
    mine_p, mine_f, gx10, dw10 = add(
        [[mine_p, across_p], parts_f], (gx10, dw10), (gx2, gx3, last_far)
    )
    near_w1 = swap(dw10[:1], "grp", 1)
    gx_slots = [gx10[1], swap(gx10[0], "grp", 1), gx2, gx3]
    own_q = combine([[(dw10, 1), (near_w1, 0), far_w]], me_four, 4, (mine_p,))
    parts_q = near_dp(own_q)
    (mine_p,) = across_dp([mine_p], (), 8)
    parts_p = near_dp([mine_p] * 4)
    (mine_f,) = across_dp([mine_f], (own_q[0],))
    parts_f = near_dp([mine_f] * 4)
    (mine_q,) = add([parts_q], (), (mine_f,))
    all_p = collect(me_four, parts_p, (mine_q,), BF16).reshape(pieces, -1, width)
    far_shared = swap(all_p, "grp", 2)
    near_shared = swap(all_p, "grp", 1)
    shared1 = [last_p, swap(last_p, "grp", 1), last_far, swap(last_far, "grp", 1)]
    (prior,) = finish_post(me_ref, 1, shared1, None, [], post, (own_q[0],))
    grad_input = collect(me_ref, gx_slots, (all_p,))
    (mine_q,) = across_dp([mine_q], (grad_input, prior))
    parts_q = near_dp([mine_q] * 4)
    shared0 = [all_p, near_shared, far_shared, swap(far_shared, "grp", 1)]

    dpost, *vec = finish_post(me_ref, 0, shared0, prior, [shared0, shared1], post, (mine_q,))
    d_inter, d_output = finish_ffn(me_four, parts_f, all1, size, (mine_q,))
    dq, dk, dv, dbq, dbv = finish_qkv(me_four, parts_q, parts_f, size, narrow)
    ffn_shape, qkv_shape = (LAYERS, 1, narrow, ff), (LAYERS, 1, narrow, narrow)
    return (
        hidden_out.reshape(row_count, narrow, seq),
        grad_input.reshape(row_count, narrow, seq),
        dq.reshape(qkv_shape),
        dbq,
        dk.reshape(qkv_shape),
        dv.reshape(qkv_shape),
        dbv,
        dpost.reshape(LAYERS, width, width),
        vec[5],
        vec[3],
        vec[4],
        d_inter.reshape(ffn_shape),
        vec[6],
        d_output.reshape(ffn_shape),
        vec[7],
        vec[0],
        vec[1],
    )


def solution(mesh):
    placed = (
        P("dp", "grp", None),
        P("dp", None),
        P(None, "grp", None, None),
        P(None, "grp", None),
        P(None, "grp", None, None),
        P(None, "grp", None, None),
        P(None, "grp", None),
        P(),
        P(),
        P(),
        P(),
        P(None, "grp", None, None),
        P(None, "grp", None),
        P(None, "grp", None, None),
        P(None, "grp", None),
        P(),
        P(),
        P("dp", "grp", None),
    )
    return jax.shard_map(
        shards,
        mesh=mesh,
        in_specs=placed,
        out_specs=(
            P("dp", "grp", None),
            P("dp", "grp", None),
            P(None, "grp", None, None),
            P(None, "grp", None),
            P(None, "grp", None, None),
            P(None, "grp", None, None),
            P(None, "grp", None),
            P(),
            P(),
            P(),
            P(),
            P(None, "grp", None, None),
            P(None, "grp", None),
            P(None, "grp", None, None),
            P(None, "grp", None),
            P(),
            P(),
        ),
        check_vma=False,
    )
```

```python
import functools

import jax
import jax.numpy as jnp
from jax import lax
from jax.experimental import pallas as pl
from jax.experimental.pallas import tpu as pltpu
from jax.sharding import PartitionSpec as P


HEADS = 12
LAYERS = 2
GROUPS = 4
EPSILON = 1e-05
MASKED = -1e30

F32 = jnp.float32
BF16 = jnp.bfloat16
NN = (((1,), (0,)), ((), ()))
NT = (((1,), (1,)), ((), ()))
TN = (((0,), (0,)), ((), ()))
MIB = 1 << 20


def dot(left, right, dims):
    return lax.dot_general(left, right, dims, preferred_element_type=F32)


def params(limit=60):
    return pltpu.CompilerParams(vmem_limit_bytes=limit * MIB)


def cost(micros):
    return pl.CostEstimate(flops=int(micros * 1e9), bytes_accessed=1 << 10, transcendentals=0)


def shape(dims, dtype):
    return jax.ShapeDtypeStruct(dims, dtype)


def hbm(dims, dtype):
    return pltpu.HBM(dims, dtype)


def vmem(dims, dtype):
    return pltpu.VMEM(dims, dtype)


def held(array, space=pltpu.VMEM):
    return pltpu.with_memory_space_constraint(array, space)


SMEM = pl.BlockSpec(memory_space=pltpu.SMEM)
ANY = pl.BlockSpec(memory_space=pl.ANY)


def launch(body, arrays, in_specs, outs, out_specs, through=(), needs=(), aliases=None, **kwargs):
    count, made = len(arrays), len(outs)
    extra = len(through) + len(needs)

    def kernel(*refs):
        body(*refs[:count], *refs[count + extra : count + extra + made], *refs[count + extra + made + len(through) :])

    results = pl.pallas_call(
        kernel,
        in_specs=list(in_specs) + [ANY] * extra,
        out_specs=list(out_specs) + [ANY] * len(through),
        out_shape=list(outs) + [shape(a.shape, a.dtype) for a in through],
        input_output_aliases={
            **(aliases or {}),
            **{count + i: made + i for i in range(len(through))},
        },
        **kwargs,
    )(*arrays, *through, *needs)
    return results[:made], results[made:]


def attend_kernel(head_dim, aliased, count, *refs):
    x_ref, km_ref, qm_ref = refs[:3]
    w_refs, b_refs = refs[3 : 3 + count], refs[3 + count : 3 + 2 * count]
    o_ref, qkv_ref, lse_ref, xs_ref, wt_ref, bias_ref = refs[3 + 2 * count + aliased :]
    narrow = x_ref.shape[-2]
    for k in range(count):

        @pl.when((pl.program_id(1) == 0) & (pl.program_id(0) == k))
        def _(k=k):
            wt_ref[...] = w_refs[k][0].T[: 3 * narrow]
            bias_ref[...] = b_refs[k][0].T[: 3 * narrow]

    x = x_ref[0, 0]
    xs_ref[0, 0] = x
    qkv = dot(wt_ref[...], x, NN) + bias_ref[:, 1:2]
    query = qkv[:narrow].astype(BF16) * (head_dim**-0.5)
    rest_low = qkv[narrow:].astype(BF16)
    qkv_ref[0, 0, :narrow] = query
    qkv_ref[0, 0, narrow:] = rest_low
    key_mask, query_mask = km_ref[0], qm_ref[0]
    logs = []
    if count == 1:
        for head in range(narrow // head_dim):
            lo = head * head_dim
            q_h = jnp.concatenate([query[lo : lo + head_dim], query_mask], 0)
            k_h = jnp.concatenate([rest_low[lo : lo + head_dim], key_mask], 0)
            v_h = rest_low[narrow + lo : narrow + lo + head_dim]
            scores = dot(k_h, q_h, TN)
            top = jnp.max(scores, axis=0, keepdims=True)
            raised = jnp.exp(scores - top)
            total = jnp.sum(raised, axis=0, keepdims=True)
            mixed = dot(v_h, raised.astype(BF16), NN) * (1.0 / total)
            o_ref[0, 0, lo : lo + head_dim] = mixed.astype(BF16)
            logs.append(top + jnp.log(total))
    else:
        heads = [head * head_dim for head in range(narrow // head_dim)]
        scores = [
            dot(
                jnp.concatenate([rest_low[lo : lo + head_dim], key_mask], 0),
                jnp.concatenate([query[lo : lo + head_dim], query_mask], 0),
                TN,
            )
            for lo in heads
        ]
        tops = [jnp.max(some, axis=0, keepdims=True) for some in scores]
        raised = [jnp.exp(some - top) for some, top in zip(scores, tops)]
        totals = [jnp.sum(some, axis=0, keepdims=True) for some in raised]
        for lo, some, top, total in zip(heads, raised, tops, totals):
            v_h = rest_low[narrow + lo : narrow + lo + head_dim]
            mixed = dot(v_h, some.astype(BF16), NN) * (1.0 / total)
            o_ref[0, 0, lo : lo + head_dim] = mixed.astype(BF16)
            logs.append(top + jnp.log(total))
    pad = jnp.zeros((8 - len(logs), x.shape[1]), F32)
    lse_ref[0, 0] = jnp.concatenate(logs + [pad], 0)


def attend(x, first, earlier, weights, biases, masks, layer, head_dim, through=(), needs=(), kind=shape):
    stacked, rows, narrow, seq = x.shape
    count = len(weights)
    dims = [(narrow, BF16), (3 * narrow, BF16), (8, F32), (narrow, BF16)]
    at = lambda s, r: (first + s, r, 0, 0)
    prior = [] if earlier is None else list(earlier)
    lanes = weights[0].shape[2]
    block = weights[0].shape[0] - 1
    here = 3 + 2 * count
    in_specs = (
        [pl.BlockSpec((1, 1, narrow, seq), at if stacked > 1 else (lambda s, r: (s, r, 0, 0)))]
        + [pl.BlockSpec((1, 16, seq), lambda s, r: (r, 0, 0))] * 2
        + [pl.BlockSpec((1, narrow, lanes), lambda s, r: (block, 0, 0))] * count
        + [pl.BlockSpec((1, 8, biases[0].shape[2]), lambda s, r: (layer, 0, 0))] * count
        + [ANY] * len(prior)
    )
    extra = len(through) + len(needs)
    inputs = [x, *masks, *weights, *biases, *prior]
    outs = [kind((GROUPS, rows, n, seq), t) for n, t in dims]
    made, base = len(outs), len(inputs)

    def kernel(*refs):
        attend_kernel(
            head_dim, len(prior), count,
            *refs[:base], *refs[base + extra : base + extra + made],
            *refs[base + extra + made + len(through) :],
        )

    aliases = {here + i: i for i in range(len(prior))}
    aliases.update({base + i: made + i for i in range(len(through))})
    results = pl.pallas_call(
        kernel,
        grid=(count, rows),
        in_specs=in_specs + [ANY] * extra,
        out_specs=[pl.BlockSpec((1, 1, n, seq), at) for n, _ in dims] + [ANY] * len(through),
        out_shape=outs + [shape(a.shape, a.dtype) for a in through],
        scratch_shapes=[
            pltpu.VMEM((3 * narrow, narrow), BF16),
            pltpu.VMEM((3 * narrow, 8), F32),
        ],
        input_output_aliases=aliases,
        compiler_params=params(12),
        cost_estimate=cost(0.01),
        name="attend_fwd",
    )(*inputs, *through, *needs)
    return results[:made], results[made:]


def attend_back_kernel(head_dim, count, aliased, *refs):
    x_ref, qkv_ref, dout_ref, da_ref, lse_ref, delta_ref, km_ref, qm_ref = refs[:8]
    w_refs, refs = refs[8 : 8 + count], refs[8 + count + aliased :]
    gx_ref, dw_ref, acc_ref, dqkv_ref, w_ref = refs
    narrow, seq = x_ref.shape[-2:]
    place, row = pl.program_id(0), pl.program_id(1)
    for s in range(count):

        @pl.when((place == s) & (row == 0))
        def _(s=s):
            w_ref[...] = w_refs[s][0, :, : 3 * narrow]

    key_mask, query_mask = km_ref[0], qm_ref[0]
    scale = head_dim**-0.5
    heads = [head * head_dim for head in range(narrow // head_dim)]
    queries = [qkv_ref[0, 0, lo : lo + head_dim] for lo in heads]
    keys = [qkv_ref[0, 0, narrow + lo : narrow + lo + head_dim] for lo in heads]
    grads = [dout_ref[0, 0, lo : lo + head_dim] for lo in heads]
    scores = [
        dot(jnp.concatenate([k, key_mask], 0), jnp.concatenate([q, query_mask], 0), TN)
        for q, k in zip(queries, keys)
    ]
    grad_probs = [
        dot(qkv_ref[0, 0, 2 * narrow + lo : 2 * narrow + lo + head_dim], g, TN)
        for lo, g in zip(heads, grads)
    ]
    probs = [jnp.exp(some - lse_ref[0, 0, i : i + 1]) for i, some in enumerate(scores)]
    grad_scores = [
        (p * (g - delta_ref[0, 0, i : i + 1])).astype(BF16)
        for i, (p, g) in enumerate(zip(probs, grad_probs))
    ]
    for i, lo in enumerate(heads):
        dqkv_ref[lo : lo + head_dim] = (dot(keys[i], grad_scores[i], NN) * scale).astype(BF16)
        dqkv_ref[narrow + lo : narrow + lo + head_dim] = dot(queries[i], grad_scores[i], NT).astype(BF16)
        dqkv_ref[2 * narrow + lo : 2 * narrow + lo + head_dim] = dot(
            grads[i], probs[i].astype(BF16), NT
        ).astype(BF16)
    dqkv = dqkv_ref[...]
    gx_ref[0, 0] = (dot(w_ref[...], dqkv, NN) + da_ref[0, 0].astype(F32)).astype(gx_ref.dtype)
    ones = jnp.ones((16, seq), BF16)
    term = dot(jnp.concatenate([x_ref[0, 0], ones], 0), dqkv, NT)

    @pl.when(row == 0)
    def _():
        acc_ref[...] = term

    @pl.when(row > 0)
    def _():
        acc_ref[...] += term

    @pl.when(row == pl.num_programs(1) - 1)
    def _():
        pieces = dw_ref.shape[1]
        step = narrow // pieces
        sums = acc_ref[narrow : narrow + 1]
        extra = jnp.concatenate(
            [sums[:, :narrow], sums[:, 2 * narrow :], jnp.zeros((step - 2, narrow), F32)], 0
        ).astype(BF16)
        for piece in range(pieces):
            part = acc_ref[piece * step : (piece + 1) * step].astype(BF16)
            dw_ref[0, piece, :, : 3 * narrow] = part
            dw_ref[0, piece, :, 3 * narrow :] = extra


def attend_back(order, pieces, acts, weights, masks, head_dim, out_type, stack, earlier=(), through=(), needs=()):
    _, rows, narrow, seq = acts[0].shape
    count = len(order)
    slot = (lambda s: (2 * s + 1) % 5) if count == 4 else (lambda s: order[0] + (order[-1] - order[0]) * s)
    at = lambda s, r: (slot(s), r, 0, 0)
    block = lambda n, where: pl.BlockSpec((1, 1, n, seq), where)
    lanes = weights[0].shape[2]
    last = weights[0].shape[0] - 1
    dims = (1, pieces, narrow // pieces, lanes)
    gx_kind, gx_count = (hbm, GROUPS) if stack else (shape, count)
    outs = [gx_kind((gx_count, rows, narrow, seq), out_type), shape((count,) + dims[1:], BF16)]
    specs = [
        block(narrow, at if stack else (lambda s, r: (s, r, 0, 0))),
        pl.BlockSpec(dims, lambda s, r: (s, 0, 0, 0)),
    ]
    return launch(
        functools.partial(attend_back_kernel, head_dim, count, len(earlier)),
        [*acts, *masks, *[weights[k] for k in order], *earlier],
        [block(a.shape[2], at) for a in acts]
        + [pl.BlockSpec((1, 16, seq), lambda s, r: (r, 0, 0))] * 2
        + [pl.BlockSpec((1, narrow, lanes), lambda s, r: (last, 0, 0))] * count
        + [ANY] * len(earlier),
        outs,
        specs,
        through,
        needs,
        aliases={8 + count: 0} if earlier else {},
        grid=(count, rows),
        scratch_shapes=[
            pltpu.VMEM((narrow + 16, 3 * narrow), F32),
            pltpu.VMEM((3 * narrow, seq), BF16),
            pltpu.VMEM((narrow, 3 * narrow), BF16),
        ],
        compiler_params=params(16),
        cost_estimate=cost(3.5 * count * rows),
        name="attend_bwd",
    )


def norm(values):
    width = values.shape[0]
    center = jnp.sum(values, axis=0, keepdims=True) * (1.0 / width)
    spread = jnp.sum(values * values, axis=0, keepdims=True) * (1.0 / width) - center * center
    inverse = lax.rsqrt(spread + EPSILON)
    return (values - center) * inverse, inverse


def norm_back(weighted, scaled, inverse):
    width = weighted.shape[0]
    first = jnp.sum(weighted, axis=0, keepdims=True) * (1.0 / width)
    second = jnp.sum(weighted * scaled, axis=0, keepdims=True) * (1.0 / width)
    return inverse * (weighted - first - scaled * second)


def normal_cdf(values):
    return 0.5 + 0.5 * lax.erf(values * 0.7071067811865476)


def whole(ref, me):
    return jnp.concatenate([ref[me ^ j, 0] for j in range(GROUPS)], 0)


def columns(layer, narrow, me, vec_refs, small_refs, small_ref):
    for k in range(GROUPS):
        small_ref[me ^ k] = small_refs[k][layer]
    out_bias = jnp.concatenate([small_ref[j, 1:2, 3 * narrow :] for j in range(GROUPS)], 1)
    rows = [ref[layer : layer + 1] for ref in vec_refs] + [out_bias]
    rows += [small_ref[j, 0:1] for j in range(GROUPS)]
    rows.append(jnp.zeros((16 - len(rows), out_bias.shape[1]), F32))
    return jnp.concatenate(rows, 0).T


def first_step():
    return (pl.program_id(0) == 0) & (pl.program_id(1) == 0)


def mix_kernel(layer, split, *refs):
    me_ref, xs_ref, o_ref, wp_ref = refs[:4]
    vec_refs, small_refs, w_refs = refs[4:9], refs[9:13], refs[13:17]
    count = GROUPS if split else 1
    next_refs, refs = refs[17 : 17 + count], refs[17 + count :]
    y1_ref, xh1_ref, xh2_ref, inv_ref, wpt_ref, wit_ref, wo_ref, small_ref, state_ref = refs
    me = me_ref[0]
    narrow = xs_ref.shape[2]

    @pl.when(first_step())
    def _():
        wpt_ref[...] = wp_ref[0].T
        for k in range(GROUPS):
            wit_ref[me ^ k] = w_refs[k][0].T
            wo_ref[me ^ k] = w_refs[k][1]

    cols = columns(layer, narrow, me, vec_refs, small_refs, small_ref)
    a = dot(wpt_ref[...], whole(o_ref, me), NN) + whole(xs_ref, me).astype(F32) + cols[:, 0:1]
    scaled_one, inverse_one = norm(a)
    y1 = (scaled_one * cols[:, 1:2] + cols[:, 2:3]).astype(BF16)
    y1_ref[0] = y1
    xh1_ref[0] = scaled_one.astype(BF16)
    hs = [
        dot(wit_ref[j], y1[j * narrow : (j + 1) * narrow], NN) + cols[:, 6 + j : 7 + j]
        for j in range(GROUPS)
    ]
    us = [(h * normal_cdf(h)).astype(BF16) for h in hs]
    z = jnp.concatenate([dot(wo_ref[j], us[j], NN) for j in range(GROUPS)], 0)
    scaled_two, inverse_two = norm(z + y1.astype(F32) + cols[:, 5:6])
    xh2_ref[0] = scaled_two.astype(BF16)
    state = (scaled_two * cols[:, 3:4] + cols[:, 4:5]).astype(BF16)
    for j in range(GROUPS):
        piece = state[j * narrow : (j + 1) * narrow]
        if split:
            state_ref[j] = piece
        else:
            next_refs[0][me ^ j, 0] = piece
    if split:
        for k in range(GROUPS):
            next_refs[k][0] = state_ref[me ^ k]
    inv_ref[0] = jnp.concatenate(
        [inverse_one, inverse_two, jnp.zeros((6, inverse_one.shape[1]), F32)], 0
    )


def mix(me, layer, split, xs, o, w_post, vectors, smalls, weights, tile, through=(), needs=(), kind=shape):
    _, rows, narrow, seq = xs.shape
    width = narrow * GROUPS
    ff = weights[0].shape[2]
    stacked = pl.BlockSpec((GROUPS, 1, narrow, tile), lambda r, t: (0, r, 0, t))
    plain = lambda n: pl.BlockSpec((1, n, tile), lambda r, t: (r, 0, t))
    const = lambda a: pl.BlockSpec(a.shape, lambda r, t: (0,) * a.ndim)
    outs = [shape((rows, narrow, seq), BF16)] * GROUPS if split else [vmem(xs.shape, BF16)]
    return launch(
        functools.partial(mix_kernel, layer, split),
        [me, xs, o, w_post, *vectors, *smalls, *weights],
        [SMEM, stacked, stacked, pl.BlockSpec((1, width, width), lambda r, t: (layer, 0, 0))]
        + [const(a) for a in (*vectors, *smalls)]
        + [pl.BlockSpec((2, narrow, ff), lambda r, t: (0, 0, 0))] * GROUPS,
        outs + [kind((rows, width, seq), BF16)] * 3 + [kind((rows, 8, seq), F32)],
        ([plain(narrow)] * GROUPS if split else [stacked]) + [plain(width)] * 3 + [plain(8)],
        through,
        needs,
        grid=(rows, seq // tile),
        scratch_shapes=[
            pltpu.VMEM((width, width), BF16),
            pltpu.VMEM((GROUPS, ff, narrow), BF16),
            pltpu.VMEM((GROUPS, narrow, ff), BF16),
            pltpu.VMEM((GROUPS, 8, ff), F32),
            pltpu.VMEM((GROUPS, narrow, tile), BF16),
        ],
        compiler_params=params(16),
        cost_estimate=cost(0.01),
        name="mix_fwd",
    )


def lane_sum(values):
    total = values[:, :128]
    for lo in range(128, values.shape[1], 128):
        total = total + values[:, lo : lo + 128]
    return total


def mix_back_kernel(layer, head_dim, *refs):
    me_ref, y1_ref, xh1_ref, xh2_ref, inv_ref, o_ref = refs[:6]
    gz_refs, wp_ref, vec_refs, small_refs, w_refs = refs[6:10], refs[10], refs[11:16], refs[16:20], refs[20:24]
    da_ref, dout_ref, delta_ref, f_odd_ref, f_even_ref, p_odd_ref, p_even_ref = refs[24:31]
    accf_ref, accp_ref, accv_ref, wit_ref, wot_ref, wi_ref, small_ref, gz_ref, tail_ref = refs[31:]
    me = me_ref[0]
    narrow, tile = o_ref.shape[2:]
    width = narrow * GROUPS
    step = pl.program_id(0) * pl.num_programs(1) + pl.program_id(1)
    steps = pl.num_programs(0) * pl.num_programs(1)

    @pl.when(first_step())
    def _():
        for k in range(GROUPS):
            wit_ref[me ^ k] = w_refs[k][0].T
            wi_ref[me ^ k] = w_refs[k][0]
            wot_ref[me ^ k] = w_refs[k][1].T
        accv_ref[...] = jnp.zeros_like(accv_ref)

    cols = columns(layer, narrow, me, vec_refs, small_refs, small_ref)
    for k in range(GROUPS):
        gz_ref[me ^ k] = gz_refs[k][0, 0].astype(F32)
    gz = jnp.concatenate([gz_ref[j] for j in range(GROUPS)], 0)
    y1 = y1_ref[0]
    scaled_one = xh1_ref[0].astype(F32)
    scaled_two = xh2_ref[0].astype(F32)
    inverse_one, inverse_two = inv_ref[0, 0:1], inv_ref[0, 1:2]
    accv_ref[0] += lane_sum(gz * scaled_two)
    accv_ref[1] += lane_sum(gz)
    dz = norm_back(gz * cols[:, 3:4], scaled_two, inverse_two)
    df = dz.astype(BF16)
    accv_ref[2] += lane_sum(df.astype(F32))
    ones = jnp.ones((16, tile), BF16)
    at = [slice(j * narrow, (j + 1) * narrow) for j in range(GROUPS)]
    hs = [dot(wit_ref[j], y1[at[j]], NN) + cols[:, 6 + j : 7 + j] for j in range(GROUPS)]
    back = [dot(wot_ref[j], df[at[j]], NN) for j in range(GROUPS)]
    us, dhs = [], []
    for h, some in zip(hs, back):
        cdf = normal_cdf(h)
        us.append((h * cdf).astype(BF16))
        dhs.append((some * (cdf + h * jnp.exp(-0.5 * h * h) * 0.3989422804014327)).astype(BF16))
    parts = [dz[at[j]] + dot(wi_ref[j], dhs[j], NN) for j in range(GROUPS)]
    so_far = lambda array: jnp.where(step == 0, 0.0, array)
    for j in range(GROUPS):
        out_term = dot(df[at[j]], us[j], NT)
        accf_ref[j, narrow + 16 :] = so_far(accf_ref[j, narrow + 16 :]) + out_term
        in_term = dot(jnp.concatenate([y1[at[j]], ones], 0), dhs[j], NT)
        accf_ref[j, : narrow + 16] = so_far(accf_ref[j, : narrow + 16]) + in_term
    dy1 = jnp.concatenate(parts, 0).astype(BF16).astype(F32)
    accv_ref[3] += lane_sum(dy1 * scaled_one)
    accv_ref[4] += lane_sum(dy1)
    da = norm_back(dy1 * cols[:, 1:2], scaled_one, inverse_one).astype(BF16)
    o = whole(o_ref, me)
    accp_ref[...] = so_far(accp_ref[...]) + dot(jnp.concatenate([o, ones], 0), da, NT)
    dout = dot(wp_ref[0], da, NN).astype(BF16)
    product = (o.astype(F32) * dout.astype(F32)).reshape(width // head_dim, head_dim, tile)
    delta = jnp.sum(product, axis=1)
    per_group = narrow // head_dim
    pad = jnp.zeros((8 - per_group, tile), F32)
    for j in range(GROUPS):
        lo = j * narrow
        da_ref[me ^ j, 0] = da[lo : lo + narrow]
        dout_ref[me ^ j, 0] = dout[lo : lo + narrow]
        delta_ref[me ^ j, 0] = jnp.concatenate(
            [delta[j * per_group : (j + 1) * per_group], pad], 0
        )

    @pl.when(step == steps - 1)
    def _():
        pieces = f_odd_ref.shape[1]
        vec = [jnp.sum(accv_ref[i].T, axis=0, keepdims=True) for i in range(5)]
        vec.append(accp_ref[width : width + 1])
        half = pieces // 2
        size, post = narrow // half, narrow // pieces
        for j in range(GROUPS):
            lo = j * narrow
            own = [v[:, lo : lo + narrow] for v in vec]
            tail_ref[j] = jnp.concatenate(
                [
                    accf_ref[j, narrow : narrow + 1],
                    jnp.concatenate(own[:4], 1),
                    jnp.concatenate(own[4:] + own[4:], 1),
                    jnp.zeros((5, width), F32),
                ],
                0,
            ).astype(BF16)
        for k in range(GROUPS):
            f_ref, p_ref = (f_odd_ref, p_odd_ref) if k % 2 else (f_even_ref, p_even_ref)
            j = me ^ k
            for piece in range(pieces):
                at = (piece % half) * size + (0 if piece < half else narrow + 16)
                f_ref[k // 2, piece] = accf_ref[j, at : at + size].astype(BF16)
                at = pl.multiple_of(j * narrow + piece * post, 8)
                p_ref[k // 2, piece, :post] = accp_ref[pl.ds(at, post)].astype(BF16)
                p_ref[k // 2, piece, post:] = tail_ref[j]


def mix_back(me, layer, pieces, kept, o, gz, w_post, vectors, smalls, weights, head_dim, tile, through=(), needs=(), kind=shape):
    _, rows, narrow, seq = o.shape
    width = narrow * GROUPS
    ff = weights[0].shape[2]
    stacked = pl.BlockSpec((GROUPS, 1, narrow, tile), lambda r, t: (0, r, 0, t))
    plain = lambda n: pl.BlockSpec((1, n, tile), lambda r, t: (r, 0, t))
    const = lambda dims: pl.BlockSpec(dims, lambda r, t: (0,) * len(dims))
    if isinstance(gz, list):
        gz_specs = [pl.BlockSpec((1, 1, narrow, tile), lambda r, t: (0, r, 0, t))] * GROUPS
    else:
        gz_specs = [
            pl.BlockSpec((1, 1, narrow, tile), lambda r, t, k=k: (k, r, 0, t))
            for k in range(GROUPS)
        ]
        gz = [gz] * GROUPS
    grads_f = (2, pieces, 2 * narrow // pieces, ff)
    grads_p = (2, pieces, narrow // pieces + 8, width)
    grads = [grads_f, grads_f, grads_p, grads_p]
    return launch(
        functools.partial(mix_back_kernel, layer, head_dim),
        [me, *kept, o, *gz, w_post, *vectors, *smalls, *weights],
        [SMEM] + [plain(width)] * 3 + [plain(8), stacked] + gz_specs
        + [pl.BlockSpec((1, width, width), lambda r, t: (layer, 0, 0))]
        + [const(a.shape) for a in (*vectors, *smalls)]
        + [const((2, narrow, ff))] * GROUPS,
        [kind(o.shape, BF16)] * 2 + [kind((GROUPS, rows, 8, seq), F32)]
        + [shape(g, BF16) for g in grads],
        [stacked, stacked, pl.BlockSpec((GROUPS, 1, 8, tile), lambda r, t: (0, r, 0, t))]
        + [const(g) for g in grads],
        through,
        needs,
        grid=(rows, seq // tile),
        scratch_shapes=[
            pltpu.VMEM((GROUPS, 2 * narrow + 16, ff), F32),
            pltpu.VMEM((width + 16, width), F32),
            pltpu.VMEM((5, width, 128), F32),
            pltpu.VMEM((GROUPS, ff, narrow), BF16),
            pltpu.VMEM((GROUPS, ff, narrow), BF16),
            pltpu.VMEM((GROUPS, narrow, ff), BF16),
            pltpu.VMEM((GROUPS, 8, ff), F32),
            pltpu.VMEM((GROUPS, narrow, tile), F32),
            pltpu.VMEM((GROUPS, 8, width), BF16),
        ],
        compiler_params=params(30),
        cost_estimate=cost(24.0),
        name="mix_bwd",
    )


def swap(array, axis, distance):
    size = lax.axis_size(axis)
    return lax.ppermute(array, axis, [(i, i ^ distance) for i in range(size)])


def collect_kernel(me_ref, *refs):
    out = refs[-1]
    for k, ref in enumerate(refs[:-1]):
        out[me_ref[0] ^ k, 0] = ref[0].astype(out.dtype)


def collect(me, arrays, needs=(), dtype=F32, through=None):
    rows, rest = arrays[0].shape[0], arrays[0].shape[1:]
    zeros = (0,) * len(rest)
    (out,), passed = launch(
        collect_kernel,
        [me, *arrays],
        [SMEM] + [pl.BlockSpec((1,) + rest, lambda r: (r,) + zeros)] * GROUPS,
        [(hbm if dtype == F32 else shape)((GROUPS, rows) + rest, dtype)],
        [pl.BlockSpec((GROUPS, 1) + rest, lambda r: (0, r) + zeros)],
        through or (),
        needs,
        grid=(rows,),
        compiler_params=params(12),
        cost_estimate=cost(0.1),
        name="collect",
    )
    return out if through is None else (out, passed)


def total(*arrays):
    return functools.reduce(lambda a, b: a + b, [a.astype(F32) for a in arrays])


def combine_kernel(sizes, spread, me_ref, *refs):
    count = sum(sizes)
    ins, outs = refs[:count], refs[count:]
    for d, out in enumerate(outs):
        start, row = 0, 0
        for size in sizes:
            terms = ins[start : start + size]
            rows = terms[0].shape[2]
            if spread:
                per = terms[0].shape[1] // len(outs)
                at = (me_ref[0] ^ d) * per
                part = total(*[ref[0, pl.ds(at, per)] for ref in terms])
            else:
                part = total(*[ref[0] for ref in terms])
            out[:, row : row + rows] = part.astype(BF16)
            start, row = start + size, row + rows


def combine(parts, me, spread=0, needs=()):
    flat = [a if isinstance(a, tuple) else (a[None], 0) for part in parts for a in part]
    pieces, _, lanes = flat[0][0].shape[1:]
    rows = sum((p[0][0].shape[2] if isinstance(p[0], tuple) else p[0].shape[1]) for p in parts)
    count = max(1, spread)
    outs, _ = launch(
        functools.partial(combine_kernel, [len(p) for p in parts], spread),
        [me] + [a for a, _ in flat],
        [SMEM]
        + [pl.BlockSpec((1, pieces, a.shape[2], lanes), lambda i, k=k: (k, 0, 0, 0)) for a, k in flat],
        [shape((pieces // count, rows, lanes), BF16)] * count,
        [pl.BlockSpec((pieces // count, rows, lanes), lambda i: (0, 0, 0))] * count,
        (),
        needs,
        grid=(1,),
        compiler_params=params(12),
        cost_estimate=cost(0.1),
        name="combine",
    )
    return outs if spread else outs[0]


def finish_post_kernel(post, layers, me_ref, *refs):
    ins, refs = refs[:GROUPS], refs[GROUPS + 1 :]
    small, refs = refs[: layers * GROUPS], refs[layers * GROUPS :]
    dpost_ref, vec_refs = refs[0], refs[1:]
    me = me_ref[0]
    for k, ref in enumerate(ins):
        dpost_ref[0, me ^ k] = ref[:, :post].astype(F32)

    if layers:
        width = vec_refs[0].shape[1]
        narrow = width // GROUPS

        @pl.when(pl.program_id(0) == pl.num_programs(0) - 1)
        def _():
            for layer in range(layers):
                for k in range(GROUPS):
                    both = small[layer * GROUPS + k][0].astype(F32)
                    rows = [
                        both[1 + i // 4 : 2 + i // 4, i % 4 * narrow : (i % 4 + 1) * narrow]
                        for i in range(6)
                    ]
                    if k == 0:
                        vec_refs[6][layer] = both[0:1]
                        vec_refs[7][layer] = rows[2]
                    for j in range(GROUPS):

                        @pl.when((me ^ k) == j)
                        def _(j=j, rows=rows, layer=layer):
                            for i in range(6):
                                vec_refs[i][layer : layer + 1, j * narrow : (j + 1) * narrow] = rows[i]


def finish_post(me, layer, slots, prior, all_slots, post, needs=()):
    pieces, rows, width = slots[0].shape
    narrow = width // GROUPS
    small = [a for some in all_slots for a in some]
    outs = [hbm((LAYERS, GROUPS, pieces, post, width), F32)]
    specs = [pl.BlockSpec((1, GROUPS, pieces // 2, post, width), lambda i: (layer, 0, i, 0, 0))]
    if small:
        outs += [shape((LAYERS, width), F32)] * 6
        outs += [shape((LAYERS, 1, width), F32), shape((LAYERS, 1, narrow), F32)]
        specs += [pl.BlockSpec(o.shape, lambda i, n=len(o.shape): (0,) * n) for o in outs[1:]]
    if prior is None:
        prior, aliases = me, {}
    else:
        aliases = {1 + GROUPS: 0}
    return launch(
        functools.partial(finish_post_kernel, post, len(all_slots)),
        [me, *slots, prior, *small],
        [SMEM]
        + [pl.BlockSpec((pieces // 2, rows, width), lambda i: (i, 0, 0))] * GROUPS
        + [ANY if aliases else SMEM]
        + [pl.BlockSpec((1, 8, width), lambda i: (0, post // 8, 0))] * len(small),
        outs,
        specs,
        (),
        needs,
        aliases=aliases,
        grid=(2,),
        compiler_params=params(12),
        cost_estimate=cost(0.1),
        name="finish_post",
    )[0]


def finish_ffn_kernel(size, me_ref, *refs):
    parts, last_ref = refs[:4], refs[4]
    wi_ref, wo_ref = refs[5:]
    layer = pl.program_id(0)

    def put(shard, part):
        @pl.when(shard < 2)
        def _():
            wi_ref[0, shard] = part.astype(F32)

        @pl.when(shard >= 2)
        def _():
            wo_ref[0, shard - 2] = part.astype(F32)

    @pl.when(layer == 0)
    def _():
        for d, ref in enumerate(parts):
            put(me_ref[0] ^ d, ref[:, :size])

    @pl.when(layer > 0)
    def _():
        for d in range(4):
            put(d, last_ref[2 * d : 2 * d + 2, :size])


def finish_ffn(me, parts, last, size, needs=()):
    half, _, lanes = parts[0].shape
    out = hbm((LAYERS, 2, half, size, lanes), F32)
    return launch(
        functools.partial(finish_ffn_kernel, size),
        [me, *parts, last],
        [SMEM] + [pl.BlockSpec(a.shape, lambda l: (0, 0, 0)) for a in (*parts, last)],
        [out] * 2,
        [pl.BlockSpec((1, 2, half, size, lanes), lambda l: (l, 0, 0, 0, 0))] * 2,
        (),
        needs,
        grid=(LAYERS,),
        compiler_params=params(12),
        cost_estimate=cost(0.1),
        name="finish_ffn",
    )[0]


def finish_qkv_kernel(lo, post, me_ref, *refs):
    sets, outs = (refs[:4], refs[4:8]), refs[8:]
    narrow = outs[0].shape[-1]
    for layer, parts in enumerate(sets):
        start = lo if layer else 0
        for d, ref in enumerate(parts):
            part = ref[:, start : start + post].astype(F32)
            for i in range(3):
                outs[i][layer, me_ref[0] ^ d] = part[:, :, i * narrow : (i + 1) * narrow]
            if d == 0:
                outs[3][layer] = part[0, 0:1, 3 * narrow :]
                outs[4][layer] = part[0, 1:2, 3 * narrow :]


def finish_qkv(me, first, second, lo, narrow):
    half, post, lanes = first[0].shape
    big = shape((LAYERS, 4, half, post, narrow), F32)
    vec = shape((LAYERS, 1, narrow), F32)
    full = pl.BlockSpec(memory_space=pltpu.VMEM)
    return launch(
        functools.partial(finish_qkv_kernel, lo, post),
        [me, *first, *second],
        [SMEM] + [full] * 8,
        [big] * 3 + [vec] * 2,
        [full] * 5,
        compiler_params=params(12),
        cost_estimate=cost(0.1),
        name="finish_qkv",
    )[0]


def fold_kernel(in_ref, out_ref):
    part = total(*[in_ref[i] for i in range(in_ref.shape[0])]).astype(BF16)
    for i in range(out_ref.shape[0]):
        out_ref[i] = part


def fold(array, through=(), needs=()):
    pieces, rows, lanes = array.shape
    block = pl.BlockSpec((pieces, rows, lanes), lambda i: (0, 0, 0))
    (out,), passed = launch(
        fold_kernel,
        [array],
        [block],
        [shape(array.shape, BF16)],
        [block],
        through,
        needs,
        grid=(1,),
        compiler_params=params(12),
        cost_estimate=cost(0.1),
        name="fold",
    )
    return (out, *passed)


def dp_groups(pieces):
    return [list(range(i, i + pieces)) for i in range(0, lax.axis_size("dp"), pieces)]


def trade(array):
    return lax.all_to_all(
        array, "dp", split_axis=0, concat_axis=0, tiled=True,
        axis_index_groups=dp_groups(array.shape[0]),
    )


def beyond(copies):
    distance = copies.shape[0]
    while distance < lax.axis_size("dp"):
        copies = total(copies, swap(copies, "dp", distance)).astype(BF16)
        distance *= 2
    return copies


def near_dp(parts):
    return [parts[0]] + [swap(part, "dp", d) for d, part in enumerate(parts) if d]


def across_dp(sums, needs=(), block=4):
    distance = block
    while distance < lax.axis_size("dp"):
        sums = add([[mine, swap(mine, "dp", distance)] for mine in sums], (), needs)
        distance *= 2
    return sums


def add_kernel(sizes, *refs):
    ins, outs = refs[: sum(sizes)], refs[sum(sizes) :]
    start = 0
    for size, out in zip(sizes, outs):
        out[...] = total(*[ref[...] for ref in ins[start : start + size]]).astype(BF16)
        start += size


def add(lists, through=(), needs=(), micros=0.1):
    flat = [a for arrays in lists for a in arrays]
    spec = lambda a: pl.BlockSpec(a.shape, lambda i: (0, 0, 0))
    outs, passed = launch(
        functools.partial(add_kernel, [len(arrays) for arrays in lists]),
        flat,
        [spec(a) for a in flat],
        [shape(arrays[0].shape, BF16) for arrays in lists],
        [spec(arrays[0]) for arrays in lists],
        through,
        needs,
        grid=(1,),
        compiler_params=params(16),
        cost_estimate=cost(micros),
        name="add",
    )
    return (*outs, *passed)


def pick(array, index):
    return lax.dynamic_index_in_dim(array, index, 0, keepdims=False)


def shards(
    hidden_in,
    segment_ids,
    w_query,
    b_query,
    w_key,
    w_value,
    b_value,
    w_post,
    b_post,
    ln1_gain,
    ln1_bias,
    w_inter,
    b_inter,
    w_output,
    b_output,
    ln2_gain,
    ln2_bias,
    cotangent,
):
    row_count, narrow, seq = hidden_in.shape
    rows = row_count // GROUPS
    width = narrow * GROUPS
    ff = w_inter.shape[-1]
    head_dim = width // HEADS
    me = lax.axis_index("grp")
    me_ref = me.reshape(1).astype(jnp.int32)
    pieces = 8
    tile = 256

    by_owner = hidden_in.reshape(GROUPS, rows, narrow, seq)
    cot_owner = cotangent.reshape(GROUPS, rows, narrow, seq)
    no_bias = jnp.zeros_like(b_query)
    small = jnp.concatenate([b_query, no_bias, b_value, b_output], 2)
    small = jnp.pad(jnp.concatenate([b_inter, small], 1), ((0, 0), (0, 6), (0, 0)))
    pad = jnp.zeros((LAYERS, 1, narrow, ff - 3 * narrow), BF16)
    w_qkv = jnp.concatenate([w_query, w_key, w_value, pad], 3)
    ffn_own = jnp.concatenate([w_inter[0], w_output[0]], 0)
    both_own = jnp.concatenate([w_inter[1], w_output[1], w_qkv[1]], 0)

    segments = lax.dynamic_slice_in_dim(segment_ids, me * rows, rows, 0)
    hot = segments[:, None, :] == jnp.arange(16, dtype=segments.dtype)[None, :, None]
    masks = (hot.astype(BF16), jnp.where(hot, 0.0, MASKED).astype(BF16))

    small_far, qkv_far = swap(small, "grp", 2), swap(w_qkv[0], "grp", 2)
    smalls = [small, swap(small, "grp", 1), small_far, swap(small_far, "grp", 1)]
    qkv0 = [w_qkv[0], swap(w_qkv[0], "grp", 1), qkv_far, swap(qkv_far, "grp", 1)]
    x_slots = [pick(by_owner, me)] + [swap(pick(by_owner, me ^ k), "grp", k) for k in (1, 2, 3)]

    acts0, _ = attend(
        x_slots[0][None], 0, None, qkv0[:1], smalls[:1], masks, 0, head_dim, kind=hbm
    )
    acts0, _ = attend(
        x_slots[1][None], 1, acts0, qkv0[1:2], smalls[1:2], masks, 0, head_dim, kind=hbm
    )
    acts0, (ffn_own,) = attend(
        x_slots[2][None], 2, acts0, qkv0[2:3], smalls[2:3], masks, 0, head_dim, [ffn_own],
        kind=hbm,
    )
    ffn_far = swap(ffn_own, "grp", 2)
    ffn0 = [ffn_own, swap(ffn_own, "grp", 1), ffn_far, swap(ffn_far, "grp", 1)]
    acts0, (both_own,) = attend(
        x_slots[3][None], 3, acts0, qkv0[3:4], smalls[3:4], masks, 0, head_dim, [both_own],
        kind=hbm,
    )
    both_far = swap(both_own, "grp", 2)
    both_near = swap(both_own, "grp", 1)
    o0, qkvs0, lse0, xs0 = [held(a, pltpu.HBM) for a in acts0]
    vectors = (b_post, ln1_gain, ln1_bias, ln2_gain, ln2_bias)
    (state, *kept0), cot_send = mix(
        me_ref, 0, False, xs0, o0, w_post, vectors, smalls, ffn0, tile,
        [pick(cot_owner, me ^ k) for k in (1, 2, 3)],
        kind=hbm,
    )
    kept0 = [held(a, pltpu.HBM) for a in kept0]
    state = held(state)
    cot_slots = [pick(cot_owner, me)[None]] + [
        swap(cot_send[k - 1], "grp", k)[None] for k in (1, 2, 3)
    ]
    acts1, (both_far,) = attend(
        state, 0, None, [both_own, both_near], smalls[:2], masks, 1, head_dim, [both_far]
    )
    both1 = [both_own, both_near, both_far, swap(both_far, "grp", 1)]
    acts1, _ = attend(state, 2, acts1, both1[2:], smalls[2:], masks, 1, head_dim)
    o1, qkvs1, lse1, xs1 = acts1
    results, _ = mix(me_ref, 1, True, xs1, o1, w_post, vectors, smalls, both1, tile)
    state_slots, kept1 = results[:GROUPS], results[GROUPS:]
    state_slots = [state_slots[0]] + [swap(state_slots[k], "grp", k) for k in (1, 2, 3)]

    me_four = (lax.axis_index("dp") % 4).reshape(1).astype(jnp.int32)
    (da1, dout1, delta1, f_odd, f_even, p_odd, p_even), _ = mix_back(
        me_ref, 1, pieces, kept1, o1, cot_slots, w_post, vectors, smalls, both1, head_dim, tile
    )
    hidden_out, passed = collect(
        me_ref, state_slots, through=(da1, dout1, delta1, f_odd, f_even, p_odd, p_even)
    )
    da1, dout1, delta1, f_odd, f_even, p_odd, p_even = passed
    f_near, p_near = swap(f_odd, "grp", 1), swap(p_odd, "grp", 1)
    send = combine([[(f_even, 1), (f_near, 1)], [(p_even, 1), (p_near, 1)]], me_ref)
    far = swap(send, "grp", 2)
    acts = (xs1, qkvs1, dout1, da1, lse1, delta1)
    (gz, dw_odd1), _ = attend_back(
        [1, 3], pieces, acts, both1, masks, head_dim, F32, True, (), (), (send,)
    )
    near_q1 = swap(dw_odd1, "grp", 1)
    own_f = combine([[(f_even, 0), (f_near, 0)], [(p_even, 0), (p_near, 0)]], me_ref, 0, (dw_odd1,))
    (gz, dw_even1), _ = attend_back(
        [0, 2], pieces, acts, both1, masks, head_dim, F32, True, (gz,), (), (own_f,)
    )
    gz = held(gz, pltpu.HBM)
    (own1,) = add([[own_f, far]], (), (dw_even1,))
    moved1 = trade(own1)
    send_q1 = combine([[(dw_even1, 1), (near_q1, 1)]], me_ref, 0, (own1,))
    far_q1 = swap(send_q1, "grp", 2)
    (da0, dout0, delta0, f_odd, f_even, p_odd, p_even), _ = mix_back(
        me_ref, 0, pieces, kept0, o0, gz, w_post, vectors, smalls, ffn0, head_dim, tile,
        (), (send_q1,), hbm,
    )
    p_near, f_near = swap(p_odd, "grp", 1), swap(f_odd, "grp", 1)
    send_p = combine([[(p_even, 1), (p_near, 1)]], me_ref)
    far_p = swap(send_p, "grp", 2)
    send_f = combine([[(f_even, 1), (f_near, 1)]], me_ref, 0, (send_p,))
    far_f = swap(send_f, "grp", 2)
    dout0, da0, delta0 = [held(a, pltpu.HBM) for a in (dout0, da0, delta0)]
    acts = (xs0, qkvs0, dout0, da0, lse0, delta0)
    qkv0 = [held(w, pltpu.HBM) for w in qkv0]
    (mine1,) = fold(moved1, (), (send_f,))
    all1 = trade(beyond(mine1))
    back = lambda order, *rest: attend_back(
        order, pieces, acts, qkv0, masks, head_dim, BF16, False, (), *rest
    )
    (gx32, dw32), _ = back([3, 2], (), (mine1, far_q1))
    near_w3 = swap(dw32[:1], "grp", 1)
    own_p = combine([[(p_even, 0), (p_near, 0), far_p]], me_four, 4, (dw32,))
    parts_p = near_dp(own_p)
    send_w = combine([[(dw32, 1), (near_w3, 0)]], me_ref, 0, (own_p[0],))
    far_w = swap(send_w, "grp", 2)
    own_f = combine(
        [[(f_even, 0), (f_near, 0), far_f], [(dw_even1, 0), (near_q1, 0), far_q1]], me_four, 4,
        (send_w, all1),
    )
    parts_f = near_dp(own_f)
    size, post = 2 * narrow // pieces, narrow // pieces
    last_p = all1[:, size:]
    last_far = swap(last_p, "grp", 2)
    (mine_p,) = add([parts_p], (), (own_f[0],))
    across_p = swap(mine_p, "dp", 4)
    (gx10, dw10), _ = back([1, 0], (), (mine_p,))
    gx2, gx3 = swap(gx32[1], "grp", 2), swap(gx32[0], "grp", 3)
    mine_p, mine_f, gx10, dw10 = add(
        [[mine_p, across_p], parts_f], (gx10, dw10), (gx2, gx3, last_far, far_w)
    )
    near_w1 = swap(dw10[:1], "grp", 1)
    gx_slots = [gx10[1], swap(gx10[0], "grp", 1), gx2, gx3]
    own_q = combine([[(dw10, 1), (near_w1, 0), far_w]], me_four, 4, (mine_p,))
    parts_q = near_dp(own_q)
    (mine_p,) = across_dp([mine_p], (), 8)
    parts_p = near_dp([mine_p] * 4)
    across_f = swap(mine_f, "dp", 4)
    (mine_q,) = add([parts_q])
    across_q = swap(mine_q, "dp", 4)
    (mine_f,) = add([[mine_f, across_f]], (), (mine_q,))
    (mine_f,) = across_dp([mine_f], (), 8)
    parts_f = near_dp([mine_f] * 4)
    all_p = collect(me_four, parts_p, (mine_f,), BF16).reshape(pieces, -1, width)
    far_shared = swap(all_p, "grp", 2)
    near_shared = swap(all_p, "grp", 1)
    shared1 = [last_p, swap(last_p, "grp", 1), last_far, swap(last_far, "grp", 1)]
    (prior,) = finish_post(me_ref, 1, shared1, None, [], post, (all_p,))
    grad_input = collect(me_ref, gx_slots, (held(prior, pltpu.HBM),))
    mine_q, far_shared = add(
        [[mine_q, across_q]], (far_shared,), (held(grad_input, pltpu.HBM),), 10.0
    )
    (mine_q,) = across_dp([mine_q], (), 8)
    parts_q = near_dp([mine_q] * 4)
    shared0 = [all_p, near_shared, far_shared, swap(far_shared, "grp", 1)]

    dpost, *vec = finish_post(me_ref, 0, shared0, prior, [shared0, shared1], post, (mine_q,))
    d_inter, d_output = finish_ffn(me_four, parts_f, all1, size, (mine_q,))
    dq, dk, dv, dbq, dbv = finish_qkv(me_four, parts_q, parts_f, size, narrow)
    ffn_shape, qkv_shape = (LAYERS, 1, narrow, ff), (LAYERS, 1, narrow, narrow)
    return (
        hidden_out.reshape(row_count, narrow, seq),
        grad_input.reshape(row_count, narrow, seq),
        dq.reshape(qkv_shape),
        dbq,
        dk.reshape(qkv_shape),
        dv.reshape(qkv_shape),
        dbv,
        dpost.reshape(LAYERS, width, width),
        vec[5],
        vec[3],
        vec[4],
        d_inter.reshape(ffn_shape),
        vec[6],
        d_output.reshape(ffn_shape),
        vec[7],
        vec[0],
        vec[1],
    )


def solution(mesh):
    placed = (
        P("dp", "grp", None),
        P("dp", None),
        P(None, "grp", None, None),
        P(None, "grp", None),
        P(None, "grp", None, None),
        P(None, "grp", None, None),
        P(None, "grp", None),
        P(),
        P(),
        P(),
        P(),
        P(None, "grp", None, None),
        P(None, "grp", None),
        P(None, "grp", None, None),
        P(None, "grp", None),
        P(),
        P(),
        P("dp", "grp", None),
    )
    return jax.shard_map(
        shards,
        mesh=mesh,
        in_specs=placed,
        out_specs=(
            P("dp", "grp", None),
            P("dp", "grp", None),
            P(None, "grp", None, None),
            P(None, "grp", None),
            P(None, "grp", None, None),
            P(None, "grp", None, None),
            P(None, "grp", None),
            P(),
            P(),
            P(),
            P(),
            P(None, "grp", None, None),
            P(None, "grp", None),
            P(None, "grp", None, None),
            P(None, "grp", None),
            P(),
            P(),
        ),
        check_vma=False,
    )
```

```python
import functools

import jax
import jax.numpy as jnp
from jax import lax
from jax.experimental import pallas as pl
from jax.experimental.pallas import tpu as pltpu
from jax.sharding import PartitionSpec as P


HEADS = 12
LAYERS = 2
GROUPS = 4
EPSILON = 1e-05
MASKED = -1e30

F32 = jnp.float32
BF16 = jnp.bfloat16
NN = (((1,), (0,)), ((), ()))
NT = (((1,), (1,)), ((), ()))
TN = (((0,), (0,)), ((), ()))
MIB = 1 << 20


def dot(left, right, dims):
    return lax.dot_general(left, right, dims, preferred_element_type=F32)


def params(limit=60):
    return pltpu.CompilerParams(vmem_limit_bytes=limit * MIB)


def cost(micros):
    return pl.CostEstimate(flops=int(micros * 1e9), bytes_accessed=1 << 10, transcendentals=0)


def shape(dims, dtype):
    return jax.ShapeDtypeStruct(dims, dtype)


def hbm(dims, dtype):
    return pltpu.HBM(dims, dtype)


def vmem(dims, dtype):
    return pltpu.VMEM(dims, dtype)


def held(array, space=pltpu.VMEM):
    return pltpu.with_memory_space_constraint(array, space)


SMEM = pl.BlockSpec(memory_space=pltpu.SMEM)
ANY = pl.BlockSpec(memory_space=pl.ANY)


def launch(body, arrays, in_specs, outs, out_specs, through=(), needs=(), aliases=None, **kwargs):
    count, made = len(arrays), len(outs)
    extra = len(through) + len(needs)

    def kernel(*refs):
        body(*refs[:count], *refs[count + extra : count + extra + made], *refs[count + extra + made + len(through) :])

    results = pl.pallas_call(
        kernel,
        in_specs=list(in_specs) + [ANY] * extra,
        out_specs=list(out_specs) + [ANY] * len(through),
        out_shape=list(outs) + [shape(a.shape, a.dtype) for a in through],
        input_output_aliases={
            **(aliases or {}),
            **{count + i: made + i for i in range(len(through))},
        },
        **kwargs,
    )(*arrays, *through, *needs)
    return results[:made], results[made:]


def attend_kernel(head_dim, aliased, count, *refs):
    x_ref, km_ref, qm_ref = refs[:3]
    w_refs, b_refs = refs[3 : 3 + count], refs[3 + count : 3 + 2 * count]
    o_ref, qkv_ref, lse_ref, xs_ref, wt_ref, bias_ref = refs[3 + 2 * count + aliased :]
    narrow = x_ref.shape[-2]
    for k in range(count):

        @pl.when((pl.program_id(1) == 0) & (pl.program_id(0) == k))
        def _(k=k):
            wt_ref[...] = w_refs[k][0].T[: 3 * narrow]
            bias_ref[...] = b_refs[k][0].T[: 3 * narrow]

    x = x_ref[0, 0]
    xs_ref[0, 0] = x
    qkv = dot(wt_ref[...], x, NN) + bias_ref[:, 1:2]
    query = qkv[:narrow].astype(BF16) * (head_dim**-0.5)
    rest_low = qkv[narrow:].astype(BF16)
    qkv_ref[0, 0, :narrow] = query
    qkv_ref[0, 0, narrow:] = rest_low
    key_mask, query_mask = km_ref[0], qm_ref[0]
    logs = []
    if count == 1:
        for head in range(narrow // head_dim):
            lo = head * head_dim
            q_h = jnp.concatenate([query[lo : lo + head_dim], query_mask], 0)
            k_h = jnp.concatenate([rest_low[lo : lo + head_dim], key_mask], 0)
            v_h = rest_low[narrow + lo : narrow + lo + head_dim]
            scores = dot(k_h, q_h, TN)
            top = jnp.max(scores, axis=0, keepdims=True)
            raised = jnp.exp(scores - top)
            total = jnp.sum(raised, axis=0, keepdims=True)
            mixed = dot(v_h, raised.astype(BF16), NN) * (1.0 / total)
            o_ref[0, 0, lo : lo + head_dim] = mixed.astype(BF16)
            logs.append(top + jnp.log(total))
    else:
        heads = [head * head_dim for head in range(narrow // head_dim)]
        scores = [
            dot(
                jnp.concatenate([rest_low[lo : lo + head_dim], key_mask], 0),
                jnp.concatenate([query[lo : lo + head_dim], query_mask], 0),
                TN,
            )
            for lo in heads
        ]
        tops = [jnp.max(some, axis=0, keepdims=True) for some in scores]
        raised = [jnp.exp(some - top) for some, top in zip(scores, tops)]
        totals = [jnp.sum(some, axis=0, keepdims=True) for some in raised]
        for lo, some, top, total in zip(heads, raised, tops, totals):
            v_h = rest_low[narrow + lo : narrow + lo + head_dim]
            mixed = dot(v_h, some.astype(BF16), NN) * (1.0 / total)
            o_ref[0, 0, lo : lo + head_dim] = mixed.astype(BF16)
            logs.append(top + jnp.log(total))
    pad = jnp.zeros((8 - len(logs), x.shape[1]), F32)
    lse_ref[0, 0] = jnp.concatenate(logs + [pad], 0)


def attend(x, first, earlier, weights, biases, masks, layer, head_dim, through=(), needs=(), kind=shape):
    stacked, rows, narrow, seq = x.shape
    count = len(weights)
    dims = [(narrow, BF16), (3 * narrow, BF16), (8, F32), (narrow, BF16)]
    at = lambda s, r: (first + s, r, 0, 0)
    prior = [] if earlier is None else list(earlier)
    lanes = weights[0].shape[2]
    block = weights[0].shape[0] - 1
    here = 3 + 2 * count
    in_specs = (
        [pl.BlockSpec((1, 1, narrow, seq), at if stacked > 1 else (lambda s, r: (s, r, 0, 0)))]
        + [pl.BlockSpec((1, 16, seq), lambda s, r: (r, 0, 0))] * 2
        + [pl.BlockSpec((1, narrow, lanes), lambda s, r: (block, 0, 0))] * count
        + [pl.BlockSpec((1, 8, biases[0].shape[2]), lambda s, r: (layer, 0, 0))] * count
        + [ANY] * len(prior)
    )
    extra = len(through) + len(needs)
    inputs = [x, *masks, *weights, *biases, *prior]
    outs = [kind((GROUPS, rows, n, seq), t) for n, t in dims]
    made, base = len(outs), len(inputs)

    def kernel(*refs):
        attend_kernel(
            head_dim, len(prior), count,
            *refs[:base], *refs[base + extra : base + extra + made],
            *refs[base + extra + made + len(through) :],
        )

    aliases = {here + i: i for i in range(len(prior))}
    aliases.update({base + i: made + i for i in range(len(through))})
    results = pl.pallas_call(
        kernel,
        grid=(count, rows),
        in_specs=in_specs + [ANY] * extra,
        out_specs=[pl.BlockSpec((1, 1, n, seq), at) for n, _ in dims] + [ANY] * len(through),
        out_shape=outs + [shape(a.shape, a.dtype) for a in through],
        scratch_shapes=[
            pltpu.VMEM((3 * narrow, narrow), BF16),
            pltpu.VMEM((3 * narrow, 8), F32),
        ],
        input_output_aliases=aliases,
        compiler_params=params(12),
        cost_estimate=cost(0.01),
        name="attend_fwd",
    )(*inputs, *through, *needs)
    return results[:made], results[made:]


def attend_back_kernel(head_dim, count, aliased, *refs):
    x_ref, qkv_ref, dout_ref, da_ref, lse_ref, delta_ref, km_ref, qm_ref = refs[:8]
    w_refs, refs = refs[8 : 8 + count], refs[8 + count + aliased :]
    gx_ref, dw_ref, acc_ref, dqkv_ref, w_ref = refs
    narrow, seq = x_ref.shape[-2:]
    place, row = pl.program_id(0), pl.program_id(1)
    for s in range(count):

        @pl.when((place == s) & (row == 0))
        def _(s=s):
            w_ref[...] = w_refs[s][0, :, : 3 * narrow]

    key_mask, query_mask = km_ref[0], qm_ref[0]
    scale = head_dim**-0.5
    heads = [head * head_dim for head in range(narrow // head_dim)]
    queries = [qkv_ref[0, 0, lo : lo + head_dim] for lo in heads]
    keys = [qkv_ref[0, 0, narrow + lo : narrow + lo + head_dim] for lo in heads]
    grads = [dout_ref[0, 0, lo : lo + head_dim] for lo in heads]
    scores = [
        dot(jnp.concatenate([k, key_mask], 0), jnp.concatenate([q, query_mask], 0), TN)
        for q, k in zip(queries, keys)
    ]
    grad_probs = [
        dot(qkv_ref[0, 0, 2 * narrow + lo : 2 * narrow + lo + head_dim], g, TN)
        for lo, g in zip(heads, grads)
    ]
    probs = [jnp.exp(some - lse_ref[0, 0, i : i + 1]) for i, some in enumerate(scores)]
    grad_scores = [
        (p * (g - delta_ref[0, 0, i : i + 1])).astype(BF16)
        for i, (p, g) in enumerate(zip(probs, grad_probs))
    ]
    for i, lo in enumerate(heads):
        dqkv_ref[lo : lo + head_dim] = (dot(keys[i], grad_scores[i], NN) * scale).astype(BF16)
        dqkv_ref[narrow + lo : narrow + lo + head_dim] = dot(queries[i], grad_scores[i], NT).astype(BF16)
        dqkv_ref[2 * narrow + lo : 2 * narrow + lo + head_dim] = dot(
            grads[i], probs[i].astype(BF16), NT
        ).astype(BF16)
    dqkv = dqkv_ref[...]
    gx_ref[0, 0] = (dot(w_ref[...], dqkv, NN) + da_ref[0, 0].astype(F32)).astype(gx_ref.dtype)
    ones = jnp.ones((16, seq), BF16)
    term = dot(jnp.concatenate([x_ref[0, 0], ones], 0), dqkv, NT)

    @pl.when(row == 0)
    def _():
        acc_ref[...] = term

    @pl.when(row > 0)
    def _():
        acc_ref[...] += term

    @pl.when(row == pl.num_programs(1) - 1)
    def _():
        pieces = dw_ref.shape[1]
        step = narrow // pieces
        sums = acc_ref[narrow : narrow + 1]
        extra = jnp.concatenate(
            [sums[:, :narrow], sums[:, 2 * narrow :], jnp.zeros((step - 2, narrow), F32)], 0
        ).astype(BF16)
        for piece in range(pieces):
            part = acc_ref[piece * step : (piece + 1) * step].astype(BF16)
            dw_ref[0, piece, :, : 3 * narrow] = part
            dw_ref[0, piece, :, 3 * narrow :] = extra


def attend_back(order, pieces, acts, weights, masks, head_dim, out_type, stack, earlier=(), through=(), needs=()):
    _, rows, narrow, seq = acts[0].shape
    count = len(order)
    slot = (lambda s: (2 * s + 1) % 5) if count == 4 else (lambda s: order[0] + (order[-1] - order[0]) * s)
    at = lambda s, r: (slot(s), r, 0, 0)
    block = lambda n, where: pl.BlockSpec((1, 1, n, seq), where)
    lanes = weights[0].shape[2]
    last = weights[0].shape[0] - 1
    dims = (1, pieces, narrow // pieces, lanes)
    gx_kind, gx_count = (hbm, GROUPS) if stack else (shape, count)
    outs = [gx_kind((gx_count, rows, narrow, seq), out_type), shape((count,) + dims[1:], BF16)]
    specs = [
        block(narrow, at if stack else (lambda s, r: (s, r, 0, 0))),
        pl.BlockSpec(dims, lambda s, r: (s, 0, 0, 0)),
    ]
    return launch(
        functools.partial(attend_back_kernel, head_dim, count, len(earlier)),
        [*acts, *masks, *[weights[k] for k in order], *earlier],
        [block(a.shape[2], at) for a in acts]
        + [pl.BlockSpec((1, 16, seq), lambda s, r: (r, 0, 0))] * 2
        + [pl.BlockSpec((1, narrow, lanes), lambda s, r: (last, 0, 0))] * count
        + [ANY] * len(earlier),
        outs,
        specs,
        through,
        needs,
        aliases={8 + count: 0} if earlier else {},
        grid=(count, rows),
        scratch_shapes=[
            pltpu.VMEM((narrow + 16, 3 * narrow), F32),
            pltpu.VMEM((3 * narrow, seq), BF16),
            pltpu.VMEM((narrow, 3 * narrow), BF16),
        ],
        compiler_params=params(16),
        cost_estimate=cost(3.5 * count * rows),
        name="attend_bwd",
    )


def norm(values):
    width = values.shape[0]
    center = jnp.sum(values, axis=0, keepdims=True) * (1.0 / width)
    spread = jnp.sum(values * values, axis=0, keepdims=True) * (1.0 / width) - center * center
    inverse = lax.rsqrt(spread + EPSILON)
    return (values - center) * inverse, inverse


def norm_back(weighted, scaled, inverse):
    width = weighted.shape[0]
    first = jnp.sum(weighted, axis=0, keepdims=True) * (1.0 / width)
    second = jnp.sum(weighted * scaled, axis=0, keepdims=True) * (1.0 / width)
    return inverse * (weighted - first - scaled * second)


def normal_cdf(values):
    return 0.5 + 0.5 * lax.erf(values * 0.7071067811865476)


def whole(ref, me):
    return jnp.concatenate([ref[me ^ j, 0] for j in range(GROUPS)], 0)


def columns(layer, narrow, me, vec_refs, small_refs, small_ref):
    for k in range(GROUPS):
        small_ref[me ^ k] = small_refs[k][layer]
    out_bias = jnp.concatenate([small_ref[j, 1:2, 3 * narrow :] for j in range(GROUPS)], 1)
    rows = [ref[layer : layer + 1] for ref in vec_refs] + [out_bias]
    rows += [small_ref[j, 0:1] for j in range(GROUPS)]
    rows.append(jnp.zeros((16 - len(rows), out_bias.shape[1]), F32))
    return jnp.concatenate(rows, 0).T


def first_step():
    return (pl.program_id(0) == 0) & (pl.program_id(1) == 0)


def mix_kernel(layer, split, *refs):
    me_ref, xs_ref, o_ref, wp_ref = refs[:4]
    vec_refs, small_refs, w_refs = refs[4:9], refs[9:13], refs[13:17]
    count = GROUPS if split else 1
    next_refs, refs = refs[17 : 17 + count], refs[17 + count :]
    y1_ref, xh1_ref, xh2_ref, inv_ref, wpt_ref, wit_ref, wo_ref, small_ref, state_ref = refs
    me = me_ref[0]
    narrow = xs_ref.shape[2]

    @pl.when(first_step())
    def _():
        wpt_ref[...] = wp_ref[0].T
        for k in range(GROUPS):
            wit_ref[me ^ k] = w_refs[k][0].T
            wo_ref[me ^ k] = w_refs[k][1]

    cols = columns(layer, narrow, me, vec_refs, small_refs, small_ref)
    a = dot(wpt_ref[...], whole(o_ref, me), NN) + whole(xs_ref, me).astype(F32) + cols[:, 0:1]
    scaled_one, inverse_one = norm(a)
    y1 = (scaled_one * cols[:, 1:2] + cols[:, 2:3]).astype(BF16)
    y1_ref[0] = y1
    xh1_ref[0] = scaled_one.astype(BF16)
    hs = [
        dot(wit_ref[j], y1[j * narrow : (j + 1) * narrow], NN) + cols[:, 6 + j : 7 + j]
        for j in range(GROUPS)
    ]
    us = [(h * normal_cdf(h)).astype(BF16) for h in hs]
    z = jnp.concatenate([dot(wo_ref[j], us[j], NN) for j in range(GROUPS)], 0)
    scaled_two, inverse_two = norm(z + y1.astype(F32) + cols[:, 5:6])
    xh2_ref[0] = scaled_two.astype(BF16)
    state = (scaled_two * cols[:, 3:4] + cols[:, 4:5]).astype(BF16)
    for j in range(GROUPS):
        piece = state[j * narrow : (j + 1) * narrow]
        if split:
            state_ref[j] = piece
        else:
            next_refs[0][me ^ j, 0] = piece
    if split:
        for k in range(GROUPS):
            next_refs[k][0] = state_ref[me ^ k]
    inv_ref[0] = jnp.concatenate(
        [inverse_one, inverse_two, jnp.zeros((6, inverse_one.shape[1]), F32)], 0
    )


def mix(me, layer, split, xs, o, w_post, vectors, smalls, weights, tile, through=(), needs=(), kind=shape):
    _, rows, narrow, seq = xs.shape
    width = narrow * GROUPS
    ff = weights[0].shape[2]
    stacked = pl.BlockSpec((GROUPS, 1, narrow, tile), lambda r, t: (0, r, 0, t))
    plain = lambda n: pl.BlockSpec((1, n, tile), lambda r, t: (r, 0, t))
    const = lambda a: pl.BlockSpec(a.shape, lambda r, t: (0,) * a.ndim)
    outs = [shape((rows, narrow, seq), BF16)] * GROUPS if split else [vmem(xs.shape, BF16)]
    return launch(
        functools.partial(mix_kernel, layer, split),
        [me, xs, o, w_post, *vectors, *smalls, *weights],
        [SMEM, stacked, stacked, pl.BlockSpec((1, width, width), lambda r, t: (layer, 0, 0))]
        + [const(a) for a in (*vectors, *smalls)]
        + [pl.BlockSpec((2, narrow, ff), lambda r, t: (0, 0, 0))] * GROUPS,
        outs + [kind((rows, width, seq), BF16)] * 3 + [kind((rows, 8, seq), F32)],
        ([plain(narrow)] * GROUPS if split else [stacked]) + [plain(width)] * 3 + [plain(8)],
        through,
        needs,
        grid=(rows, seq // tile),
        scratch_shapes=[
            pltpu.VMEM((width, width), BF16),
            pltpu.VMEM((GROUPS, ff, narrow), BF16),
            pltpu.VMEM((GROUPS, narrow, ff), BF16),
            pltpu.VMEM((GROUPS, 8, ff), F32),
            pltpu.VMEM((GROUPS, narrow, tile), BF16),
        ],
        compiler_params=params(16),
        cost_estimate=cost(0.01),
        name="mix_fwd",
    )


def lane_sum(values):
    total = values[:, :128]
    for lo in range(128, values.shape[1], 128):
        total = total + values[:, lo : lo + 128]
    return total


def mix_back_kernel(layer, head_dim, *refs):
    me_ref, y1_ref, xh1_ref, xh2_ref, inv_ref, o_ref = refs[:6]
    gz_refs, wp_ref, vec_refs, small_refs, w_refs = refs[6:10], refs[10], refs[11:16], refs[16:20], refs[20:24]
    da_ref, dout_ref, delta_ref, f_odd_ref, f_even_ref, p_odd_ref, p_even_ref = refs[24:31]
    accf_ref, accp_ref, accv_ref, wit_ref, wot_ref, wi_ref, small_ref, gz_ref, tail_ref = refs[31:]
    me = me_ref[0]
    narrow, tile = o_ref.shape[2:]
    width = narrow * GROUPS
    step = pl.program_id(0) * pl.num_programs(1) + pl.program_id(1)
    steps = pl.num_programs(0) * pl.num_programs(1)

    @pl.when(first_step())
    def _():
        for k in range(GROUPS):
            wit_ref[me ^ k] = w_refs[k][0].T
            wi_ref[me ^ k] = w_refs[k][0]
            wot_ref[me ^ k] = w_refs[k][1].T
        accv_ref[...] = jnp.zeros_like(accv_ref)

    cols = columns(layer, narrow, me, vec_refs, small_refs, small_ref)
    for k in range(GROUPS):
        gz_ref[me ^ k] = gz_refs[k][0, 0].astype(F32)
    gz = jnp.concatenate([gz_ref[j] for j in range(GROUPS)], 0)
    y1 = y1_ref[0]
    scaled_one = xh1_ref[0].astype(F32)
    scaled_two = xh2_ref[0].astype(F32)
    inverse_one, inverse_two = inv_ref[0, 0:1], inv_ref[0, 1:2]
    accv_ref[0] += lane_sum(gz * scaled_two)
    accv_ref[1] += lane_sum(gz)
    dz = norm_back(gz * cols[:, 3:4], scaled_two, inverse_two)
    df = dz.astype(BF16)
    accv_ref[2] += lane_sum(df.astype(F32))
    ones = jnp.ones((16, tile), BF16)
    at = [slice(j * narrow, (j + 1) * narrow) for j in range(GROUPS)]
    hs = [dot(wit_ref[j], y1[at[j]], NN) + cols[:, 6 + j : 7 + j] for j in range(GROUPS)]
    back = [dot(wot_ref[j], df[at[j]], NN) for j in range(GROUPS)]
    us, dhs = [], []
    for h, some in zip(hs, back):
        cdf = normal_cdf(h)
        us.append((h * cdf).astype(BF16))
        dhs.append((some * (cdf + h * jnp.exp(-0.5 * h * h) * 0.3989422804014327)).astype(BF16))
    parts = [dz[at[j]] + dot(wi_ref[j], dhs[j], NN) for j in range(GROUPS)]
    so_far = lambda array: jnp.where(step == 0, 0.0, array)
    for j in range(GROUPS):
        out_term = dot(df[at[j]], us[j], NT)
        accf_ref[j, narrow + 16 :] = so_far(accf_ref[j, narrow + 16 :]) + out_term
        in_term = dot(jnp.concatenate([y1[at[j]], ones], 0), dhs[j], NT)
        accf_ref[j, : narrow + 16] = so_far(accf_ref[j, : narrow + 16]) + in_term
    dy1 = jnp.concatenate(parts, 0).astype(BF16).astype(F32)
    accv_ref[3] += lane_sum(dy1 * scaled_one)
    accv_ref[4] += lane_sum(dy1)
    da = norm_back(dy1 * cols[:, 1:2], scaled_one, inverse_one).astype(BF16)
    o = whole(o_ref, me)
    accp_ref[...] = so_far(accp_ref[...]) + dot(jnp.concatenate([o, ones], 0), da, NT)
    dout = dot(wp_ref[0], da, NN).astype(BF16)
    product = (o.astype(F32) * dout.astype(F32)).reshape(width // head_dim, head_dim, tile)
    delta = jnp.sum(product, axis=1)
    per_group = narrow // head_dim
    pad = jnp.zeros((8 - per_group, tile), F32)
    for j in range(GROUPS):
        lo = j * narrow
        da_ref[me ^ j, 0] = da[lo : lo + narrow]
        dout_ref[me ^ j, 0] = dout[lo : lo + narrow]
        delta_ref[me ^ j, 0] = jnp.concatenate(
            [delta[j * per_group : (j + 1) * per_group], pad], 0
        )

    @pl.when(step == steps - 1)
    def _():
        pieces = f_odd_ref.shape[1]
        vec = [jnp.sum(accv_ref[i].T, axis=0, keepdims=True) for i in range(5)]
        vec.append(accp_ref[width : width + 1])
        half = pieces // 2
        size, post = narrow // half, narrow // pieces
        for j in range(GROUPS):
            lo = j * narrow
            own = [v[:, lo : lo + narrow] for v in vec]
            tail_ref[j] = jnp.concatenate(
                [
                    accf_ref[j, narrow : narrow + 1],
                    jnp.concatenate(own[:4], 1),
                    jnp.concatenate(own[4:] + own[4:], 1),
                    jnp.zeros((5, width), F32),
                ],
                0,
            ).astype(BF16)
        for k in range(GROUPS):
            f_ref, p_ref = (f_odd_ref, p_odd_ref) if k % 2 else (f_even_ref, p_even_ref)
            j = me ^ k
            for piece in range(pieces):
                at = (piece % half) * size + (0 if piece < half else narrow + 16)
                f_ref[k // 2, piece] = accf_ref[j, at : at + size].astype(BF16)
                at = pl.multiple_of(j * narrow + piece * post, 8)
                p_ref[k // 2, piece, :post] = accp_ref[pl.ds(at, post)].astype(BF16)
                p_ref[k // 2, piece, post:] = tail_ref[j]


def mix_back(me, layer, pieces, kept, o, gz, w_post, vectors, smalls, weights, head_dim, tile, through=(), needs=(), kind=shape):
    _, rows, narrow, seq = o.shape
    width = narrow * GROUPS
    ff = weights[0].shape[2]
    stacked = pl.BlockSpec((GROUPS, 1, narrow, tile), lambda r, t: (0, r, 0, t))
    plain = lambda n: pl.BlockSpec((1, n, tile), lambda r, t: (r, 0, t))
    const = lambda dims: pl.BlockSpec(dims, lambda r, t: (0,) * len(dims))
    if isinstance(gz, list):
        gz_specs = [pl.BlockSpec((1, 1, narrow, tile), lambda r, t: (0, r, 0, t))] * GROUPS
    else:
        gz_specs = [
            pl.BlockSpec((1, 1, narrow, tile), lambda r, t, k=k: (k, r, 0, t))
            for k in range(GROUPS)
        ]
        gz = [gz] * GROUPS
    grads_f = (2, pieces, 2 * narrow // pieces, ff)
    grads_p = (2, pieces, narrow // pieces + 8, width)
    grads = [grads_f, grads_f, grads_p, grads_p]
    return launch(
        functools.partial(mix_back_kernel, layer, head_dim),
        [me, *kept, o, *gz, w_post, *vectors, *smalls, *weights],
        [SMEM] + [plain(width)] * 3 + [plain(8), stacked] + gz_specs
        + [pl.BlockSpec((1, width, width), lambda r, t: (layer, 0, 0))]
        + [const(a.shape) for a in (*vectors, *smalls)]
        + [const((2, narrow, ff))] * GROUPS,
        [kind(o.shape, BF16)] * 2 + [kind((GROUPS, rows, 8, seq), F32)]
        + [shape(g, BF16) for g in grads],
        [stacked, stacked, pl.BlockSpec((GROUPS, 1, 8, tile), lambda r, t: (0, r, 0, t))]
        + [const(g) for g in grads],
        through,
        needs,
        grid=(rows, seq // tile),
        scratch_shapes=[
            pltpu.VMEM((GROUPS, 2 * narrow + 16, ff), F32),
            pltpu.VMEM((width + 16, width), F32),
            pltpu.VMEM((5, width, 128), F32),
            pltpu.VMEM((GROUPS, ff, narrow), BF16),
            pltpu.VMEM((GROUPS, ff, narrow), BF16),
            pltpu.VMEM((GROUPS, narrow, ff), BF16),
            pltpu.VMEM((GROUPS, 8, ff), F32),
            pltpu.VMEM((GROUPS, narrow, tile), F32),
            pltpu.VMEM((GROUPS, 8, width), BF16),
        ],
        compiler_params=params(30),
        cost_estimate=cost(24.0),
        name="mix_bwd",
    )


def swap(array, axis, distance):
    size = lax.axis_size(axis)
    return lax.ppermute(array, axis, [(i, i ^ distance) for i in range(size)])


def collect_kernel(me_ref, *refs):
    out = refs[-1]
    for k, ref in enumerate(refs[:-1]):
        out[me_ref[0] ^ k, 0] = ref[0].astype(out.dtype)


def collect(me, arrays, needs=(), dtype=F32, through=None):
    rows, rest = arrays[0].shape[0], arrays[0].shape[1:]
    zeros = (0,) * len(rest)
    (out,), passed = launch(
        collect_kernel,
        [me, *arrays],
        [SMEM] + [pl.BlockSpec((1,) + rest, lambda r: (r,) + zeros)] * GROUPS,
        [(hbm if dtype == F32 else shape)((GROUPS, rows) + rest, dtype)],
        [pl.BlockSpec((GROUPS, 1) + rest, lambda r: (0, r) + zeros)],
        through or (),
        needs,
        grid=(rows,),
        compiler_params=params(12),
        cost_estimate=cost(0.1),
        name="collect",
    )
    return out if through is None else (out, passed)


def total(*arrays):
    return functools.reduce(lambda a, b: a + b, [a.astype(F32) for a in arrays])


def combine_kernel(sizes, spread, me_ref, *refs):
    count = sum(sizes)
    ins, outs = refs[:count], refs[count:]
    for d, out in enumerate(outs):
        start, row = 0, 0
        for size in sizes:
            terms = ins[start : start + size]
            rows = terms[0].shape[2]
            if spread:
                per = terms[0].shape[1] // len(outs)
                at = (me_ref[0] ^ d) * per
                part = total(*[ref[0, pl.ds(at, per)] for ref in terms])
            else:
                part = total(*[ref[0] for ref in terms])
            out[:, row : row + rows] = part.astype(BF16)
            start, row = start + size, row + rows


def combine(parts, me, spread=0, needs=()):
    flat = [a if isinstance(a, tuple) else (a[None], 0) for part in parts for a in part]
    pieces, _, lanes = flat[0][0].shape[1:]
    rows = sum((p[0][0].shape[2] if isinstance(p[0], tuple) else p[0].shape[1]) for p in parts)
    count = max(1, spread)
    outs, _ = launch(
        functools.partial(combine_kernel, [len(p) for p in parts], spread),
        [me] + [a for a, _ in flat],
        [SMEM]
        + [pl.BlockSpec((1, pieces, a.shape[2], lanes), lambda i, k=k: (k, 0, 0, 0)) for a, k in flat],
        [shape((pieces // count, rows, lanes), BF16)] * count,
        [pl.BlockSpec((pieces // count, rows, lanes), lambda i: (0, 0, 0))] * count,
        (),
        needs,
        grid=(1,),
        compiler_params=params(12),
        cost_estimate=cost(0.1),
        name="combine",
    )
    return outs if spread else outs[0]


def finish_post_kernel(post, layers, me_ref, *refs):
    ins, refs = refs[:GROUPS], refs[GROUPS + 1 :]
    small, refs = refs[: layers * GROUPS], refs[layers * GROUPS :]
    dpost_ref, vec_refs = refs[0], refs[1:]
    me = me_ref[0]
    for k, ref in enumerate(ins):
        dpost_ref[0, me ^ k] = ref[:, :post].astype(F32)

    if layers:
        width = vec_refs[0].shape[1]
        narrow = width // GROUPS

        @pl.when(pl.program_id(0) == pl.num_programs(0) - 1)
        def _():
            for layer in range(layers):
                for k in range(GROUPS):
                    both = small[layer * GROUPS + k][0].astype(F32)
                    rows = [
                        both[1 + i // 4 : 2 + i // 4, i % 4 * narrow : (i % 4 + 1) * narrow]
                        for i in range(6)
                    ]
                    if k == 0:
                        vec_refs[6][layer] = both[0:1]
                        vec_refs[7][layer] = rows[2]
                    for j in range(GROUPS):

                        @pl.when((me ^ k) == j)
                        def _(j=j, rows=rows, layer=layer):
                            for i in range(6):
                                vec_refs[i][layer : layer + 1, j * narrow : (j + 1) * narrow] = rows[i]


def finish_post(me, layer, slots, prior, all_slots, post, needs=()):
    pieces, rows, width = slots[0].shape
    narrow = width // GROUPS
    small = [a for some in all_slots for a in some]
    outs = [hbm((LAYERS, GROUPS, pieces, post, width), F32)]
    specs = [pl.BlockSpec((1, GROUPS, pieces // 2, post, width), lambda i: (layer, 0, i, 0, 0))]
    if small:
        outs += [shape((LAYERS, width), F32)] * 6
        outs += [shape((LAYERS, 1, width), F32), shape((LAYERS, 1, narrow), F32)]
        specs += [pl.BlockSpec(o.shape, lambda i, n=len(o.shape): (0,) * n) for o in outs[1:]]
    if prior is None:
        prior, aliases = me, {}
    else:
        aliases = {1 + GROUPS: 0}
    return launch(
        functools.partial(finish_post_kernel, post, len(all_slots)),
        [me, *slots, prior, *small],
        [SMEM]
        + [pl.BlockSpec((pieces // 2, rows, width), lambda i: (i, 0, 0))] * GROUPS
        + [ANY if aliases else SMEM]
        + [pl.BlockSpec((1, 8, width), lambda i: (0, post // 8, 0))] * len(small),
        outs,
        specs,
        (),
        needs,
        aliases=aliases,
        grid=(2,),
        compiler_params=params(12),
        cost_estimate=cost(0.1),
        name="finish_post",
    )[0]


def finish_ffn_kernel(size, me_ref, *refs):
    parts, last_ref = refs[:4], refs[4]
    wi_ref, wo_ref = refs[5:]
    layer = pl.program_id(0)

    def put(shard, part):
        @pl.when(shard < 2)
        def _():
            wi_ref[0, shard] = part.astype(F32)

        @pl.when(shard >= 2)
        def _():
            wo_ref[0, shard - 2] = part.astype(F32)

    @pl.when(layer == 0)
    def _():
        for d, ref in enumerate(parts):
            put(me_ref[0] ^ d, ref[:, :size])

    @pl.when(layer > 0)
    def _():
        for d in range(4):
            put(d, last_ref[2 * d : 2 * d + 2, :size])


def finish_ffn(me, parts, last, size, needs=()):
    half, _, lanes = parts[0].shape
    out = hbm((LAYERS, 2, half, size, lanes), F32)
    return launch(
        functools.partial(finish_ffn_kernel, size),
        [me, *parts, last],
        [SMEM] + [pl.BlockSpec(a.shape, lambda l: (0, 0, 0)) for a in (*parts, last)],
        [out] * 2,
        [pl.BlockSpec((1, 2, half, size, lanes), lambda l: (l, 0, 0, 0, 0))] * 2,
        (),
        needs,
        grid=(LAYERS,),
        compiler_params=params(12),
        cost_estimate=cost(0.1),
        name="finish_ffn",
    )[0]


def finish_qkv_kernel(lo, post, me_ref, *refs):
    sets, outs = (refs[:4], refs[4:8]), refs[8:]
    narrow = outs[0].shape[-1]
    for layer, parts in enumerate(sets):
        start = lo if layer else 0
        for d, ref in enumerate(parts):
            part = ref[:, start : start + post].astype(F32)
            for i in range(3):
                outs[i][layer, me_ref[0] ^ d] = part[:, :, i * narrow : (i + 1) * narrow]
            if d == 0:
                outs[3][layer] = part[0, 0:1, 3 * narrow :]
                outs[4][layer] = part[0, 1:2, 3 * narrow :]


def finish_qkv(me, first, second, lo, narrow, needs=()):
    half, post, lanes = first[0].shape
    big = shape((LAYERS, 4, half, post, narrow), F32)
    vec = shape((LAYERS, 1, narrow), F32)
    full = pl.BlockSpec(memory_space=pltpu.VMEM)
    return launch(
        functools.partial(finish_qkv_kernel, lo, post),
        [me, *first, *second],
        [SMEM] + [full] * 8,
        [big] * 3 + [vec] * 2,
        [full] * 5,
        (),
        needs,
        compiler_params=params(12),
        cost_estimate=cost(0.1),
        name="finish_qkv",
    )[0]


def fold_kernel(in_ref, out_ref):
    part = total(*[in_ref[i] for i in range(in_ref.shape[0])]).astype(BF16)
    for i in range(out_ref.shape[0]):
        out_ref[i] = part


def fold(array, through=(), needs=()):
    pieces, rows, lanes = array.shape
    block = pl.BlockSpec((pieces, rows, lanes), lambda i: (0, 0, 0))
    (out,), passed = launch(
        fold_kernel,
        [array],
        [block],
        [shape(array.shape, BF16)],
        [block],
        through,
        needs,
        grid=(1,),
        compiler_params=params(12),
        cost_estimate=cost(0.1),
        name="fold",
    )
    return (out, *passed)


def dp_groups(pieces):
    return [list(range(i, i + pieces)) for i in range(0, lax.axis_size("dp"), pieces)]


def trade(array):
    return lax.all_to_all(
        array, "dp", split_axis=0, concat_axis=0, tiled=True,
        axis_index_groups=dp_groups(array.shape[0]),
    )


def beyond(copies):
    distance = copies.shape[0]
    while distance < lax.axis_size("dp"):
        copies = total(copies, swap(copies, "dp", distance)).astype(BF16)
        distance *= 2
    return copies


def near_dp(parts):
    return [parts[0]] + [swap(part, "dp", d) for d, part in enumerate(parts) if d]


def across_dp(sums, needs=(), block=4):
    distance = block
    while distance < lax.axis_size("dp"):
        sums = add([[mine, swap(mine, "dp", distance)] for mine in sums], (), needs)
        distance *= 2
    return sums


def add_kernel(sizes, *refs):
    ins, outs = refs[: sum(sizes)], refs[sum(sizes) :]
    start = 0
    for size, out in zip(sizes, outs):
        out[...] = total(*[ref[...] for ref in ins[start : start + size]]).astype(BF16)
        start += size


def add(lists, through=(), needs=(), micros=0.1):
    flat = [a for arrays in lists for a in arrays]
    spec = lambda a: pl.BlockSpec(a.shape, lambda i: (0, 0, 0))
    outs, passed = launch(
        functools.partial(add_kernel, [len(arrays) for arrays in lists]),
        flat,
        [spec(a) for a in flat],
        [shape(arrays[0].shape, BF16) for arrays in lists],
        [spec(arrays[0]) for arrays in lists],
        through,
        needs,
        grid=(1,),
        compiler_params=params(16),
        cost_estimate=cost(micros),
        name="add",
    )
    return (*outs, *passed)


def pick(array, index):
    return lax.dynamic_index_in_dim(array, index, 0, keepdims=False)


def shards(
    hidden_in,
    segment_ids,
    w_query,
    b_query,
    w_key,
    w_value,
    b_value,
    w_post,
    b_post,
    ln1_gain,
    ln1_bias,
    w_inter,
    b_inter,
    w_output,
    b_output,
    ln2_gain,
    ln2_bias,
    cotangent,
):
    row_count, narrow, seq = hidden_in.shape
    rows = row_count // GROUPS
    width = narrow * GROUPS
    ff = w_inter.shape[-1]
    head_dim = width // HEADS
    me = lax.axis_index("grp")
    me_ref = me.reshape(1).astype(jnp.int32)
    pieces = 8
    tile = 256

    by_owner = hidden_in.reshape(GROUPS, rows, narrow, seq)
    cot_owner = cotangent.reshape(GROUPS, rows, narrow, seq)
    no_bias = jnp.zeros_like(b_query)
    small = jnp.concatenate([b_query, no_bias, b_value, b_output], 2)
    small = jnp.pad(jnp.concatenate([b_inter, small], 1), ((0, 0), (0, 6), (0, 0)))
    pad = jnp.zeros((LAYERS, 1, narrow, ff - 3 * narrow), BF16)
    w_qkv = jnp.concatenate([w_query, w_key, w_value, pad], 3)
    ffn_own = jnp.concatenate([w_inter[0], w_output[0]], 0)
    both_own = jnp.concatenate([w_inter[1], w_output[1], w_qkv[1]], 0)

    segments = lax.dynamic_slice_in_dim(segment_ids, me * rows, rows, 0)
    hot = segments[:, None, :] == jnp.arange(16, dtype=segments.dtype)[None, :, None]
    masks = (hot.astype(BF16), jnp.where(hot, 0.0, MASKED).astype(BF16))

    small_far, qkv_far = swap(small, "grp", 2), swap(w_qkv[0], "grp", 2)
    smalls = [small, swap(small, "grp", 1), small_far, swap(small_far, "grp", 1)]
    qkv0 = [w_qkv[0], swap(w_qkv[0], "grp", 1), qkv_far, swap(qkv_far, "grp", 1)]
    x_slots = [pick(by_owner, me)] + [swap(pick(by_owner, me ^ k), "grp", k) for k in (1, 2, 3)]

    acts0, _ = attend(
        x_slots[0][None], 0, None, qkv0[:1], smalls[:1], masks, 0, head_dim, kind=hbm
    )
    acts0, _ = attend(
        x_slots[1][None], 1, acts0, qkv0[1:2], smalls[1:2], masks, 0, head_dim, kind=hbm
    )
    acts0, (ffn_own,) = attend(
        x_slots[2][None], 2, acts0, qkv0[2:3], smalls[2:3], masks, 0, head_dim, [ffn_own],
        kind=hbm,
    )
    ffn_far = swap(ffn_own, "grp", 2)
    ffn0 = [ffn_own, swap(ffn_own, "grp", 1), ffn_far, swap(ffn_far, "grp", 1)]
    acts0, (both_own,) = attend(
        x_slots[3][None], 3, acts0, qkv0[3:4], smalls[3:4], masks, 0, head_dim, [both_own],
        kind=hbm,
    )
    both_far = swap(both_own, "grp", 2)
    both_near = swap(both_own, "grp", 1)
    o0, qkvs0, lse0, xs0 = [held(a, pltpu.HBM) for a in acts0]
    vectors = (b_post, ln1_gain, ln1_bias, ln2_gain, ln2_bias)
    (state, *kept0), cot_send = mix(
        me_ref, 0, False, xs0, o0, w_post, vectors, smalls, ffn0, tile,
        [pick(cot_owner, me ^ k) for k in (1, 2, 3)],
        kind=hbm,
    )
    kept0 = [held(a, pltpu.HBM) for a in kept0]
    state = held(state)
    cot_slots = [pick(cot_owner, me)[None]] + [
        swap(cot_send[k - 1], "grp", k)[None] for k in (1, 2, 3)
    ]
    acts1, (both_far,) = attend(
        state, 0, None, [both_own, both_near], smalls[:2], masks, 1, head_dim, [both_far]
    )
    both1 = [both_own, both_near, both_far, swap(both_far, "grp", 1)]
    acts1, _ = attend(state, 2, acts1, both1[2:], smalls[2:], masks, 1, head_dim)
    o1, qkvs1, lse1, xs1 = acts1
    results, _ = mix(me_ref, 1, True, xs1, o1, w_post, vectors, smalls, both1, tile)
    state_slots, kept1 = results[:GROUPS], results[GROUPS:]
    state_slots = [state_slots[0]] + [swap(state_slots[k], "grp", k) for k in (1, 2, 3)]

    me_four = (lax.axis_index("dp") % 4).reshape(1).astype(jnp.int32)
    (da1, dout1, delta1, f_odd, f_even, p_odd, p_even), _ = mix_back(
        me_ref, 1, pieces, kept1, o1, cot_slots, w_post, vectors, smalls, both1, head_dim, tile
    )
    hidden_out, passed = collect(
        me_ref, state_slots, through=(da1, dout1, delta1, f_odd, f_even, p_odd, p_even)
    )
    da1, dout1, delta1, f_odd, f_even, p_odd, p_even = passed
    f_near, p_near = swap(f_odd, "grp", 1), swap(p_odd, "grp", 1)
    send = combine([[(f_even, 1), (f_near, 1)], [(p_even, 1), (p_near, 1)]], me_ref)
    far = swap(send, "grp", 2)
    acts = (xs1, qkvs1, dout1, da1, lse1, delta1)
    (gz, dw_odd1), _ = attend_back(
        [1, 3], pieces, acts, both1, masks, head_dim, F32, True, (), (), (send,)
    )
    near_q1 = swap(dw_odd1, "grp", 1)
    own_f = combine([[(f_even, 0), (f_near, 0)], [(p_even, 0), (p_near, 0)]], me_ref, 0, (dw_odd1,))
    (gz, dw_even1), _ = attend_back(
        [0, 2], pieces, acts, both1, masks, head_dim, F32, True, (gz,), (), (own_f,)
    )
    gz = held(gz, pltpu.HBM)
    (own1,) = add([[own_f, far]], (), (dw_even1,))
    moved1 = trade(own1)
    send_q1 = combine([[(dw_even1, 1), (near_q1, 1)]], me_ref, 0, (own1,))
    far_q1 = swap(send_q1, "grp", 2)
    (da0, dout0, delta0, f_odd, f_even, p_odd, p_even), _ = mix_back(
        me_ref, 0, pieces, kept0, o0, gz, w_post, vectors, smalls, ffn0, head_dim, tile,
        (), (send_q1,), hbm,
    )
    p_near, f_near = swap(p_odd, "grp", 1), swap(f_odd, "grp", 1)
    send_p = combine([[(p_even, 1), (p_near, 1)]], me_ref)
    far_p = swap(send_p, "grp", 2)
    send_f = combine([[(f_even, 1), (f_near, 1)]], me_ref, 0, (send_p,))
    far_f = swap(send_f, "grp", 2)
    dout0, da0, delta0 = [held(a, pltpu.HBM) for a in (dout0, da0, delta0)]
    acts = (xs0, qkvs0, dout0, da0, lse0, delta0)
    qkv0 = [held(w, pltpu.HBM) for w in qkv0]
    (mine1,) = fold(moved1, (), (send_f,))
    all1 = trade(beyond(mine1))
    back = lambda order, *rest: attend_back(
        order, pieces, acts, qkv0, masks, head_dim, BF16, False, (), *rest
    )
    (gx32, dw32), _ = back([3, 2], (), (mine1, far_q1))
    near_w3 = swap(dw32[:1], "grp", 1)
    own_p = combine([[(p_even, 0), (p_near, 0), far_p]], me_four, 4, (dw32,))
    parts_p = near_dp(own_p)
    send_w = combine([[(dw32, 1), (near_w3, 0)]], me_ref, 0, (own_p[0],))
    far_w = swap(send_w, "grp", 2)
    own_f = combine(
        [[(f_even, 0), (f_near, 0), far_f], [(dw_even1, 0), (near_q1, 0), far_q1]], me_four, 4,
        (send_w, all1),
    )
    parts_f = near_dp(own_f)
    size, post = 2 * narrow // pieces, narrow // pieces
    last_p = all1[:, size:]
    last_far = swap(last_p, "grp", 2)
    (mine_p,) = add([parts_p], (), (own_f[0],))
    across_p = swap(mine_p, "dp", 4)
    (gx10, dw10), _ = back([1, 0], (), (mine_p,))
    gx2, gx3 = swap(gx32[1], "grp", 2), swap(gx32[0], "grp", 3)
    mine_p, mine_f, gx10, dw10 = add(
        [[mine_p, across_p], parts_f], (gx10, dw10), (gx2, gx3, last_far, far_w)
    )
    near_w1 = swap(dw10[:1], "grp", 1)
    gx_slots = [gx10[1], swap(gx10[0], "grp", 1), gx2, gx3]
    own_q = combine([[(dw10, 1), (near_w1, 0), far_w]], me_four, 4, (mine_p,))
    parts_q = near_dp(own_q)
    (mine_p,) = across_dp([mine_p], (), 8)
    parts_p = near_dp([mine_p] * 4)
    across_f = swap(mine_f, "dp", 4)
    (mine_q,) = add([parts_q])
    across_q = swap(mine_q, "dp", 4)
    (mine_f,) = add([[mine_f, across_f]], (), (mine_q,))
    (mine_f,) = across_dp([mine_f], (), 8)
    parts_f = near_dp([mine_f] * 4)
    all_p = collect(me_four, parts_p, (mine_f,), BF16).reshape(pieces, -1, width)
    far_shared = swap(all_p, "grp", 2)
    near_shared = swap(all_p, "grp", 1)
    shared1 = [last_p, swap(last_p, "grp", 1), last_far, swap(last_far, "grp", 1)]
    (prior,) = finish_post(me_ref, 1, shared1, None, [], post, (all_p,))
    grad_input = collect(me_ref, gx_slots, (held(prior, pltpu.HBM),))
    mine_q, far_shared = add(
        [[mine_q, across_q]], (far_shared,), (held(grad_input, pltpu.HBM), *parts_f[1:]), 10.0
    )
    (mine_q,) = across_dp([mine_q], (), 8)
    parts_q = near_dp([mine_q] * 4)
    shared0 = [all_p, near_shared, far_shared, swap(far_shared, "grp", 1)]

    dpost, *vec = finish_post(me_ref, 0, shared0, prior, [shared0, shared1], post, (mine_q,))
    d_inter, d_output = finish_ffn(me_four, parts_f, all1, size, (mine_q,))
    dq, dk, dv, dbq, dbv = finish_qkv(
        me_four, parts_q, parts_f, size, narrow,
        (held(d_inter, pltpu.HBM), held(dpost, pltpu.HBM)),
    )
    ffn_shape, qkv_shape = (LAYERS, 1, narrow, ff), (LAYERS, 1, narrow, narrow)
    return (
        hidden_out.reshape(row_count, narrow, seq),
        grad_input.reshape(row_count, narrow, seq),
        dq.reshape(qkv_shape),
        dbq,
        dk.reshape(qkv_shape),
        dv.reshape(qkv_shape),
        dbv,
        dpost.reshape(LAYERS, width, width),
        vec[5],
        vec[3],
        vec[4],
        d_inter.reshape(ffn_shape),
        vec[6],
        d_output.reshape(ffn_shape),
        vec[7],
        vec[0],
        vec[1],
    )


def solution(mesh):
    placed = (
        P("dp", "grp", None),
        P("dp", None),
        P(None, "grp", None, None),
        P(None, "grp", None),
        P(None, "grp", None, None),
        P(None, "grp", None, None),
        P(None, "grp", None),
        P(),
        P(),
        P(),
        P(),
        P(None, "grp", None, None),
        P(None, "grp", None),
        P(None, "grp", None, None),
        P(None, "grp", None),
        P(),
        P(),
        P("dp", "grp", None),
    )
    return jax.shard_map(
        shards,
        mesh=mesh,
        in_specs=placed,
        out_specs=(
            P("dp", "grp", None),
            P("dp", "grp", None),
            P(None, "grp", None, None),
            P(None, "grp", None),
            P(None, "grp", None, None),
            P(None, "grp", None, None),
            P(None, "grp", None),
            P(),
            P(),
            P(),
            P(),
            P(None, "grp", None, None),
            P(None, "grp", None),
            P(None, "grp", None, None),
            P(None, "grp", None),
            P(),
            P(),
        ),
        check_vma=False,
    )
```

```python
import functools

import jax
import jax.numpy as jnp
from jax import lax
from jax.experimental import pallas as pl
from jax.experimental.pallas import tpu as pltpu
from jax.sharding import PartitionSpec as P


HEADS = 12
LAYERS = 2
GROUPS = 4
EPSILON = 1e-05
MASKED = -1e30

F32 = jnp.float32
BF16 = jnp.bfloat16
NN = (((1,), (0,)), ((), ()))
NT = (((1,), (1,)), ((), ()))
TN = (((0,), (0,)), ((), ()))
MIB = 1 << 20


def dot(left, right, dims):
    return lax.dot_general(left, right, dims, preferred_element_type=F32)


def params(limit=60):
    return pltpu.CompilerParams(vmem_limit_bytes=limit * MIB)


def cost(micros):
    return pl.CostEstimate(flops=int(micros * 1e9), bytes_accessed=1 << 10, transcendentals=0)


def shape(dims, dtype):
    return jax.ShapeDtypeStruct(dims, dtype)


def hbm(dims, dtype):
    return pltpu.HBM(dims, dtype)


def vmem(dims, dtype):
    return pltpu.VMEM(dims, dtype)


def held(array, space=pltpu.VMEM):
    return pltpu.with_memory_space_constraint(array, space)


SMEM = pl.BlockSpec(memory_space=pltpu.SMEM)
ANY = pl.BlockSpec(memory_space=pl.ANY)


def launch(body, arrays, in_specs, outs, out_specs, through=(), needs=(), aliases=None, **kwargs):
    count, made = len(arrays), len(outs)
    extra = len(through) + len(needs)

    def kernel(*refs):
        body(*refs[:count], *refs[count + extra : count + extra + made], *refs[count + extra + made + len(through) :])

    results = pl.pallas_call(
        kernel,
        in_specs=list(in_specs) + [ANY] * extra,
        out_specs=list(out_specs) + [ANY] * len(through),
        out_shape=list(outs) + [shape(a.shape, a.dtype) for a in through],
        input_output_aliases={
            **(aliases or {}),
            **{count + i: made + i for i in range(len(through))},
        },
        **kwargs,
    )(*arrays, *through, *needs)
    return results[:made], results[made:]


def attend_kernel(head_dim, aliased, count, *refs):
    x_ref, km_ref, qm_ref = refs[:3]
    w_refs, b_refs = refs[3 : 3 + count], refs[3 + count : 3 + 2 * count]
    o_ref, qkv_ref, lse_ref, xs_ref, wt_ref, bias_ref = refs[3 + 2 * count + aliased :]
    narrow = x_ref.shape[-2]
    for k in range(count):

        @pl.when((pl.program_id(1) == 0) & (pl.program_id(0) == k))
        def _(k=k):
            wt_ref[...] = w_refs[k][0].T[: 3 * narrow]
            bias_ref[...] = b_refs[k][0].T[: 3 * narrow]

    x = x_ref[0, 0]
    xs_ref[0, 0] = x
    qkv = dot(wt_ref[...], x, NN) + bias_ref[:, 1:2]
    query = qkv[:narrow].astype(BF16) * (head_dim**-0.5)
    rest_low = qkv[narrow:].astype(BF16)
    qkv_ref[0, 0, :narrow] = query
    qkv_ref[0, 0, narrow:] = rest_low
    key_mask, query_mask = km_ref[0], qm_ref[0]
    logs = []
    if count == 1:
        for head in range(narrow // head_dim):
            lo = head * head_dim
            q_h = jnp.concatenate([query[lo : lo + head_dim], query_mask], 0)
            k_h = jnp.concatenate([rest_low[lo : lo + head_dim], key_mask], 0)
            v_h = rest_low[narrow + lo : narrow + lo + head_dim]
            scores = dot(k_h, q_h, TN)
            top = jnp.max(scores, axis=0, keepdims=True)
            raised = jnp.exp(scores - top)
            total = jnp.sum(raised, axis=0, keepdims=True)
            mixed = dot(v_h, raised.astype(BF16), NN) * (1.0 / total)
            o_ref[0, 0, lo : lo + head_dim] = mixed.astype(BF16)
            logs.append(top + jnp.log(total))
    else:
        heads = [head * head_dim for head in range(narrow // head_dim)]
        scores = [
            dot(
                jnp.concatenate([rest_low[lo : lo + head_dim], key_mask], 0),
                jnp.concatenate([query[lo : lo + head_dim], query_mask], 0),
                TN,
            )
            for lo in heads
        ]
        tops = [jnp.max(some, axis=0, keepdims=True) for some in scores]
        raised = [jnp.exp(some - top) for some, top in zip(scores, tops)]
        totals = [jnp.sum(some, axis=0, keepdims=True) for some in raised]
        for lo, some, top, total in zip(heads, raised, tops, totals):
            v_h = rest_low[narrow + lo : narrow + lo + head_dim]
            mixed = dot(v_h, some.astype(BF16), NN) * (1.0 / total)
            o_ref[0, 0, lo : lo + head_dim] = mixed.astype(BF16)
            logs.append(top + jnp.log(total))
    pad = jnp.zeros((8 - len(logs), x.shape[1]), F32)
    lse_ref[0, 0] = jnp.concatenate(logs + [pad], 0)


def attend(x, first, earlier, weights, biases, masks, layer, head_dim, through=(), needs=(), kind=shape):
    stacked, rows, narrow, seq = x.shape
    count = len(weights)
    dims = [(narrow, BF16), (3 * narrow, BF16), (8, F32), (narrow, BF16)]
    at = lambda s, r: (first + s, r, 0, 0)
    prior = [] if earlier is None else list(earlier)
    lanes = weights[0].shape[2]
    block = weights[0].shape[0] - 1
    here = 3 + 2 * count
    in_specs = (
        [pl.BlockSpec((1, 1, narrow, seq), at if stacked > 1 else (lambda s, r: (s, r, 0, 0)))]
        + [pl.BlockSpec((1, 16, seq), lambda s, r: (r, 0, 0))] * 2
        + [pl.BlockSpec((1, narrow, lanes), lambda s, r: (block, 0, 0))] * count
        + [pl.BlockSpec((1, 8, biases[0].shape[2]), lambda s, r: (layer, 0, 0))] * count
        + [ANY] * len(prior)
    )
    extra = len(through) + len(needs)
    inputs = [x, *masks, *weights, *biases, *prior]
    outs = [kind((GROUPS, rows, n, seq), t) for n, t in dims]
    made, base = len(outs), len(inputs)

    def kernel(*refs):
        attend_kernel(
            head_dim, len(prior), count,
            *refs[:base], *refs[base + extra : base + extra + made],
            *refs[base + extra + made + len(through) :],
        )

    aliases = {here + i: i for i in range(len(prior))}
    aliases.update({base + i: made + i for i in range(len(through))})
    results = pl.pallas_call(
        kernel,
        grid=(count, rows),
        in_specs=in_specs + [ANY] * extra,
        out_specs=[pl.BlockSpec((1, 1, n, seq), at) for n, _ in dims] + [ANY] * len(through),
        out_shape=outs + [shape(a.shape, a.dtype) for a in through],
        scratch_shapes=[
            pltpu.VMEM((3 * narrow, narrow), BF16),
            pltpu.VMEM((3 * narrow, 8), F32),
        ],
        input_output_aliases=aliases,
        compiler_params=params(12),
        cost_estimate=cost(0.01),
        name="attend_fwd",
    )(*inputs, *through, *needs)
    return results[:made], results[made:]


def attend_back_kernel(head_dim, count, aliased, *refs):
    x_ref, qkv_ref, dout_ref, da_ref, lse_ref, delta_ref, km_ref, qm_ref = refs[:8]
    w_refs, refs = refs[8 : 8 + count], refs[8 + count + aliased :]
    gx_ref, dw_ref, acc_ref, dqkv_ref, w_ref = refs
    narrow, seq = x_ref.shape[-2:]
    place, row = pl.program_id(0), pl.program_id(1)
    for s in range(count):

        @pl.when((place == s) & (row == 0))
        def _(s=s):
            w_ref[...] = w_refs[s][0, :, : 3 * narrow]

    key_mask, query_mask = km_ref[0], qm_ref[0]
    scale = head_dim**-0.5
    heads = [head * head_dim for head in range(narrow // head_dim)]
    queries = [qkv_ref[0, 0, lo : lo + head_dim] for lo in heads]
    keys = [qkv_ref[0, 0, narrow + lo : narrow + lo + head_dim] for lo in heads]
    grads = [dout_ref[0, 0, lo : lo + head_dim] for lo in heads]
    scores = [
        dot(jnp.concatenate([k, key_mask], 0), jnp.concatenate([q, query_mask], 0), TN)
        for q, k in zip(queries, keys)
    ]
    grad_probs = [
        dot(qkv_ref[0, 0, 2 * narrow + lo : 2 * narrow + lo + head_dim], g, TN)
        for lo, g in zip(heads, grads)
    ]
    probs = [jnp.exp(some - lse_ref[0, 0, i : i + 1]) for i, some in enumerate(scores)]
    grad_scores = [
        (p * (g - delta_ref[0, 0, i : i + 1])).astype(BF16)
        for i, (p, g) in enumerate(zip(probs, grad_probs))
    ]
    for i, lo in enumerate(heads):
        dqkv_ref[lo : lo + head_dim] = (dot(keys[i], grad_scores[i], NN) * scale).astype(BF16)
        dqkv_ref[narrow + lo : narrow + lo + head_dim] = dot(queries[i], grad_scores[i], NT).astype(BF16)
        dqkv_ref[2 * narrow + lo : 2 * narrow + lo + head_dim] = dot(
            grads[i], probs[i].astype(BF16), NT
        ).astype(BF16)
    dqkv = dqkv_ref[...]
    gx_ref[0, 0] = (dot(w_ref[...], dqkv, NN) + da_ref[0, 0].astype(F32)).astype(gx_ref.dtype)
    ones = jnp.ones((16, seq), BF16)
    term = dot(jnp.concatenate([x_ref[0, 0], ones], 0), dqkv, NT)

    @pl.when(row == 0)
    def _():
        acc_ref[...] = term

    @pl.when(row > 0)
    def _():
        acc_ref[...] += term

    @pl.when(row == pl.num_programs(1) - 1)
    def _():
        pieces = dw_ref.shape[1]
        step = narrow // pieces
        sums = acc_ref[narrow : narrow + 1]
        extra = jnp.concatenate(
            [sums[:, :narrow], sums[:, 2 * narrow :], jnp.zeros((step - 2, narrow), F32)], 0
        ).astype(BF16)
        for piece in range(pieces):
            part = acc_ref[piece * step : (piece + 1) * step].astype(BF16)
            dw_ref[0, piece, :, : 3 * narrow] = part
            dw_ref[0, piece, :, 3 * narrow :] = extra


def attend_back(order, pieces, acts, weights, masks, head_dim, out_type, stack, earlier=(), through=(), needs=()):
    _, rows, narrow, seq = acts[0].shape
    count = len(order)
    slot = (lambda s: (2 * s + 1) % 5) if count == 4 else (lambda s: order[0] + (order[-1] - order[0]) * s)
    at = lambda s, r: (slot(s), r, 0, 0)
    block = lambda n, where: pl.BlockSpec((1, 1, n, seq), where)
    lanes = weights[0].shape[2]
    last = weights[0].shape[0] - 1
    dims = (1, pieces, narrow // pieces, lanes)
    gx_kind, gx_count = (hbm, GROUPS) if stack else (shape, count)
    outs = [gx_kind((gx_count, rows, narrow, seq), out_type), shape((count,) + dims[1:], BF16)]
    specs = [
        block(narrow, at if stack else (lambda s, r: (s, r, 0, 0))),
        pl.BlockSpec(dims, lambda s, r: (s, 0, 0, 0)),
    ]
    return launch(
        functools.partial(attend_back_kernel, head_dim, count, len(earlier)),
        [*acts, *masks, *[weights[k] for k in order], *earlier],
        [block(a.shape[2], at) for a in acts]
        + [pl.BlockSpec((1, 16, seq), lambda s, r: (r, 0, 0))] * 2
        + [pl.BlockSpec((1, narrow, lanes), lambda s, r: (last, 0, 0))] * count
        + [ANY] * len(earlier),
        outs,
        specs,
        through,
        needs,
        aliases={8 + count: 0} if earlier else {},
        grid=(count, rows),
        scratch_shapes=[
            pltpu.VMEM((narrow + 16, 3 * narrow), F32),
            pltpu.VMEM((3 * narrow, seq), BF16),
            pltpu.VMEM((narrow, 3 * narrow), BF16),
        ],
        compiler_params=params(16),
        cost_estimate=cost(3.5 * count * rows),
        name="attend_bwd",
    )


def norm(values):
    width = values.shape[0]
    center = jnp.sum(values, axis=0, keepdims=True) * (1.0 / width)
    spread = jnp.sum(values * values, axis=0, keepdims=True) * (1.0 / width) - center * center
    inverse = lax.rsqrt(spread + EPSILON)
    return (values - center) * inverse, inverse


def norm_back(weighted, scaled, inverse):
    width = weighted.shape[0]
    first = jnp.sum(weighted, axis=0, keepdims=True) * (1.0 / width)
    second = jnp.sum(weighted * scaled, axis=0, keepdims=True) * (1.0 / width)
    return inverse * (weighted - first - scaled * second)


def normal_cdf(values):
    return 0.5 + 0.5 * lax.erf(values * 0.7071067811865476)


def whole(ref, me):
    return jnp.concatenate([ref[me ^ j, 0] for j in range(GROUPS)], 0)


def columns(layer, narrow, me, vec_refs, small_refs, small_ref):
    for k in range(GROUPS):
        small_ref[me ^ k] = small_refs[k][layer]
    out_bias = jnp.concatenate([small_ref[j, 1:2, 3 * narrow :] for j in range(GROUPS)], 1)
    rows = [ref[layer : layer + 1] for ref in vec_refs] + [out_bias]
    rows += [small_ref[j, 0:1] for j in range(GROUPS)]
    rows.append(jnp.zeros((16 - len(rows), out_bias.shape[1]), F32))
    return jnp.concatenate(rows, 0).T


def first_step():
    return (pl.program_id(0) == 0) & (pl.program_id(1) == 0)


def mix_kernel(layer, split, *refs):
    me_ref, xs_ref, o_ref, wp_ref = refs[:4]
    vec_refs, small_refs, w_refs = refs[4:9], refs[9:13], refs[13:17]
    count = GROUPS if split else 1
    next_refs, refs = refs[17 : 17 + count], refs[17 + count :]
    y1_ref, xh1_ref, xh2_ref, inv_ref, wpt_ref, wit_ref, wo_ref, small_ref, state_ref = refs
    me = me_ref[0]
    narrow = xs_ref.shape[2]

    @pl.when(first_step())
    def _():
        wpt_ref[...] = wp_ref[0].T
        for k in range(GROUPS):
            wit_ref[me ^ k] = w_refs[k][0].T
            wo_ref[me ^ k] = w_refs[k][1]

    cols = columns(layer, narrow, me, vec_refs, small_refs, small_ref)
    a = dot(wpt_ref[...], whole(o_ref, me), NN) + whole(xs_ref, me).astype(F32) + cols[:, 0:1]
    scaled_one, inverse_one = norm(a)
    y1 = (scaled_one * cols[:, 1:2] + cols[:, 2:3]).astype(BF16)
    y1_ref[0] = y1
    xh1_ref[0] = scaled_one.astype(BF16)
    hs = [
        dot(wit_ref[j], y1[j * narrow : (j + 1) * narrow], NN) + cols[:, 6 + j : 7 + j]
        for j in range(GROUPS)
    ]
    us = [(h * normal_cdf(h)).astype(BF16) for h in hs]
    z = jnp.concatenate([dot(wo_ref[j], us[j], NN) for j in range(GROUPS)], 0)
    scaled_two, inverse_two = norm(z + y1.astype(F32) + cols[:, 5:6])
    xh2_ref[0] = scaled_two.astype(BF16)
    state = (scaled_two * cols[:, 3:4] + cols[:, 4:5]).astype(BF16)
    for j in range(GROUPS):
        piece = state[j * narrow : (j + 1) * narrow]
        if split:
            state_ref[j] = piece
        else:
            next_refs[0][me ^ j, 0] = piece
    if split:
        for k in range(GROUPS):
            next_refs[k][0] = state_ref[me ^ k]
    inv_ref[0] = jnp.concatenate(
        [inverse_one, inverse_two, jnp.zeros((6, inverse_one.shape[1]), F32)], 0
    )


def mix(me, layer, split, xs, o, w_post, vectors, smalls, weights, tile, through=(), needs=(), kind=shape):
    _, rows, narrow, seq = xs.shape
    width = narrow * GROUPS
    ff = weights[0].shape[2]
    stacked = pl.BlockSpec((GROUPS, 1, narrow, tile), lambda r, t: (0, r, 0, t))
    plain = lambda n: pl.BlockSpec((1, n, tile), lambda r, t: (r, 0, t))
    const = lambda a: pl.BlockSpec(a.shape, lambda r, t: (0,) * a.ndim)
    outs = [shape((rows, narrow, seq), BF16)] * GROUPS if split else [vmem(xs.shape, BF16)]
    return launch(
        functools.partial(mix_kernel, layer, split),
        [me, xs, o, w_post, *vectors, *smalls, *weights],
        [SMEM, stacked, stacked, pl.BlockSpec((1, width, width), lambda r, t: (layer, 0, 0))]
        + [const(a) for a in (*vectors, *smalls)]
        + [pl.BlockSpec((2, narrow, ff), lambda r, t: (0, 0, 0))] * GROUPS,
        outs + [kind((rows, width, seq), BF16)] * 3 + [kind((rows, 8, seq), F32)],
        ([plain(narrow)] * GROUPS if split else [stacked]) + [plain(width)] * 3 + [plain(8)],
        through,
        needs,
        grid=(rows, seq // tile),
        scratch_shapes=[
            pltpu.VMEM((width, width), BF16),
            pltpu.VMEM((GROUPS, ff, narrow), BF16),
            pltpu.VMEM((GROUPS, narrow, ff), BF16),
            pltpu.VMEM((GROUPS, 8, ff), F32),
            pltpu.VMEM((GROUPS, narrow, tile), BF16),
        ],
        compiler_params=params(16),
        cost_estimate=cost(0.01),
        name="mix_fwd",
    )


def lane_sum(values):
    total = values[:, :128]
    for lo in range(128, values.shape[1], 128):
        total = total + values[:, lo : lo + 128]
    return total


def mix_back_kernel(layer, head_dim, *refs):
    me_ref, y1_ref, xh1_ref, xh2_ref, inv_ref, o_ref = refs[:6]
    gz_refs, wp_ref, vec_refs, small_refs, w_refs = refs[6:10], refs[10], refs[11:16], refs[16:20], refs[20:24]
    da_ref, dout_ref, delta_ref, f_odd_ref, f_even_ref, p_odd_ref, p_even_ref = refs[24:31]
    accf_ref, accp_ref, accv_ref, wit_ref, wot_ref, wi_ref, small_ref, gz_ref, tail_ref = refs[31:]
    me = me_ref[0]
    narrow, tile = o_ref.shape[2:]
    width = narrow * GROUPS
    step = pl.program_id(0) * pl.num_programs(1) + pl.program_id(1)
    steps = pl.num_programs(0) * pl.num_programs(1)

    @pl.when(first_step())
    def _():
        for k in range(GROUPS):
            wit_ref[me ^ k] = w_refs[k][0].T
            wi_ref[me ^ k] = w_refs[k][0]
            wot_ref[me ^ k] = w_refs[k][1].T
        accv_ref[...] = jnp.zeros_like(accv_ref)

    cols = columns(layer, narrow, me, vec_refs, small_refs, small_ref)
    for k in range(GROUPS):
        gz_ref[me ^ k] = gz_refs[k][0, 0].astype(F32)
    gz = jnp.concatenate([gz_ref[j] for j in range(GROUPS)], 0)
    y1 = y1_ref[0]
    scaled_one = xh1_ref[0].astype(F32)
    scaled_two = xh2_ref[0].astype(F32)
    inverse_one, inverse_two = inv_ref[0, 0:1], inv_ref[0, 1:2]
    accv_ref[0] += lane_sum(gz * scaled_two)
    accv_ref[1] += lane_sum(gz)
    dz = norm_back(gz * cols[:, 3:4], scaled_two, inverse_two)
    df = dz.astype(BF16)
    accv_ref[2] += lane_sum(df.astype(F32))
    ones = jnp.ones((16, tile), BF16)
    at = [slice(j * narrow, (j + 1) * narrow) for j in range(GROUPS)]
    hs = [dot(wit_ref[j], y1[at[j]], NN) + cols[:, 6 + j : 7 + j] for j in range(GROUPS)]
    back = [dot(wot_ref[j], df[at[j]], NN) for j in range(GROUPS)]
    us, dhs = [], []
    for h, some in zip(hs, back):
        cdf = normal_cdf(h)
        us.append((h * cdf).astype(BF16))
        dhs.append((some * (cdf + h * jnp.exp(-0.5 * h * h) * 0.3989422804014327)).astype(BF16))
    parts = [dz[at[j]] + dot(wi_ref[j], dhs[j], NN) for j in range(GROUPS)]
    so_far = lambda array: jnp.where(step == 0, 0.0, array)
    for j in range(GROUPS):
        out_term = dot(df[at[j]], us[j], NT)
        accf_ref[j, narrow + 16 :] = so_far(accf_ref[j, narrow + 16 :]) + out_term
        in_term = dot(jnp.concatenate([y1[at[j]], ones], 0), dhs[j], NT)
        accf_ref[j, : narrow + 16] = so_far(accf_ref[j, : narrow + 16]) + in_term
    dy1 = jnp.concatenate(parts, 0).astype(BF16).astype(F32)
    accv_ref[3] += lane_sum(dy1 * scaled_one)
    accv_ref[4] += lane_sum(dy1)
    da = norm_back(dy1 * cols[:, 1:2], scaled_one, inverse_one).astype(BF16)
    o = whole(o_ref, me)
    accp_ref[...] = so_far(accp_ref[...]) + dot(jnp.concatenate([o, ones], 0), da, NT)
    dout = dot(wp_ref[0], da, NN).astype(BF16)
    product = (o.astype(F32) * dout.astype(F32)).reshape(width // head_dim, head_dim, tile)
    delta = jnp.sum(product, axis=1)
    per_group = narrow // head_dim
    pad = jnp.zeros((8 - per_group, tile), F32)
    for j in range(GROUPS):
        lo = j * narrow
        da_ref[me ^ j, 0] = da[lo : lo + narrow]
        dout_ref[me ^ j, 0] = dout[lo : lo + narrow]
        delta_ref[me ^ j, 0] = jnp.concatenate(
            [delta[j * per_group : (j + 1) * per_group], pad], 0
        )

    @pl.when(step == steps - 1)
    def _():
        pieces = f_odd_ref.shape[1]
        vec = [jnp.sum(accv_ref[i].T, axis=0, keepdims=True) for i in range(5)]
        vec.append(accp_ref[width : width + 1])
        half = pieces // 2
        size, post = narrow // half, narrow // pieces
        for j in range(GROUPS):
            lo = j * narrow
            own = [v[:, lo : lo + narrow] for v in vec]
            tail_ref[j] = jnp.concatenate(
                [
                    accf_ref[j, narrow : narrow + 1],
                    jnp.concatenate(own[:4], 1),
                    jnp.concatenate(own[4:] + own[4:], 1),
                    jnp.zeros((5, width), F32),
                ],
                0,
            ).astype(BF16)
        for k in range(GROUPS):
            f_ref, p_ref = (f_odd_ref, p_odd_ref) if k % 2 else (f_even_ref, p_even_ref)
            j = me ^ k
            for piece in range(pieces):
                at = (piece % half) * size + (0 if piece < half else narrow + 16)
                f_ref[k // 2, piece] = accf_ref[j, at : at + size].astype(BF16)
                at = pl.multiple_of(j * narrow + piece * post, 8)
                p_ref[k // 2, piece, :post] = accp_ref[pl.ds(at, post)].astype(BF16)
                p_ref[k // 2, piece, post:] = tail_ref[j]


def mix_back(me, layer, pieces, kept, o, gz, w_post, vectors, smalls, weights, head_dim, tile, through=(), needs=(), kind=shape):
    _, rows, narrow, seq = o.shape
    width = narrow * GROUPS
    ff = weights[0].shape[2]
    stacked = pl.BlockSpec((GROUPS, 1, narrow, tile), lambda r, t: (0, r, 0, t))
    plain = lambda n: pl.BlockSpec((1, n, tile), lambda r, t: (r, 0, t))
    const = lambda dims: pl.BlockSpec(dims, lambda r, t: (0,) * len(dims))
    if isinstance(gz, list):
        gz_specs = [pl.BlockSpec((1, 1, narrow, tile), lambda r, t: (0, r, 0, t))] * GROUPS
    else:
        gz_specs = [
            pl.BlockSpec((1, 1, narrow, tile), lambda r, t, k=k: (k, r, 0, t))
            for k in range(GROUPS)
        ]
        gz = [gz] * GROUPS
    grads_f = (2, pieces, 2 * narrow // pieces, ff)
    grads_p = (2, pieces, narrow // pieces + 8, width)
    grads = [grads_f, grads_f, grads_p, grads_p]
    return launch(
        functools.partial(mix_back_kernel, layer, head_dim),
        [me, *kept, o, *gz, w_post, *vectors, *smalls, *weights],
        [SMEM] + [plain(width)] * 3 + [plain(8), stacked] + gz_specs
        + [pl.BlockSpec((1, width, width), lambda r, t: (layer, 0, 0))]
        + [const(a.shape) for a in (*vectors, *smalls)]
        + [const((2, narrow, ff))] * GROUPS,
        [kind(o.shape, BF16)] * 2 + [kind((GROUPS, rows, 8, seq), F32)]
        + [shape(g, BF16) for g in grads],
        [stacked, stacked, pl.BlockSpec((GROUPS, 1, 8, tile), lambda r, t: (0, r, 0, t))]
        + [const(g) for g in grads],
        through,
        needs,
        grid=(rows, seq // tile),
        scratch_shapes=[
            pltpu.VMEM((GROUPS, 2 * narrow + 16, ff), F32),
            pltpu.VMEM((width + 16, width), F32),
            pltpu.VMEM((5, width, 128), F32),
            pltpu.VMEM((GROUPS, ff, narrow), BF16),
            pltpu.VMEM((GROUPS, ff, narrow), BF16),
            pltpu.VMEM((GROUPS, narrow, ff), BF16),
            pltpu.VMEM((GROUPS, 8, ff), F32),
            pltpu.VMEM((GROUPS, narrow, tile), F32),
            pltpu.VMEM((GROUPS, 8, width), BF16),
        ],
        compiler_params=params(30),
        cost_estimate=cost(24.0),
        name="mix_bwd",
    )


def swap(array, axis, distance):
    size = lax.axis_size(axis)
    return lax.ppermute(array, axis, [(i, i ^ distance) for i in range(size)])


def collect_kernel(me_ref, *refs):
    out = refs[-1]
    for k, ref in enumerate(refs[:-1]):
        out[me_ref[0] ^ k, 0] = ref[0].astype(out.dtype)


def collect(me, arrays, needs=(), dtype=F32, through=None):
    rows, rest = arrays[0].shape[0], arrays[0].shape[1:]
    zeros = (0,) * len(rest)
    (out,), passed = launch(
        collect_kernel,
        [me, *arrays],
        [SMEM] + [pl.BlockSpec((1,) + rest, lambda r: (r,) + zeros)] * GROUPS,
        [(hbm if dtype == F32 else shape)((GROUPS, rows) + rest, dtype)],
        [pl.BlockSpec((GROUPS, 1) + rest, lambda r: (0, r) + zeros)],
        through or (),
        needs,
        grid=(rows,),
        compiler_params=params(12),
        cost_estimate=cost(0.1),
        name="collect",
    )
    return out if through is None else (out, passed)


def total(*arrays):
    return functools.reduce(lambda a, b: a + b, [a.astype(F32) for a in arrays])


def combine_kernel(sizes, spread, me_ref, *refs):
    count = sum(sizes)
    ins, outs = refs[:count], refs[count:]
    for d, out in enumerate(outs):
        start, row = 0, 0
        for size in sizes:
            terms = ins[start : start + size]
            rows = terms[0].shape[2]
            if spread:
                per = terms[0].shape[1] // len(outs)
                at = (me_ref[0] ^ d) * per
                part = total(*[ref[0, pl.ds(at, per)] for ref in terms])
            else:
                part = total(*[ref[0] for ref in terms])
            out[:, row : row + rows] = part.astype(BF16)
            start, row = start + size, row + rows


def combine(parts, me, spread=0, needs=()):
    flat = [a if isinstance(a, tuple) else (a[None], 0) for part in parts for a in part]
    pieces, _, lanes = flat[0][0].shape[1:]
    rows = sum((p[0][0].shape[2] if isinstance(p[0], tuple) else p[0].shape[1]) for p in parts)
    count = max(1, spread)
    outs, _ = launch(
        functools.partial(combine_kernel, [len(p) for p in parts], spread),
        [me] + [a for a, _ in flat],
        [SMEM]
        + [pl.BlockSpec((1, pieces, a.shape[2], lanes), lambda i, k=k: (k, 0, 0, 0)) for a, k in flat],
        [shape((pieces // count, rows, lanes), BF16)] * count,
        [pl.BlockSpec((pieces // count, rows, lanes), lambda i: (0, 0, 0))] * count,
        (),
        needs,
        grid=(1,),
        compiler_params=params(12),
        cost_estimate=cost(0.1),
        name="combine",
    )
    return outs if spread else outs[0]


def finish_post_kernel(post, layers, me_ref, *refs):
    ins, refs = refs[:GROUPS], refs[GROUPS + 1 :]
    small, refs = refs[: layers * GROUPS], refs[layers * GROUPS :]
    dpost_ref, vec_refs = refs[0], refs[1:]
    me = me_ref[0]
    for k, ref in enumerate(ins):
        dpost_ref[0, me ^ k] = ref[:, :post].astype(F32)

    if layers:
        width = vec_refs[0].shape[1]
        narrow = width // GROUPS

        @pl.when(pl.program_id(0) == pl.num_programs(0) - 1)
        def _():
            for layer in range(layers):
                for k in range(GROUPS):
                    both = small[layer * GROUPS + k][0].astype(F32)[8:]
                    rows = [
                        both[1 + i // 4 : 2 + i // 4, i % 4 * narrow : (i % 4 + 1) * narrow]
                        for i in range(6)
                    ]
                    if k == 0:
                        vec_refs[6][layer] = both[0:1]
                        vec_refs[7][layer] = rows[2]
                    for j in range(GROUPS):

                        @pl.when((me ^ k) == j)
                        def _(j=j, rows=rows, layer=layer):
                            for i in range(6):
                                vec_refs[i][layer : layer + 1, j * narrow : (j + 1) * narrow] = rows[i]


def finish_post(me, layer, slots, prior, all_slots, post, needs=()):
    pieces, rows, width = slots[0].shape
    narrow = width // GROUPS
    small = [a for some in all_slots for a in some]
    outs = [hbm((LAYERS, GROUPS, pieces, post, width), F32)]
    specs = [pl.BlockSpec((1, GROUPS, pieces // 2, post, width), lambda i: (layer, 0, i, 0, 0))]
    if small:
        outs += [shape((LAYERS, width), F32)] * 6
        outs += [shape((LAYERS, 1, width), F32), shape((LAYERS, 1, narrow), F32)]
        specs += [pl.BlockSpec(o.shape, lambda i, n=len(o.shape): (0,) * n) for o in outs[1:]]
    if prior is None:
        prior, aliases = me, {}
    else:
        aliases = {1 + GROUPS: 0}
    return launch(
        functools.partial(finish_post_kernel, post, len(all_slots)),
        [me, *slots, prior, *small],
        [SMEM]
        + [pl.BlockSpec((pieces // 2, rows, width), lambda i: (i, 0, 0))] * GROUPS
        + [ANY if aliases else SMEM]
        + [pl.BlockSpec((1, 16, width), lambda i: (0, (rows - 16) // 16, 0))] * len(small),
        outs,
        specs,
        (),
        needs,
        aliases=aliases,
        grid=(2,),
        compiler_params=params(12),
        cost_estimate=cost(0.1),
        name="finish_post",
    )[0]


def finish_ffn_kernel(size, me_ref, *refs):
    parts, last_ref = refs[:4], refs[4]
    wi_ref, wo_ref = refs[5:]
    layer = pl.program_id(0)

    def put(shard, part):
        @pl.when(shard < 2)
        def _():
            wi_ref[0, shard] = part.astype(F32)

        @pl.when(shard >= 2)
        def _():
            wo_ref[0, shard - 2] = part.astype(F32)

    @pl.when(layer == 0)
    def _():
        for d, ref in enumerate(parts):
            put(me_ref[0] ^ d, ref[:, :size])

    @pl.when(layer > 0)
    def _():
        for d in range(4):
            put(d, last_ref[2 * d : 2 * d + 2, :size])


def finish_ffn(me, parts, last, size, needs=()):
    half, _, lanes = parts[0].shape
    out = hbm((LAYERS, 2, half, size, lanes), F32)
    return launch(
        functools.partial(finish_ffn_kernel, size),
        [me, *parts, last],
        [SMEM] + [pl.BlockSpec(a.shape, lambda l: (0, 0, 0)) for a in (*parts, last)],
        [out] * 2,
        [pl.BlockSpec((1, 2, half, size, lanes), lambda l: (l, 0, 0, 0, 0))] * 2,
        (),
        needs,
        grid=(LAYERS,),
        compiler_params=params(12),
        cost_estimate=cost(0.1),
        name="finish_ffn",
    )[0]


def finish_qkv_kernel(lo, post, me_ref, *refs):
    sets, outs = (refs[:4], refs[4:8]), refs[8:]
    narrow = outs[0].shape[-1]
    for layer, parts in enumerate(sets):
        start = lo if layer else 0
        for d, ref in enumerate(parts):
            part = ref[:, start : start + post].astype(F32)
            for i in range(3):
                outs[i][layer, me_ref[0] ^ d] = part[:, :, i * narrow : (i + 1) * narrow]
            if d == 0:
                outs[3][layer] = part[0, 0:1, 3 * narrow :]
                outs[4][layer] = part[0, 1:2, 3 * narrow :]


def finish_qkv(me, first, second, lo, narrow, needs=()):
    half, post, lanes = first[0].shape
    big = shape((LAYERS, 4, half, post, narrow), F32)
    vec = shape((LAYERS, 1, narrow), F32)
    full = pl.BlockSpec(memory_space=pltpu.VMEM)
    return launch(
        functools.partial(finish_qkv_kernel, lo, post),
        [me, *first, *second],
        [SMEM] + [full] * 8,
        [big] * 3 + [vec] * 2,
        [full] * 5,
        (),
        needs,
        compiler_params=params(12),
        cost_estimate=cost(0.1),
        name="finish_qkv",
    )[0]


def fold_kernel(in_ref, out_ref):
    part = total(*[in_ref[i] for i in range(in_ref.shape[0])]).astype(BF16)
    for i in range(out_ref.shape[0]):
        out_ref[i] = part


def fold(array, through=(), needs=()):
    pieces, rows, lanes = array.shape
    block = pl.BlockSpec((pieces, rows, lanes), lambda i: (0, 0, 0))
    (out,), passed = launch(
        fold_kernel,
        [array],
        [block],
        [shape(array.shape, BF16)],
        [block],
        through,
        needs,
        grid=(1,),
        compiler_params=params(12),
        cost_estimate=cost(0.1),
        name="fold",
    )
    return (out, *passed)


def dp_groups(pieces):
    return [list(range(i, i + pieces)) for i in range(0, lax.axis_size("dp"), pieces)]


def trade(array):
    return lax.all_to_all(
        array, "dp", split_axis=0, concat_axis=0, tiled=True,
        axis_index_groups=dp_groups(array.shape[0]),
    )


def beyond(copies):
    distance = copies.shape[0]
    while distance < lax.axis_size("dp"):
        copies = total(copies, swap(copies, "dp", distance)).astype(BF16)
        distance *= 2
    return copies


def near_dp(parts):
    return [parts[0]] + [swap(part, "dp", d) for d, part in enumerate(parts) if d]


def across_dp(sums, needs=(), block=4):
    distance = block
    while distance < lax.axis_size("dp"):
        sums = add([[mine, swap(mine, "dp", distance)] for mine in sums], (), needs)
        distance *= 2
    return sums


def add_kernel(sizes, *refs):
    ins, outs = refs[: sum(sizes)], refs[sum(sizes) :]
    start = 0
    for size, out in zip(sizes, outs):
        out[...] = total(*[ref[...] for ref in ins[start : start + size]]).astype(BF16)
        start += size


def add(lists, through=(), needs=(), micros=0.1):
    flat = [a for arrays in lists for a in arrays]
    spec = lambda a: pl.BlockSpec(a.shape, lambda i: (0, 0, 0))
    outs, passed = launch(
        functools.partial(add_kernel, [len(arrays) for arrays in lists]),
        flat,
        [spec(a) for a in flat],
        [shape(arrays[0].shape, BF16) for arrays in lists],
        [spec(arrays[0]) for arrays in lists],
        through,
        needs,
        grid=(1,),
        compiler_params=params(16),
        cost_estimate=cost(micros),
        name="add",
    )
    return (*outs, *passed)


def pick(array, index):
    return lax.dynamic_index_in_dim(array, index, 0, keepdims=False)


def shards(
    hidden_in,
    segment_ids,
    w_query,
    b_query,
    w_key,
    w_value,
    b_value,
    w_post,
    b_post,
    ln1_gain,
    ln1_bias,
    w_inter,
    b_inter,
    w_output,
    b_output,
    ln2_gain,
    ln2_bias,
    cotangent,
):
    row_count, narrow, seq = hidden_in.shape
    rows = row_count // GROUPS
    width = narrow * GROUPS
    ff = w_inter.shape[-1]
    head_dim = width // HEADS
    me = lax.axis_index("grp")
    me_ref = me.reshape(1).astype(jnp.int32)
    pieces = 8
    tile = 256

    by_owner = hidden_in.reshape(GROUPS, rows, narrow, seq)
    cot_owner = cotangent.reshape(GROUPS, rows, narrow, seq)
    no_bias = jnp.zeros_like(b_query)
    small = jnp.concatenate([b_query, no_bias, b_value, b_output], 2)
    small = jnp.pad(jnp.concatenate([b_inter, small], 1), ((0, 0), (0, 6), (0, 0)))
    pad = jnp.zeros((LAYERS, 1, narrow, ff - 3 * narrow), BF16)
    w_qkv = jnp.concatenate([w_query, w_key, w_value, pad], 3)
    ffn_own = jnp.concatenate([w_inter[0], w_output[0]], 0)
    both_own = jnp.concatenate([w_inter[1], w_output[1], w_qkv[1]], 0)

    segments = lax.dynamic_slice_in_dim(segment_ids, me * rows, rows, 0)
    hot = segments[:, None, :] == jnp.arange(16, dtype=segments.dtype)[None, :, None]
    masks = (hot.astype(BF16), jnp.where(hot, 0.0, MASKED).astype(BF16))

    small_far, qkv_far = swap(small, "grp", 2), swap(w_qkv[0], "grp", 2)
    smalls = [small, swap(small, "grp", 1), small_far, swap(small_far, "grp", 1)]
    qkv0 = [w_qkv[0], swap(w_qkv[0], "grp", 1), qkv_far, swap(qkv_far, "grp", 1)]
    x_slots = [pick(by_owner, me)] + [swap(pick(by_owner, me ^ k), "grp", k) for k in (1, 2, 3)]

    acts0, _ = attend(
        x_slots[0][None], 0, None, qkv0[:1], smalls[:1], masks, 0, head_dim, kind=hbm
    )
    acts0, _ = attend(
        x_slots[1][None], 1, acts0, qkv0[1:2], smalls[1:2], masks, 0, head_dim, kind=hbm
    )
    acts0, (ffn_own,) = attend(
        x_slots[2][None], 2, acts0, qkv0[2:3], smalls[2:3], masks, 0, head_dim, [ffn_own],
        kind=hbm,
    )
    ffn_far = swap(ffn_own, "grp", 2)
    ffn0 = [ffn_own, swap(ffn_own, "grp", 1), ffn_far, swap(ffn_far, "grp", 1)]
    acts0, (both_own,) = attend(
        x_slots[3][None], 3, acts0, qkv0[3:4], smalls[3:4], masks, 0, head_dim, [both_own],
        kind=hbm,
    )
    both_far = swap(both_own, "grp", 2)
    both_near = swap(both_own, "grp", 1)
    o0, qkvs0, lse0, xs0 = [held(a, pltpu.HBM) for a in acts0]
    vectors = (b_post, ln1_gain, ln1_bias, ln2_gain, ln2_bias)
    (state, *kept0), cot_send = mix(
        me_ref, 0, False, xs0, o0, w_post, vectors, smalls, ffn0, tile,
        [pick(cot_owner, me ^ k) for k in (1, 2, 3)],
        kind=hbm,
    )
    kept0 = [held(a, pltpu.HBM) for a in kept0]
    state = held(state)
    cot_slots = [pick(cot_owner, me)[None]] + [
        swap(cot_send[k - 1], "grp", k)[None] for k in (1, 2, 3)
    ]
    acts1, (both_far,) = attend(
        state, 0, None, [both_own, both_near], smalls[:2], masks, 1, head_dim, [both_far]
    )
    both1 = [both_own, both_near, both_far, swap(both_far, "grp", 1)]
    acts1, _ = attend(state, 2, acts1, both1[2:], smalls[2:], masks, 1, head_dim)
    o1, qkvs1, lse1, xs1 = acts1
    results, _ = mix(me_ref, 1, True, xs1, o1, w_post, vectors, smalls, both1, tile)
    state_slots, kept1 = results[:GROUPS], results[GROUPS:]
    state_slots = [state_slots[0]] + [swap(state_slots[k], "grp", k) for k in (1, 2, 3)]

    me_four = (lax.axis_index("dp") % 4).reshape(1).astype(jnp.int32)
    (da1, dout1, delta1, f_odd, f_even, p_odd, p_even), _ = mix_back(
        me_ref, 1, pieces, kept1, o1, cot_slots, w_post, vectors, smalls, both1, head_dim, tile
    )
    hidden_out, passed = collect(
        me_ref, state_slots, through=(da1, dout1, delta1, f_odd, f_even, p_odd, p_even)
    )
    da1, dout1, delta1, f_odd, f_even, p_odd, p_even = passed
    f_near, p_near = swap(f_odd, "grp", 1), swap(p_odd, "grp", 1)
    send = combine([[(f_even, 1), (f_near, 1)], [(p_even, 1), (p_near, 1)]], me_ref)
    far = swap(send, "grp", 2)
    acts = (xs1, qkvs1, dout1, da1, lse1, delta1)
    (gz, dw_odd1), _ = attend_back(
        [1, 3], pieces, acts, both1, masks, head_dim, F32, True, (), (), (send,)
    )
    near_q1 = swap(dw_odd1, "grp", 1)
    own_f = combine([[(f_even, 0), (f_near, 0)], [(p_even, 0), (p_near, 0)]], me_ref, 0, (dw_odd1,))
    (gz, dw_even1), _ = attend_back(
        [0, 2], pieces, acts, both1, masks, head_dim, F32, True, (gz,), (), (own_f,)
    )
    gz = held(gz, pltpu.HBM)
    (own1,) = add([[own_f, far]], (), (dw_even1,))
    moved1 = trade(own1)
    send_q1 = combine([[(dw_even1, 1), (near_q1, 1)]], me_ref, 0, (own1,))
    far_q1 = swap(send_q1, "grp", 2)
    (da0, dout0, delta0, f_odd, f_even, p_odd, p_even), _ = mix_back(
        me_ref, 0, pieces, kept0, o0, gz, w_post, vectors, smalls, ffn0, head_dim, tile,
        (), (send_q1,), hbm,
    )
    p_near, f_near = swap(p_odd, "grp", 1), swap(f_odd, "grp", 1)
    send_p = combine([[(p_even, 1), (p_near, 1)]], me_ref)
    far_p = swap(send_p, "grp", 2)
    send_f = combine([[(f_even, 1), (f_near, 1)]], me_ref, 0, (send_p,))
    far_f = swap(send_f, "grp", 2)
    dout0, da0, delta0 = [held(a, pltpu.HBM) for a in (dout0, da0, delta0)]
    acts = (xs0, qkvs0, dout0, da0, lse0, delta0)
    qkv0 = [held(w, pltpu.HBM) for w in qkv0]
    (mine1,) = fold(moved1, (), (send_f,))
    all1 = trade(beyond(mine1))
    back = lambda order, *rest: attend_back(
        order, pieces, acts, qkv0, masks, head_dim, BF16, False, (), *rest
    )
    (gx32, dw32), _ = back([3, 2], (), (mine1, far_q1))
    near_w3 = swap(dw32[:1], "grp", 1)
    own_p = combine([[(p_even, 0), (p_near, 0), far_p]], me_four, 4, (dw32,))
    parts_p = near_dp(own_p)
    send_w = combine([[(dw32, 1), (near_w3, 0)]], me_ref, 0, (own_p[0],))
    far_w = swap(send_w, "grp", 2)
    own_f = combine(
        [[(f_even, 0), (f_near, 0), far_f], [(dw_even1, 0), (near_q1, 0), far_q1]], me_four, 4,
        (send_w, all1),
    )
    parts_f = near_dp(own_f)
    size, post = 2 * narrow // pieces, narrow // pieces
    last_p = all1[:, size:]
    last_far = swap(last_p, "grp", 2)
    (mine_p,) = add([parts_p], (), (own_f[0],))
    across_p = swap(mine_p, "dp", 4)
    (gx10, dw10), _ = back([1, 0], (), (mine_p,))
    gx2, gx3 = swap(gx32[1], "grp", 2), swap(gx32[0], "grp", 3)
    mine_p, mine_f, gx10, dw10 = add(
        [[mine_p, across_p], parts_f], (gx10, dw10), (gx2, gx3, last_far, far_w)
    )
    near_w1 = swap(dw10[:1], "grp", 1)
    gx_slots = [gx10[1], swap(gx10[0], "grp", 1), gx2, gx3]
    own_q = combine([[(dw10, 1), (near_w1, 0), far_w]], me_four, 4, (mine_p,))
    parts_q = near_dp(own_q)
    (mine_p,) = across_dp([mine_p], (), 8)
    parts_p = near_dp([mine_p] * 4)
    across_f = swap(mine_f, "dp", 4)
    (mine_q,) = add([parts_q])
    across_q = swap(mine_q, "dp", 4)
    (mine_f,) = add([[mine_f, across_f]], (), (mine_q,))
    (mine_f,) = across_dp([mine_f], (), 8)
    parts_f = near_dp([mine_f] * 4)
    all_p = collect(me_four, parts_p, (mine_f,), BF16).reshape(pieces, -1, width)
    far_shared = swap(all_p, "grp", 2)
    near_shared = swap(all_p, "grp", 1)
    shared1 = [last_p, swap(last_p, "grp", 1), last_far, swap(last_far, "grp", 1)]
    (prior,) = finish_post(me_ref, 1, shared1, None, [], post, (all_p,))
    grad_input = collect(me_ref, gx_slots, (held(prior, pltpu.HBM),))
    mine_q, far_shared = add(
        [[mine_q, across_q]], (far_shared,), (held(grad_input, pltpu.HBM), *parts_f[1:]), 10.0
    )
    (mine_q,) = across_dp([mine_q], (), 8)
    parts_q = near_dp([mine_q] * 4)
    shared0 = [all_p, near_shared, far_shared, swap(far_shared, "grp", 1)]

    dpost, *vec = finish_post(me_ref, 0, shared0, prior, [shared0, shared1], post, (mine_q,))
    d_inter, d_output = finish_ffn(me_four, parts_f, all1, size, (mine_q,))
    dq, dk, dv, dbq, dbv = finish_qkv(
        me_four, parts_q, parts_f, size, narrow,
        (held(d_inter, pltpu.HBM), held(dpost, pltpu.HBM)),
    )
    ffn_shape, qkv_shape = (LAYERS, 1, narrow, ff), (LAYERS, 1, narrow, narrow)
    return (
        hidden_out.reshape(row_count, narrow, seq),
        grad_input.reshape(row_count, narrow, seq),
        dq.reshape(qkv_shape),
        dbq,
        dk.reshape(qkv_shape),
        dv.reshape(qkv_shape),
        dbv,
        dpost.reshape(LAYERS, width, width),
        vec[5],
        vec[3],
        vec[4],
        d_inter.reshape(ffn_shape),
        vec[6],
        d_output.reshape(ffn_shape),
        vec[7],
        vec[0],
        vec[1],
    )


def solution(mesh):
    placed = (
        P("dp", "grp", None),
        P("dp", None),
        P(None, "grp", None, None),
        P(None, "grp", None),
        P(None, "grp", None, None),
        P(None, "grp", None, None),
        P(None, "grp", None),
        P(),
        P(),
        P(),
        P(),
        P(None, "grp", None, None),
        P(None, "grp", None),
        P(None, "grp", None, None),
        P(None, "grp", None),
        P(),
        P(),
        P("dp", "grp", None),
    )
    return jax.shard_map(
        shards,
        mesh=mesh,
        in_specs=placed,
        out_specs=(
            P("dp", "grp", None),
            P("dp", "grp", None),
            P(None, "grp", None, None),
            P(None, "grp", None),
            P(None, "grp", None, None),
            P(None, "grp", None, None),
            P(None, "grp", None),
            P(),
            P(),
            P(),
            P(),
            P(None, "grp", None, None),
            P(None, "grp", None),
            P(None, "grp", None, None),
            P(None, "grp", None),
            P(),
            P(),
        ),
        check_vma=False,
    )
```

```python
import functools

import jax
import jax.numpy as jnp
from jax import lax
from jax.experimental import pallas as pl
from jax.experimental.pallas import tpu as pltpu
from jax.sharding import PartitionSpec as P


HEADS = 12
LAYERS = 2
GROUPS = 4
EPSILON = 1e-05
MASKED = -1e30

F32 = jnp.float32
BF16 = jnp.bfloat16
NN = (((1,), (0,)), ((), ()))
NT = (((1,), (1,)), ((), ()))
TN = (((0,), (0,)), ((), ()))
MIB = 1 << 20


def dot(left, right, dims):
    return lax.dot_general(left, right, dims, preferred_element_type=F32)


def params(limit=60):
    return pltpu.CompilerParams(vmem_limit_bytes=limit * MIB)


def cost(micros):
    return pl.CostEstimate(flops=int(micros * 1e9), bytes_accessed=1 << 10, transcendentals=0)


def shape(dims, dtype):
    return jax.ShapeDtypeStruct(dims, dtype)


def hbm(dims, dtype):
    return pltpu.HBM(dims, dtype)


def vmem(dims, dtype):
    return pltpu.VMEM(dims, dtype)


def held(array, space=pltpu.VMEM):
    return pltpu.with_memory_space_constraint(array, space)


SMEM = pl.BlockSpec(memory_space=pltpu.SMEM)
ANY = pl.BlockSpec(memory_space=pl.ANY)


def launch(body, arrays, in_specs, outs, out_specs, through=(), needs=(), aliases=None, **kwargs):
    count, made = len(arrays), len(outs)
    extra = len(through) + len(needs)

    def kernel(*refs):
        body(*refs[:count], *refs[count + extra : count + extra + made], *refs[count + extra + made + len(through) :])

    results = pl.pallas_call(
        kernel,
        in_specs=list(in_specs) + [ANY] * extra,
        out_specs=list(out_specs) + [ANY] * len(through),
        out_shape=list(outs) + [shape(a.shape, a.dtype) for a in through],
        input_output_aliases={
            **(aliases or {}),
            **{count + i: made + i for i in range(len(through))},
        },
        **kwargs,
    )(*arrays, *through, *needs)
    return results[:made], results[made:]


def attend_kernel(head_dim, aliased, count, *refs):
    x_ref, km_ref, qm_ref = refs[:3]
    w_refs, b_refs = refs[3 : 3 + count], refs[3 + count : 3 + 2 * count]
    o_ref, qkv_ref, lse_ref, xs_ref, wt_ref, bias_ref = refs[3 + 2 * count + aliased :]
    narrow = x_ref.shape[-2]
    for k in range(count):

        @pl.when((pl.program_id(1) == 0) & (pl.program_id(0) == k))
        def _(k=k):
            wt_ref[...] = w_refs[k][0].T[: 3 * narrow]
            bias_ref[...] = b_refs[k][0].T[: 3 * narrow]

    x = x_ref[0, 0]
    xs_ref[0, 0] = x
    qkv = dot(wt_ref[...], x, NN) + bias_ref[:, 1:2]
    query = qkv[:narrow].astype(BF16) * (head_dim**-0.5)
    rest_low = qkv[narrow:].astype(BF16)
    qkv_ref[0, 0, :narrow] = query
    qkv_ref[0, 0, narrow:] = rest_low
    key_mask, query_mask = km_ref[0], qm_ref[0]
    logs = []
    if count == 1:
        for head in range(narrow // head_dim):
            lo = head * head_dim
            q_h = jnp.concatenate([query[lo : lo + head_dim], query_mask], 0)
            k_h = jnp.concatenate([rest_low[lo : lo + head_dim], key_mask], 0)
            v_h = rest_low[narrow + lo : narrow + lo + head_dim]
            scores = dot(k_h, q_h, TN)
            top = jnp.max(scores, axis=0, keepdims=True)
            raised = jnp.exp(scores - top)
            total = jnp.sum(raised, axis=0, keepdims=True)
            mixed = dot(v_h, raised.astype(BF16), NN) * (1.0 / total)
            o_ref[0, 0, lo : lo + head_dim] = mixed.astype(BF16)
            logs.append(top + jnp.log(total))
    else:
        heads = [head * head_dim for head in range(narrow // head_dim)]
        scores = [
            dot(
                jnp.concatenate([rest_low[lo : lo + head_dim], key_mask], 0),
                jnp.concatenate([query[lo : lo + head_dim], query_mask], 0),
                TN,
            )
            for lo in heads
        ]
        tops = [jnp.max(some, axis=0, keepdims=True) for some in scores]
        raised = [jnp.exp(some - top) for some, top in zip(scores, tops)]
        totals = [jnp.sum(some, axis=0, keepdims=True) for some in raised]
        for lo, some, top, total in zip(heads, raised, tops, totals):
            v_h = rest_low[narrow + lo : narrow + lo + head_dim]
            mixed = dot(v_h, some.astype(BF16), NN) * (1.0 / total)
            o_ref[0, 0, lo : lo + head_dim] = mixed.astype(BF16)
            logs.append(top + jnp.log(total))
    pad = jnp.zeros((8 - len(logs), x.shape[1]), F32)
    lse_ref[0, 0] = jnp.concatenate(logs + [pad], 0)


def attend(x, first, earlier, weights, biases, masks, layer, head_dim, through=(), needs=(), kind=shape):
    stacked, rows, narrow, seq = x.shape
    count = len(weights)
    dims = [(narrow, BF16), (3 * narrow, BF16), (8, F32), (narrow, BF16)]
    at = lambda s, r: (first + s, r, 0, 0)
    prior = [] if earlier is None else list(earlier)
    lanes = weights[0].shape[2]
    block = weights[0].shape[0] - 1
    here = 3 + 2 * count
    in_specs = (
        [pl.BlockSpec((1, 1, narrow, seq), at if stacked > 1 else (lambda s, r: (s, r, 0, 0)))]
        + [pl.BlockSpec((1, 16, seq), lambda s, r: (r, 0, 0))] * 2
        + [pl.BlockSpec((1, narrow, lanes), lambda s, r: (block, 0, 0))] * count
        + [pl.BlockSpec((1, 8, biases[0].shape[2]), lambda s, r: (layer, 0, 0))] * count
        + [ANY] * len(prior)
    )
    extra = len(through) + len(needs)
    inputs = [x, *masks, *weights, *biases, *prior]
    outs = [kind((GROUPS, rows, n, seq), t) for n, t in dims]
    made, base = len(outs), len(inputs)

    def kernel(*refs):
        attend_kernel(
            head_dim, len(prior), count,
            *refs[:base], *refs[base + extra : base + extra + made],
            *refs[base + extra + made + len(through) :],
        )

    aliases = {here + i: i for i in range(len(prior))}
    aliases.update({base + i: made + i for i in range(len(through))})
    results = pl.pallas_call(
        kernel,
        grid=(count, rows),
        in_specs=in_specs + [ANY] * extra,
        out_specs=[pl.BlockSpec((1, 1, n, seq), at) for n, _ in dims] + [ANY] * len(through),
        out_shape=outs + [shape(a.shape, a.dtype) for a in through],
        scratch_shapes=[
            pltpu.VMEM((3 * narrow, narrow), BF16),
            pltpu.VMEM((3 * narrow, 8), F32),
        ],
        input_output_aliases=aliases,
        compiler_params=params(12),
        cost_estimate=cost(0.01),
        name="attend_fwd",
    )(*inputs, *through, *needs)
    return results[:made], results[made:]


def attend_back_kernel(head_dim, count, aliased, *refs):
    x_ref, qkv_ref, dout_ref, da_ref, lse_ref, delta_ref, km_ref, qm_ref = refs[:8]
    w_refs, refs = refs[8 : 8 + count], refs[8 + count + aliased :]
    gx_ref, dw_ref, acc_ref, dqkv_ref, w_ref = refs
    narrow, seq = x_ref.shape[-2:]
    place, row = pl.program_id(0), pl.program_id(1)
    for s in range(count):

        @pl.when((place == s) & (row == 0))
        def _(s=s):
            w_ref[...] = w_refs[s][0, :, : 3 * narrow]

    key_mask, query_mask = km_ref[0], qm_ref[0]
    scale = head_dim**-0.5
    heads = [head * head_dim for head in range(narrow // head_dim)]
    queries = [qkv_ref[0, 0, lo : lo + head_dim] for lo in heads]
    keys = [qkv_ref[0, 0, narrow + lo : narrow + lo + head_dim] for lo in heads]
    grads = [dout_ref[0, 0, lo : lo + head_dim] for lo in heads]
    scores = [
        dot(jnp.concatenate([k, key_mask], 0), jnp.concatenate([q, query_mask], 0), TN)
        for q, k in zip(queries, keys)
    ]
    grad_probs = [
        dot(qkv_ref[0, 0, 2 * narrow + lo : 2 * narrow + lo + head_dim], g, TN)
        for lo, g in zip(heads, grads)
    ]
    probs = [jnp.exp(some - lse_ref[0, 0, i : i + 1]) for i, some in enumerate(scores)]
    grad_scores = [
        (p * (g - delta_ref[0, 0, i : i + 1])).astype(BF16)
        for i, (p, g) in enumerate(zip(probs, grad_probs))
    ]
    for i, lo in enumerate(heads):
        dqkv_ref[lo : lo + head_dim] = (dot(keys[i], grad_scores[i], NN) * scale).astype(BF16)
        dqkv_ref[narrow + lo : narrow + lo + head_dim] = dot(queries[i], grad_scores[i], NT).astype(BF16)
        dqkv_ref[2 * narrow + lo : 2 * narrow + lo + head_dim] = dot(
            grads[i], probs[i].astype(BF16), NT
        ).astype(BF16)
    dqkv = dqkv_ref[...]
    gx_ref[0, 0] = (dot(w_ref[...], dqkv, NN) + da_ref[0, 0].astype(F32)).astype(gx_ref.dtype)
    ones = jnp.ones((16, seq), BF16)
    term = dot(jnp.concatenate([x_ref[0, 0], ones], 0), dqkv, NT)

    @pl.when(row == 0)
    def _():
        acc_ref[...] = term

    @pl.when(row > 0)
    def _():
        acc_ref[...] += term

    @pl.when(row == pl.num_programs(1) - 1)
    def _():
        pieces = dw_ref.shape[1]
        step = narrow // pieces
        sums = acc_ref[narrow : narrow + 1]
        extra = jnp.concatenate(
            [sums[:, :narrow], sums[:, 2 * narrow :], jnp.zeros((step - 2, narrow), F32)], 0
        ).astype(BF16)
        for piece in range(pieces):
            part = acc_ref[piece * step : (piece + 1) * step].astype(BF16)
            dw_ref[0, piece, :, : 3 * narrow] = part
            dw_ref[0, piece, :, 3 * narrow :] = extra


def attend_back(order, pieces, acts, weights, masks, head_dim, out_type, stack, earlier=(), through=(), needs=()):
    _, rows, narrow, seq = acts[0].shape
    count = len(order)
    slot = (lambda s: (2 * s + 1) % 5) if count == 4 else (lambda s: order[0] + (order[-1] - order[0]) * s)
    at = lambda s, r: (slot(s), r, 0, 0)
    block = lambda n, where: pl.BlockSpec((1, 1, n, seq), where)
    lanes = weights[0].shape[2]
    last = weights[0].shape[0] - 1
    dims = (1, pieces, narrow // pieces, lanes)
    gx_kind, gx_count = (hbm, GROUPS) if stack else (shape, count)
    outs = [gx_kind((gx_count, rows, narrow, seq), out_type), shape((count,) + dims[1:], BF16)]
    specs = [
        block(narrow, at if stack else (lambda s, r: (s, r, 0, 0))),
        pl.BlockSpec(dims, lambda s, r: (s, 0, 0, 0)),
    ]
    return launch(
        functools.partial(attend_back_kernel, head_dim, count, len(earlier)),
        [*acts, *masks, *[weights[k] for k in order], *earlier],
        [block(a.shape[2], at) for a in acts]
        + [pl.BlockSpec((1, 16, seq), lambda s, r: (r, 0, 0))] * 2
        + [pl.BlockSpec((1, narrow, lanes), lambda s, r: (last, 0, 0))] * count
        + [ANY] * len(earlier),
        outs,
        specs,
        through,
        needs,
        aliases={8 + count: 0} if earlier else {},
        grid=(count, rows),
        scratch_shapes=[
            pltpu.VMEM((narrow + 16, 3 * narrow), F32),
            pltpu.VMEM((3 * narrow, seq), BF16),
            pltpu.VMEM((narrow, 3 * narrow), BF16),
        ],
        compiler_params=params(16),
        cost_estimate=cost(3.5 * count * rows),
        name="attend_bwd",
    )


def norm(values):
    width = values.shape[0]
    center = jnp.sum(values, axis=0, keepdims=True) * (1.0 / width)
    spread = jnp.sum(values * values, axis=0, keepdims=True) * (1.0 / width) - center * center
    inverse = lax.rsqrt(spread + EPSILON)
    return (values - center) * inverse, inverse


def norm_back(weighted, scaled, inverse):
    width = weighted.shape[0]
    first = jnp.sum(weighted, axis=0, keepdims=True) * (1.0 / width)
    second = jnp.sum(weighted * scaled, axis=0, keepdims=True) * (1.0 / width)
    return inverse * (weighted - first - scaled * second)


def normal_cdf(values):
    return 0.5 + 0.5 * lax.erf(values * 0.7071067811865476)


def whole(ref, me):
    return jnp.concatenate([ref[me ^ j, 0] for j in range(GROUPS)], 0)


def columns(layer, narrow, me, vec_refs, small_refs, small_ref):
    for k in range(GROUPS):
        small_ref[me ^ k] = small_refs[k][layer]
    out_bias = jnp.concatenate([small_ref[j, 1:2, 3 * narrow :] for j in range(GROUPS)], 1)
    rows = [ref[layer : layer + 1] for ref in vec_refs] + [out_bias]
    rows += [small_ref[j, 0:1] for j in range(GROUPS)]
    rows.append(jnp.zeros((16 - len(rows), out_bias.shape[1]), F32))
    return jnp.concatenate(rows, 0).T


def first_step():
    return (pl.program_id(0) == 0) & (pl.program_id(1) == 0)


def mix_kernel(layer, split, *refs):
    me_ref, xs_ref, o_ref, wp_ref = refs[:4]
    vec_refs, small_refs, w_refs = refs[4:9], refs[9:13], refs[13:17]
    count = GROUPS if split else 1
    next_refs, refs = refs[17 : 17 + count], refs[17 + count :]
    y1_ref, xh1_ref, xh2_ref, inv_ref, wpt_ref, wit_ref, wo_ref, small_ref, state_ref = refs
    me = me_ref[0]
    narrow = xs_ref.shape[2]

    @pl.when(first_step())
    def _():
        wpt_ref[...] = wp_ref[0].T
        for k in range(GROUPS):
            wit_ref[me ^ k] = w_refs[k][0].T
            wo_ref[me ^ k] = w_refs[k][1]

    cols = columns(layer, narrow, me, vec_refs, small_refs, small_ref)
    a = dot(wpt_ref[...], whole(o_ref, me), NN) + whole(xs_ref, me).astype(F32) + cols[:, 0:1]
    scaled_one, inverse_one = norm(a)
    y1 = (scaled_one * cols[:, 1:2] + cols[:, 2:3]).astype(BF16)
    y1_ref[0] = y1
    xh1_ref[0] = scaled_one.astype(BF16)
    hs = [
        dot(wit_ref[j], y1[j * narrow : (j + 1) * narrow], NN) + cols[:, 6 + j : 7 + j]
        for j in range(GROUPS)
    ]
    us = [(h * normal_cdf(h)).astype(BF16) for h in hs]
    z = jnp.concatenate([dot(wo_ref[j], us[j], NN) for j in range(GROUPS)], 0)
    scaled_two, inverse_two = norm(z + y1.astype(F32) + cols[:, 5:6])
    xh2_ref[0] = scaled_two.astype(BF16)
    state = (scaled_two * cols[:, 3:4] + cols[:, 4:5]).astype(BF16)
    for j in range(GROUPS):
        piece = state[j * narrow : (j + 1) * narrow]
        if split:
            state_ref[j] = piece
        else:
            next_refs[0][me ^ j, 0] = piece
    if split:
        for k in range(GROUPS):
            next_refs[k][0] = state_ref[me ^ k]
    inv_ref[0] = jnp.concatenate(
        [inverse_one, inverse_two, jnp.zeros((6, inverse_one.shape[1]), F32)], 0
    )


def mix(me, layer, split, xs, o, w_post, vectors, smalls, weights, tile, through=(), needs=(), kind=shape):
    _, rows, narrow, seq = xs.shape
    width = narrow * GROUPS
    ff = weights[0].shape[2]
    stacked = pl.BlockSpec((GROUPS, 1, narrow, tile), lambda r, t: (0, r, 0, t))
    plain = lambda n: pl.BlockSpec((1, n, tile), lambda r, t: (r, 0, t))
    const = lambda a: pl.BlockSpec(a.shape, lambda r, t: (0,) * a.ndim)
    outs = [shape((rows, narrow, seq), BF16)] * GROUPS if split else [vmem(xs.shape, BF16)]
    return launch(
        functools.partial(mix_kernel, layer, split),
        [me, xs, o, w_post, *vectors, *smalls, *weights],
        [SMEM, stacked, stacked, pl.BlockSpec((1, width, width), lambda r, t: (layer, 0, 0))]
        + [const(a) for a in (*vectors, *smalls)]
        + [pl.BlockSpec((2, narrow, ff), lambda r, t: (0, 0, 0))] * GROUPS,
        outs + [kind((rows, width, seq), BF16)] * 3 + [kind((rows, 8, seq), F32)],
        ([plain(narrow)] * GROUPS if split else [stacked]) + [plain(width)] * 3 + [plain(8)],
        through,
        needs,
        grid=(rows, seq // tile),
        scratch_shapes=[
            pltpu.VMEM((width, width), BF16),
            pltpu.VMEM((GROUPS, ff, narrow), BF16),
            pltpu.VMEM((GROUPS, narrow, ff), BF16),
            pltpu.VMEM((GROUPS, 8, ff), F32),
            pltpu.VMEM((GROUPS, narrow, tile), BF16),
        ],
        compiler_params=params(16),
        cost_estimate=cost(0.01),
        name="mix_fwd",
    )


def lane_sum(values):
    total = values[:, :128]
    for lo in range(128, values.shape[1], 128):
        total = total + values[:, lo : lo + 128]
    return total


def mix_back_kernel(layer, head_dim, *refs):
    me_ref, y1_ref, xh1_ref, xh2_ref, inv_ref, o_ref = refs[:6]
    gz_refs, wp_ref, vec_refs, small_refs, w_refs = refs[6:10], refs[10], refs[11:16], refs[16:20], refs[20:24]
    da_ref, dout_ref, delta_ref, f_odd_ref, f_even_ref, p_odd_ref, p_even_ref = refs[24:31]
    accf_ref, accp_ref, accv_ref, wit_ref, wot_ref, wi_ref, small_ref, gz_ref, tail_ref = refs[31:]
    me = me_ref[0]
    narrow, tile = o_ref.shape[2:]
    width = narrow * GROUPS
    step = pl.program_id(0) * pl.num_programs(1) + pl.program_id(1)
    steps = pl.num_programs(0) * pl.num_programs(1)

    @pl.when(first_step())
    def _():
        for k in range(GROUPS):
            wit_ref[me ^ k] = w_refs[k][0].T
            wi_ref[me ^ k] = w_refs[k][0]
            wot_ref[me ^ k] = w_refs[k][1].T
        accv_ref[...] = jnp.zeros_like(accv_ref)

    cols = columns(layer, narrow, me, vec_refs, small_refs, small_ref)
    for k in range(GROUPS):
        gz_ref[me ^ k] = gz_refs[k][0, 0].astype(F32)
    gz = jnp.concatenate([gz_ref[j] for j in range(GROUPS)], 0)
    y1 = y1_ref[0]
    scaled_one = xh1_ref[0].astype(F32)
    scaled_two = xh2_ref[0].astype(F32)
    inverse_one, inverse_two = inv_ref[0, 0:1], inv_ref[0, 1:2]
    accv_ref[0] += lane_sum(gz * scaled_two)
    accv_ref[1] += lane_sum(gz)
    dz = norm_back(gz * cols[:, 3:4], scaled_two, inverse_two)
    df = dz.astype(BF16)
    accv_ref[2] += lane_sum(df.astype(F32))
    ones = jnp.ones((16, tile), BF16)
    at = [slice(j * narrow, (j + 1) * narrow) for j in range(GROUPS)]
    hs = [dot(wit_ref[j], y1[at[j]], NN) + cols[:, 6 + j : 7 + j] for j in range(GROUPS)]
    back = [dot(wot_ref[j], df[at[j]], NN) for j in range(GROUPS)]
    us, dhs = [], []
    for h, some in zip(hs, back):
        cdf = normal_cdf(h)
        us.append((h * cdf).astype(BF16))
        dhs.append((some * (cdf + h * jnp.exp(-0.5 * h * h) * 0.3989422804014327)).astype(BF16))
    parts = [dz[at[j]] + dot(wi_ref[j], dhs[j], NN) for j in range(GROUPS)]
    so_far = lambda array: jnp.where(step == 0, 0.0, array)
    for j in range(GROUPS):
        out_term = dot(df[at[j]], us[j], NT)
        accf_ref[j, narrow + 16 :] = so_far(accf_ref[j, narrow + 16 :]) + out_term
        in_term = dot(jnp.concatenate([y1[at[j]], ones], 0), dhs[j], NT)
        accf_ref[j, : narrow + 16] = so_far(accf_ref[j, : narrow + 16]) + in_term
    dy1 = jnp.concatenate(parts, 0).astype(BF16).astype(F32)
    accv_ref[3] += lane_sum(dy1 * scaled_one)
    accv_ref[4] += lane_sum(dy1)
    da = norm_back(dy1 * cols[:, 1:2], scaled_one, inverse_one).astype(BF16)
    o = whole(o_ref, me)
    accp_ref[...] = so_far(accp_ref[...]) + dot(jnp.concatenate([o, ones], 0), da, NT)
    dout = dot(wp_ref[0], da, NN).astype(BF16)
    product = (o.astype(F32) * dout.astype(F32)).reshape(width // head_dim, head_dim, tile)
    delta = jnp.sum(product, axis=1)
    per_group = narrow // head_dim
    pad = jnp.zeros((8 - per_group, tile), F32)
    for j in range(GROUPS):
        lo = j * narrow
        da_ref[me ^ j, 0] = da[lo : lo + narrow]
        dout_ref[me ^ j, 0] = dout[lo : lo + narrow]
        delta_ref[me ^ j, 0] = jnp.concatenate(
            [delta[j * per_group : (j + 1) * per_group], pad], 0
        )

    @pl.when(step == steps - 1)
    def _():
        pieces = f_odd_ref.shape[1]
        vec = [jnp.sum(accv_ref[i].T, axis=0, keepdims=True) for i in range(5)]
        vec.append(accp_ref[width : width + 1])
        half = pieces // 2
        size, post = narrow // half, narrow // pieces
        for j in range(GROUPS):
            lo = j * narrow
            own = [v[:, lo : lo + narrow] for v in vec]
            tail_ref[j] = jnp.concatenate(
                [
                    accf_ref[j, narrow : narrow + 1],
                    jnp.concatenate(own[:4], 1),
                    jnp.concatenate(own[4:] + own[4:], 1),
                    jnp.zeros((5, width), F32),
                ],
                0,
            ).astype(BF16)
        for k in range(GROUPS):
            f_ref, p_ref = (f_odd_ref, p_odd_ref) if k % 2 else (f_even_ref, p_even_ref)
            j = me ^ k
            for piece in range(pieces):
                at = (piece % half) * size + (0 if piece < half else narrow + 16)
                f_ref[k // 2, piece] = accf_ref[j, at : at + size].astype(BF16)
                at = pl.multiple_of(j * narrow + piece * post, 8)
                p_ref[k // 2, piece, :post] = accp_ref[pl.ds(at, post)].astype(BF16)
                p_ref[k // 2, piece, post:] = tail_ref[j]


def mix_back(me, layer, pieces, kept, o, gz, w_post, vectors, smalls, weights, head_dim, tile, through=(), needs=(), kind=shape):
    _, rows, narrow, seq = o.shape
    width = narrow * GROUPS
    ff = weights[0].shape[2]
    stacked = pl.BlockSpec((GROUPS, 1, narrow, tile), lambda r, t: (0, r, 0, t))
    plain = lambda n: pl.BlockSpec((1, n, tile), lambda r, t: (r, 0, t))
    const = lambda dims: pl.BlockSpec(dims, lambda r, t: (0,) * len(dims))
    if isinstance(gz, list):
        gz_specs = [pl.BlockSpec((1, 1, narrow, tile), lambda r, t: (0, r, 0, t))] * GROUPS
    else:
        gz_specs = [
            pl.BlockSpec((1, 1, narrow, tile), lambda r, t, k=k: (k, r, 0, t))
            for k in range(GROUPS)
        ]
        gz = [gz] * GROUPS
    grads_f = (2, pieces, 2 * narrow // pieces, ff)
    grads_p = (2, pieces, narrow // pieces + 8, width)
    grads = [grads_f, grads_f, grads_p, grads_p]
    return launch(
        functools.partial(mix_back_kernel, layer, head_dim),
        [me, *kept, o, *gz, w_post, *vectors, *smalls, *weights],
        [SMEM] + [plain(width)] * 3 + [plain(8), stacked] + gz_specs
        + [pl.BlockSpec((1, width, width), lambda r, t: (layer, 0, 0))]
        + [const(a.shape) for a in (*vectors, *smalls)]
        + [const((2, narrow, ff))] * GROUPS,
        [kind(o.shape, BF16)] * 2 + [kind((GROUPS, rows, 8, seq), F32)]
        + [shape(g, BF16) for g in grads],
        [stacked, stacked, pl.BlockSpec((GROUPS, 1, 8, tile), lambda r, t: (0, r, 0, t))]
        + [const(g) for g in grads],
        through,
        needs,
        grid=(rows, seq // tile),
        scratch_shapes=[
            pltpu.VMEM((GROUPS, 2 * narrow + 16, ff), F32),
            pltpu.VMEM((width + 16, width), F32),
            pltpu.VMEM((5, width, 128), F32),
            pltpu.VMEM((GROUPS, ff, narrow), BF16),
            pltpu.VMEM((GROUPS, ff, narrow), BF16),
            pltpu.VMEM((GROUPS, narrow, ff), BF16),
            pltpu.VMEM((GROUPS, 8, ff), F32),
            pltpu.VMEM((GROUPS, narrow, tile), F32),
            pltpu.VMEM((GROUPS, 8, width), BF16),
        ],
        compiler_params=params(30),
        cost_estimate=cost(24.0),
        name="mix_bwd",
    )


def swap(array, axis, distance):
    size = lax.axis_size(axis)
    return lax.ppermute(array, axis, [(i, i ^ distance) for i in range(size)])


def collect_kernel(me_ref, *refs):
    out = refs[-1]
    for k, ref in enumerate(refs[:-1]):
        out[me_ref[0] ^ k, 0] = ref[0].astype(out.dtype)


def collect(me, arrays, needs=(), dtype=F32, through=None):
    rows, rest = arrays[0].shape[0], arrays[0].shape[1:]
    zeros = (0,) * len(rest)
    (out,), passed = launch(
        collect_kernel,
        [me, *arrays],
        [SMEM] + [pl.BlockSpec((1,) + rest, lambda r: (r,) + zeros)] * GROUPS,
        [(hbm if dtype == F32 else shape)((GROUPS, rows) + rest, dtype)],
        [pl.BlockSpec((GROUPS, 1) + rest, lambda r: (0, r) + zeros)],
        through or (),
        needs,
        grid=(rows,),
        compiler_params=params(12),
        cost_estimate=cost(0.1),
        name="collect",
    )
    return out if through is None else (out, passed)


def total(*arrays):
    return functools.reduce(lambda a, b: a + b, [a.astype(F32) for a in arrays])


def combine_kernel(sizes, spread, me_ref, *refs):
    count = sum(sizes)
    ins, outs = refs[:count], refs[count:]
    for d, out in enumerate(outs):
        start, row = 0, 0
        for size in sizes:
            terms = ins[start : start + size]
            rows = terms[0].shape[2]
            if spread:
                per = terms[0].shape[1] // len(outs)
                at = (me_ref[0] ^ d) * per
                part = total(*[ref[0, pl.ds(at, per)] for ref in terms])
            else:
                part = total(*[ref[0] for ref in terms])
            out[:, row : row + rows] = part.astype(BF16)
            start, row = start + size, row + rows


def combine(parts, me, spread=0, needs=()):
    flat = [a if isinstance(a, tuple) else (a[None], 0) for part in parts for a in part]
    pieces, _, lanes = flat[0][0].shape[1:]
    rows = sum((p[0][0].shape[2] if isinstance(p[0], tuple) else p[0].shape[1]) for p in parts)
    count = max(1, spread)
    outs, _ = launch(
        functools.partial(combine_kernel, [len(p) for p in parts], spread),
        [me] + [a for a, _ in flat],
        [SMEM]
        + [pl.BlockSpec((1, pieces, a.shape[2], lanes), lambda i, k=k: (k, 0, 0, 0)) for a, k in flat],
        [shape((pieces // count, rows, lanes), BF16)] * count,
        [pl.BlockSpec((pieces // count, rows, lanes), lambda i: (0, 0, 0))] * count,
        (),
        needs,
        grid=(1,),
        compiler_params=params(12),
        cost_estimate=cost(0.1),
        name="combine",
    )
    return outs if spread else outs[0]


def finish_post_kernel(post, layers, me_ref, *refs):
    ins, refs = refs[:GROUPS], refs[GROUPS + 1 :]
    small, refs = refs[: layers * GROUPS], refs[layers * GROUPS :]
    dpost_ref, vec_refs = refs[0], refs[1:]
    me = me_ref[0]
    for k, ref in enumerate(ins):
        dpost_ref[0, me ^ k] = ref[:, :post].astype(F32)

    if layers:
        width = vec_refs[0].shape[1]
        narrow = width // GROUPS

        @pl.when(pl.program_id(0) == pl.num_programs(0) - 1)
        def _():
            for layer in range(layers):
                for k in range(GROUPS):
                    both = small[layer * GROUPS + k][0].astype(F32)[8:]
                    rows = [
                        both[1 + i // 4 : 2 + i // 4, i % 4 * narrow : (i % 4 + 1) * narrow]
                        for i in range(6)
                    ]
                    if k == 0:
                        vec_refs[6][layer] = both[0:1]
                        vec_refs[7][layer] = rows[2]
                    for j in range(GROUPS):

                        @pl.when((me ^ k) == j)
                        def _(j=j, rows=rows, layer=layer):
                            for i in range(6):
                                vec_refs[i][layer : layer + 1, j * narrow : (j + 1) * narrow] = rows[i]


def finish_post(me, layer, slots, prior, all_slots, post, needs=()):
    pieces, rows, width = slots[0].shape
    narrow = width // GROUPS
    small = [a for some in all_slots for a in some]
    outs = [hbm((LAYERS, GROUPS, pieces, post, width), F32)]
    specs = [pl.BlockSpec((1, GROUPS, pieces // 2, post, width), lambda i: (layer, 0, i, 0, 0))]
    if small:
        outs += [shape((LAYERS, width), F32)] * 6
        outs += [shape((LAYERS, 1, width), F32), shape((LAYERS, 1, narrow), F32)]
        specs += [pl.BlockSpec(o.shape, lambda i, n=len(o.shape): (0,) * n) for o in outs[1:]]
    if prior is None:
        prior, aliases = me, {}
    else:
        aliases = {1 + GROUPS: 0}
    return launch(
        functools.partial(finish_post_kernel, post, len(all_slots)),
        [me, *slots, prior, *small],
        [SMEM]
        + [pl.BlockSpec((pieces // 2, rows, width), lambda i: (i, 0, 0))] * GROUPS
        + [ANY if aliases else SMEM]
        + [pl.BlockSpec((1, 16, width), lambda i: (0, (rows - 16) // 16, 0))] * len(small),
        outs,
        specs,
        (),
        needs,
        aliases=aliases,
        grid=(2,),
        compiler_params=params(12),
        cost_estimate=cost(0.1),
        name="finish_post",
    )[0]


def finish_ffn_kernel(size, me_ref, *refs):
    parts, last_ref = refs[:4], refs[4]
    wi_ref, wo_ref = refs[5:]
    layer = pl.program_id(0)

    def put(shard, part):
        @pl.when(shard < 2)
        def _():
            wi_ref[0, shard] = part.astype(F32)

        @pl.when(shard >= 2)
        def _():
            wo_ref[0, shard - 2] = part.astype(F32)

    @pl.when(layer == 0)
    def _():
        for d, ref in enumerate(parts):
            put(me_ref[0] ^ d, ref[:, :size])

    @pl.when(layer > 0)
    def _():
        for d in range(4):
            put(d, last_ref[2 * d : 2 * d + 2, :size])


def finish_ffn(me, parts, last, size, needs=()):
    half, _, lanes = parts[0].shape
    out = hbm((LAYERS, 2, half, size, lanes), F32)
    return launch(
        functools.partial(finish_ffn_kernel, size),
        [me, *parts, last],
        [SMEM] + [pl.BlockSpec(a.shape, lambda l: (0, 0, 0)) for a in (*parts, last)],
        [out] * 2,
        [pl.BlockSpec((1, 2, half, size, lanes), lambda l: (l, 0, 0, 0, 0))] * 2,
        (),
        needs,
        grid=(LAYERS,),
        compiler_params=params(12),
        cost_estimate=cost(0.1),
        name="finish_ffn",
    )[0]


def finish_qkv_kernel(lo, post, me_ref, *refs):
    sets, outs = (refs[:4], refs[4:8]), refs[8:]
    narrow = outs[0].shape[-1]
    for layer, parts in enumerate(sets):
        start = lo if layer else 0
        for d, ref in enumerate(parts):
            part = ref[:, start : start + post].astype(F32)
            for i in range(3):
                outs[i][layer, me_ref[0] ^ d] = part[:, :, i * narrow : (i + 1) * narrow]
            if d == 0:
                outs[3][layer] = part[0, 0:1, 3 * narrow :]
                outs[4][layer] = part[0, 1:2, 3 * narrow :]


def finish_qkv(me, first, second, lo, narrow, needs=()):
    half, post, lanes = first[0].shape
    big = shape((LAYERS, 4, half, post, narrow), F32)
    vec = shape((LAYERS, 1, narrow), F32)
    full = pl.BlockSpec(memory_space=pltpu.VMEM)
    return launch(
        functools.partial(finish_qkv_kernel, lo, post),
        [me, *first, *second],
        [SMEM] + [full] * 8,
        [big] * 3 + [vec] * 2,
        [full] * 5,
        (),
        needs,
        compiler_params=params(12),
        cost_estimate=cost(0.1),
        name="finish_qkv",
    )[0]


def fold_kernel(in_ref, out_ref):
    part = total(*[in_ref[i] for i in range(in_ref.shape[0])]).astype(BF16)
    for i in range(out_ref.shape[0]):
        out_ref[i] = part


def fold(array, through=(), needs=()):
    pieces, rows, lanes = array.shape
    block = pl.BlockSpec((pieces, rows, lanes), lambda i: (0, 0, 0))
    (out,), passed = launch(
        fold_kernel,
        [array],
        [block],
        [shape(array.shape, BF16)],
        [block],
        through,
        needs,
        grid=(1,),
        compiler_params=params(12),
        cost_estimate=cost(0.1),
        name="fold",
    )
    return (out, *passed)


def dp_groups(pieces):
    return [list(range(i, i + pieces)) for i in range(0, lax.axis_size("dp"), pieces)]


def trade(array):
    return lax.all_to_all(
        array, "dp", split_axis=0, concat_axis=0, tiled=True,
        axis_index_groups=dp_groups(array.shape[0]),
    )


def beyond(copies):
    distance = copies.shape[0]
    while distance < lax.axis_size("dp"):
        copies = total(copies, swap(copies, "dp", distance)).astype(BF16)
        distance *= 2
    return copies


def near_dp(parts):
    return [parts[0]] + [swap(part, "dp", d) for d, part in enumerate(parts) if d]


def across_dp(sums, needs=(), block=4):
    distance = block
    while distance < lax.axis_size("dp"):
        sums = add([[mine, swap(mine, "dp", distance)] for mine in sums], (), needs)
        distance *= 2
    return sums


def add_kernel(sizes, *refs):
    ins, outs = refs[: sum(sizes)], refs[sum(sizes) :]
    start = 0
    for size, out in zip(sizes, outs):
        out[...] = total(*[ref[...] for ref in ins[start : start + size]]).astype(BF16)
        start += size


def add(lists, through=(), needs=(), micros=0.1):
    flat = [a for arrays in lists for a in arrays]
    spec = lambda a: pl.BlockSpec(a.shape, lambda i: (0, 0, 0))
    outs, passed = launch(
        functools.partial(add_kernel, [len(arrays) for arrays in lists]),
        flat,
        [spec(a) for a in flat],
        [shape(arrays[0].shape, BF16) for arrays in lists],
        [spec(arrays[0]) for arrays in lists],
        through,
        needs,
        grid=(1,),
        compiler_params=params(16),
        cost_estimate=cost(micros),
        name="add",
    )
    return (*outs, *passed)


def pick(array, index):
    return lax.dynamic_index_in_dim(array, index, 0, keepdims=False)


def shards(
    hidden_in,
    segment_ids,
    w_query,
    b_query,
    w_key,
    w_value,
    b_value,
    w_post,
    b_post,
    ln1_gain,
    ln1_bias,
    w_inter,
    b_inter,
    w_output,
    b_output,
    ln2_gain,
    ln2_bias,
    cotangent,
):
    row_count, narrow, seq = hidden_in.shape
    rows = row_count // GROUPS
    width = narrow * GROUPS
    ff = w_inter.shape[-1]
    head_dim = width // HEADS
    me = lax.axis_index("grp")
    me_ref = me.reshape(1).astype(jnp.int32)
    pieces = 8
    tile = 256

    by_owner = hidden_in.reshape(GROUPS, rows, narrow, seq)
    cot_owner = cotangent.reshape(GROUPS, rows, narrow, seq)
    no_bias = jnp.zeros_like(b_query)
    small = jnp.concatenate([b_query, no_bias, b_value, b_output], 2)
    small = jnp.pad(jnp.concatenate([b_inter, small], 1), ((0, 0), (0, 6), (0, 0)))
    pad = jnp.zeros((LAYERS, 1, narrow, ff - 3 * narrow), BF16)
    w_qkv = jnp.concatenate([w_query, w_key, w_value, pad], 3)
    ffn_own = jnp.concatenate([w_inter[0], w_output[0]], 0)
    both_own = jnp.concatenate([w_inter[1], w_output[1], w_qkv[1]], 0)

    segments = lax.dynamic_slice_in_dim(segment_ids, me * rows, rows, 0)
    hot = segments[:, None, :] == jnp.arange(16, dtype=segments.dtype)[None, :, None]
    masks = (hot.astype(BF16), jnp.where(hot, 0.0, MASKED).astype(BF16))

    small_far, qkv_far = swap(small, "grp", 2), swap(w_qkv[0], "grp", 2)
    smalls = [small, swap(small, "grp", 1), small_far, swap(small_far, "grp", 1)]
    qkv0 = [w_qkv[0], swap(w_qkv[0], "grp", 1), qkv_far, swap(qkv_far, "grp", 1)]
    x_slots = [pick(by_owner, me)] + [swap(pick(by_owner, me ^ k), "grp", k) for k in (1, 2, 3)]

    acts0, _ = attend(
        x_slots[0][None], 0, None, qkv0[:1], smalls[:1], masks, 0, head_dim, kind=hbm
    )
    acts0, _ = attend(
        x_slots[1][None], 1, acts0, qkv0[1:2], smalls[1:2], masks, 0, head_dim, kind=hbm
    )
    acts0, (ffn_own,) = attend(
        x_slots[2][None], 2, acts0, qkv0[2:3], smalls[2:3], masks, 0, head_dim, [ffn_own],
        kind=hbm,
    )
    ffn_far = swap(ffn_own, "grp", 2)
    ffn0 = [ffn_own, swap(ffn_own, "grp", 1), ffn_far, swap(ffn_far, "grp", 1)]
    acts0, (both_own,) = attend(
        x_slots[3][None], 3, acts0, qkv0[3:4], smalls[3:4], masks, 0, head_dim, [both_own],
        kind=hbm,
    )
    both_far = swap(both_own, "grp", 2)
    both_near = swap(both_own, "grp", 1)
    o0, qkvs0, lse0, xs0 = [held(a, pltpu.HBM) for a in acts0]
    vectors = (b_post, ln1_gain, ln1_bias, ln2_gain, ln2_bias)
    (state, *kept0), cot_send = mix(
        me_ref, 0, False, xs0, o0, w_post, vectors, smalls, ffn0, tile,
        [pick(cot_owner, me ^ k) for k in (1, 2, 3)],
        kind=hbm,
    )
    kept0 = [held(a, pltpu.HBM) for a in kept0]
    state = held(state)
    cot_slots = [pick(cot_owner, me)[None]] + [
        swap(cot_send[k - 1], "grp", k)[None] for k in (1, 2, 3)
    ]
    acts1, (both_far,) = attend(
        state, 0, None, [both_own, both_near], smalls[:2], masks, 1, head_dim, [both_far]
    )
    both1 = [both_own, both_near, both_far, swap(both_far, "grp", 1)]
    acts1, _ = attend(state, 2, acts1, both1[2:], smalls[2:], masks, 1, head_dim)
    o1, qkvs1, lse1, xs1 = acts1
    results, _ = mix(me_ref, 1, True, xs1, o1, w_post, vectors, smalls, both1, tile)
    state_slots, kept1 = results[:GROUPS], results[GROUPS:]
    state_slots = [state_slots[0]] + [swap(state_slots[k], "grp", k) for k in (1, 2, 3)]

    me_four = (lax.axis_index("dp") % 4).reshape(1).astype(jnp.int32)
    (da1, dout1, delta1, f_odd, f_even, p_odd, p_even), _ = mix_back(
        me_ref, 1, pieces, kept1, o1, cot_slots, w_post, vectors, smalls, both1, head_dim, tile
    )
    hidden_out, passed = collect(
        me_ref, state_slots, through=(da1, dout1, delta1, f_odd, f_even, p_odd, p_even)
    )
    da1, dout1, delta1, f_odd, f_even, p_odd, p_even = passed
    f_near, p_near = swap(f_odd, "grp", 1), swap(p_odd, "grp", 1)
    send = combine([[(f_even, 1), (f_near, 1)], [(p_even, 1), (p_near, 1)]], me_ref)
    far = swap(send, "grp", 2)
    acts = (xs1, qkvs1, dout1, da1, lse1, delta1)
    (gz, dw_odd1), _ = attend_back(
        [1, 3], pieces, acts, both1, masks, head_dim, F32, True, (), (), (send,)
    )
    near_q1 = swap(dw_odd1, "grp", 1)
    own_f = combine([[(f_even, 0), (f_near, 0)], [(p_even, 0), (p_near, 0)]], me_ref, 0, (dw_odd1,))
    (gz, dw_even1), _ = attend_back(
        [0, 2], pieces, acts, both1, masks, head_dim, F32, True, (gz,), (), (own_f,)
    )
    gz = held(gz, pltpu.HBM)
    (own1,) = add([[own_f, far]], (), (dw_even1,))
    moved1 = trade(own1)
    send_q1 = combine([[(dw_even1, 1), (near_q1, 1)]], me_ref, 0, (own1,))
    far_q1 = swap(send_q1, "grp", 2)
    (da0, dout0, delta0, f_odd, f_even, p_odd, p_even), _ = mix_back(
        me_ref, 0, pieces, kept0, o0, gz, w_post, vectors, smalls, ffn0, head_dim, tile,
        (), (send_q1,), hbm,
    )
    p_near, f_near = swap(p_odd, "grp", 1), swap(f_odd, "grp", 1)
    send_p = combine([[(p_even, 1), (p_near, 1)]], me_ref)
    far_p = swap(send_p, "grp", 2)
    send_f = combine([[(f_even, 1), (f_near, 1)]], me_ref, 0, (send_p,))
    far_f = swap(send_f, "grp", 2)
    dout0, da0, delta0 = [held(a, pltpu.HBM) for a in (dout0, da0, delta0)]
    acts = (xs0, qkvs0, dout0, da0, lse0, delta0)
    qkv0 = [held(w, pltpu.HBM) for w in qkv0]
    (mine1,) = fold(moved1, (), (send_f,))
    all1 = trade(beyond(mine1))
    back = lambda order, *rest: attend_back(
        order, pieces, acts, qkv0, masks, head_dim, BF16, False, (), *rest
    )
    (gx32, dw32), _ = back([3, 2], (), (mine1, far_q1))
    near_w3 = swap(dw32[:1], "grp", 1)
    p_late, f_late, q_late = [
        [held(a, pltpu.HBM) for a in pair]
        for pair in ((p_even, p_near), (f_even, f_near), (dw_even1, near_q1))
    ]
    own_p = combine([[(p_late[0], 0), (p_late[1], 0), far_p]], me_four, 4, (dw32,))
    parts_p = near_dp(own_p)
    send_w = combine([[(dw32, 1), (near_w3, 0)]], me_ref, 0, (own_p[0],))
    far_w = swap(send_w, "grp", 2)
    own_f = combine(
        [[(f_late[0], 0), (f_late[1], 0), far_f], [(q_late[0], 0), (q_late[1], 0), far_q1]], me_four, 4,
        (send_w, all1),
    )
    parts_f = near_dp(own_f)
    size, post = 2 * narrow // pieces, narrow // pieces
    last_p = all1[:, size:]
    (mine_p,) = add([parts_p], (), (own_f[0],))
    across_p = swap(mine_p, "dp", 4)
    (gx10, dw10), _ = back([1, 0], (), (mine_p,))
    gx2, gx3 = swap(gx32[1], "grp", 2), swap(gx32[0], "grp", 3)
    mine_p, mine_f, gx10, dw10 = add(
        [[mine_p, across_p], parts_f], (gx10, dw10), (gx2, gx3)
    )
    near_w1 = swap(dw10[:1], "grp", 1)
    gx_slots = [gx10[1], swap(gx10[0], "grp", 1), gx2, gx3]
    own_q = combine([[(dw10, 1), (near_w1, 0), far_w]], me_four, 4, (mine_p,))
    parts_q = near_dp(own_q)
    (mine_p,) = across_dp([mine_p], (), 8)
    parts_p = near_dp([mine_p] * 4)
    across_f = swap(mine_f, "dp", 4)
    last_far = swap(last_p, "grp", 2)
    (mine_q,) = add([parts_q], (), (last_far,))
    across_q = swap(mine_q, "dp", 4)
    (mine_f,) = add([[mine_f, across_f]], (), (mine_q,))
    (mine_f,) = across_dp([mine_f], (), 8)
    parts_f = near_dp([mine_f] * 4)
    all_p = collect(me_four, parts_p, (mine_f,), BF16).reshape(pieces, -1, width)
    far_shared = swap(all_p, "grp", 2)
    near_shared = swap(all_p, "grp", 1)
    shared1 = [last_p, swap(last_p, "grp", 1), last_far, swap(last_far, "grp", 1)]
    (prior,) = finish_post(me_ref, 1, shared1, None, [], post, (all_p,))
    grad_input = collect(me_ref, gx_slots, (held(prior, pltpu.HBM),))
    mine_q, far_shared = add(
        [[mine_q, across_q]], (far_shared,), (held(grad_input, pltpu.HBM), *parts_f[1:]), 10.0
    )
    (mine_q,) = across_dp([mine_q], (), 8)
    parts_q = near_dp([mine_q] * 4)
    shared0 = [all_p, near_shared, far_shared, swap(far_shared, "grp", 1)]

    dpost, *vec = finish_post(me_ref, 0, shared0, prior, [shared0, shared1], post, (mine_q,))
    d_inter, d_output = finish_ffn(me_four, parts_f, all1, size, (mine_q,))
    dq, dk, dv, dbq, dbv = finish_qkv(
        me_four, parts_q, parts_f, size, narrow,
        (held(d_inter, pltpu.HBM), held(dpost, pltpu.HBM)),
    )
    ffn_shape, qkv_shape = (LAYERS, 1, narrow, ff), (LAYERS, 1, narrow, narrow)
    return (
        hidden_out.reshape(row_count, narrow, seq),
        grad_input.reshape(row_count, narrow, seq),
        dq.reshape(qkv_shape),
        dbq,
        dk.reshape(qkv_shape),
        dv.reshape(qkv_shape),
        dbv,
        dpost.reshape(LAYERS, width, width),
        vec[5],
        vec[3],
        vec[4],
        d_inter.reshape(ffn_shape),
        vec[6],
        d_output.reshape(ffn_shape),
        vec[7],
        vec[0],
        vec[1],
    )


def solution(mesh):
    placed = (
        P("dp", "grp", None),
        P("dp", None),
        P(None, "grp", None, None),
        P(None, "grp", None),
        P(None, "grp", None, None),
        P(None, "grp", None, None),
        P(None, "grp", None),
        P(),
        P(),
        P(),
        P(),
        P(None, "grp", None, None),
        P(None, "grp", None),
        P(None, "grp", None, None),
        P(None, "grp", None),
        P(),
        P(),
        P("dp", "grp", None),
    )
    return jax.shard_map(
        shards,
        mesh=mesh,
        in_specs=placed,
        out_specs=(
            P("dp", "grp", None),
            P("dp", "grp", None),
            P(None, "grp", None, None),
            P(None, "grp", None),
            P(None, "grp", None, None),
            P(None, "grp", None, None),
            P(None, "grp", None),
            P(),
            P(),
            P(),
            P(),
            P(None, "grp", None, None),
            P(None, "grp", None),
            P(None, "grp", None, None),
            P(None, "grp", None),
            P(),
            P(),
        ),
        check_vma=False,
    )
```
